32 devices in a mesh: wide: 8 (over z, x), narrow: 4 (over y, core).
Axes of the slice: x: 2, y: 2, z: 4, core: 2. Of those that a mesh axis runs over, the one named last changes fastest.
Arguments:
- tokens: bfloat16 [24576, 1024], P(('wide', 'narrow')), may hold values from -6 to 6
- cotangent: bfloat16 [24576, 1024], P(('wide', 'narrow')), may hold values from -6 to 6
- lengths: int32 [8], P('wide'), may hold values from 2305 to 3072, as said below
- owners: int32 [192], replicated, may hold values from 0 to 31, as said below
- w_qkv: float32 [4, 256, 3072], P(None, ('wide', 'narrow')), may hold values from -0.125 to 0.125
- w_out: float32 [4, 256, 1024], P(None, ('wide', 'narrow')), may hold values from -2.5 to 2.5
- w_up: float32 [4, 256, 4096], P(None, ('wide', 'narrow')), may hold values from -0.1875 to 0.1875
- w_down: float32 [16, 256, 1024], P(None, ('wide', 'narrow')), may hold values from -0.09375 to 0.09375
- norm_gains: float32 [2, 1024], P(None, ('wide', 'narrow')), may hold values from 0.5 to 3.5
- gain_first: float32 [2, 1024], P(None, ('wide', 'narrow')), may hold values from -0.01171875 to 0.01171875
- gain_second: float32 [2, 1024], P(None, ('wide', 'narrow')), may hold values from 7.151393e-07 to 2.8605573e-06
- moment_first: float32 [192, 256, 256], P(('wide', 'narrow')), may hold values from -0.00390625 to 0.00390625
- moment_second: float32 [192, 256, 256], P(('wide', 'narrow')), may hold values from 7.945993e-08 to 3.1783972e-07
- left_stat: float32 [192, 256, 256], P(('wide', 'narrow')), as said below
- right_stat: float32 [192, 256, 256], P(('wide', 'narrow')), as said below
- left_basis: float32 [192, 256, 256], P(('wide', 'narrow')), may hold values from -1 to 1, as said below
- right_basis: float32 [192, 256, 256], P(('wide', 'narrow')), may hold values from -1 to 1, as said below
Outputs:
- block_out: bfloat16 [24576, 1024], P(('wide', 'narrow'))
- grad_tokens: bfloat16 [24576, 1024], P(('wide', 'narrow'))
- grad_norm: float32 [], replicated
- new_qkv: float32 [4, 256, 3072], P(None, ('wide', 'narrow'))
- new_out: float32 [4, 256, 1024], P(None, ('wide', 'narrow'))
- new_up: float32 [4, 256, 4096], P(None, ('wide', 'narrow'))
- new_down: float32 [16, 256, 1024], P(None, ('wide', 'narrow'))
- gain_values: float32 [2, 1024], P(None, ('wide', 'narrow'))
- gain_first_new: float32 [2, 1024], P(None, ('wide', 'narrow'))
- gain_second_new: float32 [2, 1024], P(None, ('wide', 'narrow'))
- moment_first_new: float32 [192, 256, 256], P(('wide', 'narrow'))
- moment_second_new: float32 [192, 256, 256], P(('wide', 'narrow'))
- left_stat_new: float32 [192, 256, 256], P(('wide', 'narrow'))
- right_stat_new: float32 [192, 256, 256], P(('wide', 'narrow'))
- left_basis_new: float32 [192, 256, 256], P(('wide', 'narrow'))
- right_basis_new: float32 [192, 256, 256], P(('wide', 'narrow'))
The draws below stay inside these ranges and needn't reach their ends.
Inputs may be any that keep to these rules, and one draw needn't show every extreme that they name: `lengths`: some scene has all 3072 tokens valid. `owners`: no device owns more than 6 blocks, and some device owns exactly 6. `left_stat`: each slot's statistics are symmetric positive definite. `right_stat`: each slot's statistics are symmetric positive definite. `left_basis`: each slot's basis is orthogonal. `right_basis`: each slot's basis is orthogonal.
All inputs are finite; a program needn't handle non-finite values.
Results may differ from the reference program's by a relative error of at most 0.017.
The reference program's roundings to bfloat16 on the way count: a program that leaves them out, or rounds other values in their place, can miss the bound.
Values may be sent and summed in bfloat16 or wider, within the bound.
A program may use at most 256 MiB of HBM per device.

```python
import math
from functools import partial
import jax
import jax.numpy as jnp
from jax import lax

D = 1024
FF = 4096
HEADS = 16
HEAD = 64
BLOCK = 256
STEP = 10
TOK_DEV = 768
SEQ = 3072
SCENES = 8
TOKENS = 24576
P_ALL = 12584960
BLOCKS = 192
CAP = 6
SLOTS = 192
N_WIDE = 8
N_NARROW = 4


def draw_lengths(key, part):
    key = jax.random.fold_in(key, 11)
    key_vals, key_full = jax.random.split(key)
    values = jax.random.randint(key_vals, (SCENES,), SEQ - TOK_DEV + 1, SEQ + 1)
    chosen = jax.random.randint(key_full, (), 0, SCENES)
    return jnp.where(jnp.arange(SCENES) == chosen, SEQ, values).astype(jnp.int32)


def draw_owners(key, part):
    key = jax.random.fold_in(key, 12)
    order = jax.random.permutation(key, SLOTS)
    return (order[:BLOCKS] // CAP).astype(jnp.int32)


def rising_gains(key, start):
    feature = jnp.arange(D)
    device = feature % BLOCK * (N_WIDE * N_NARROW) // BLOCK
    outer = (device // N_NARROW).astype(jnp.float32) / max(N_WIDE - 1, 1)
    inner = (device % N_NARROW).astype(jnp.float32) / max(N_NARROW - 1, 1)
    rising = start + outer + inner
    noise = jax.random.uniform(key, (2, D), minval=0.85, maxval=1.15)
    return (rising[None, :] * noise).astype(jnp.float32)


def draw_norm_gains(key, part):
    key = jax.random.fold_in(key, 13)
    return rising_gains(key, 1.0)


def definite(key, ratio):
    size_diag = BLOCK * P_ALL ** (-1)
    key_diag, key_off = jax.random.split(key)
    diagonal = size_diag * jnp.exp(jax.random.uniform(key_diag, (SLOTS, BLOCK), minval=0.0, maxval=math.log(ratio)))
    raw = jax.random.truncated_normal(key_off, -3.0, 3.0, (SLOTS, BLOCK, BLOCK))
    symmetric = (raw + raw.transpose(0, 2, 1)) * 0.7071
    off_diag = symmetric * (0.3 * size_diag / math.sqrt(BLOCK))
    identity = jnp.eye(BLOCK, dtype=bool)
    return jnp.where(identity[None], diagonal[:, :, None], off_diag).astype(jnp.float32)


def draw_left_stat(key, part):
    key = jax.random.fold_in(key, 14)
    return definite(key, 4.0)


def draw_right_stat(key, part):
    key = jax.random.fold_in(key, 15)
    return definite(key, 4.0)


def cosine_basis(key, first_row):
    key_perm, key_rows, key_cols = jax.random.split(key, 3)
    index = jnp.arange(BLOCK).astype(jnp.float32)
    table = jnp.cos(math.pi * (index[None, :] + 0.5) * index[:, None] / BLOCK) * math.sqrt(2.0 / BLOCK)
    table = jnp.where(index[:, None] == 0.0, table * first_row, table)
    perms = jax.vmap(lambda one_key: jax.random.permutation(one_key, BLOCK))(jax.random.split(key_perm, SLOTS))
    rows_taken = table[perms]
    row_signs = (2 * jax.random.randint(key_rows, (SLOTS, BLOCK, 1), 0, 2) - 1).astype(jnp.float32)
    col_signs = (2 * jax.random.randint(key_cols, (SLOTS, 1, BLOCK), 0, 2) - 1).astype(jnp.float32)
    return (rows_taken * row_signs * col_signs).astype(jnp.float32)


def draw_left_basis(key, part):
    key = jax.random.fold_in(key, 16)
    return cosine_basis(key, 0.70710678)


def draw_right_basis(key, part):
    key = jax.random.fold_in(key, 17)
    return cosine_basis(key, 0.70710678)


def levels(own_key, shape, cuts, least, high):
    def one(axis_at, blocks):
        draws = jax.random.uniform(jax.random.fold_in(jax.random.fold_in(own_key, 6), axis_at), (blocks,), jnp.float32, least / len(cuts), high / len(cuts))
        return jnp.repeat(jnp.exp(draws), shape[axis_at] // blocks).reshape((-1,) + (1,) * (len(shape) - axis_at - 1))

    level = one(*cuts[0])
    for cut in cuts[1:]:
        level = level * one(*cut)
    return level


def normal_values(rng, extent, deviation, most, shards=(), kind=jnp.bfloat16):
    drawn = jax.random.normal(rng, extent, jnp.float32) * deviation
    if len(shards) > 0:
        drawn = levels(rng, extent, shards, -0.22, 0.18) * drawn
    return jnp.clip(drawn, min=-most, max=most).astype(kind)


def setup_inputs(seed: int = 0) -> dict:
    key_list = jax.random.split(jax.random.key(seed), 18)
    tokens = normal_values(key_list[0], (TOKENS, D), 1.0, 6.0, ((0, 32),))
    cotangent = normal_values(key_list[1], (TOKENS, D), 1.0, 6.0, ((0, 32),))
    lengths = draw_lengths(jax.random.fold_in(key_list[17], 71), 0)
    owners = draw_owners(jax.random.fold_in(key_list[17], 71), 0)
    w_qkv = normal_values(key_list[4], (D // BLOCK, BLOCK, 3 * D), (2 * D) ** -0.5, 0.125, ((1, 32),), jnp.float32)
    w_out = normal_values(key_list[5], (D // BLOCK, BLOCK, D), (max(1, D * 16 // SEQ)) ** -0.5, 2.5, ((1, 32),), jnp.float32)
    w_up = normal_values(key_list[6], (D // BLOCK, BLOCK, FF), D ** -0.5, 0.1875, ((1, 32),), jnp.float32)
    w_down = normal_values(key_list[7], (FF // BLOCK, BLOCK, D), FF ** -0.5, 0.09375, ((1, 32),), jnp.float32)
    norm_gains = draw_norm_gains(jax.random.fold_in(key_list[17], 71), 0)
    gain_first = normal_values(key_list[9], (2, D), (3 * P_ALL ** -0.5), 0.01171875, ((1, 32),), jnp.float32)
    gain_second = jnp.clip(jnp.exp(math.log(2.8605572879314423e-06) - 1.3862944 * jax.random.uniform(key_list[10], (2, D), jnp.float32) ** levels(key_list[10], (2, D), ((1, 32),), -0.2, 0.2)), 7.151393219828606e-07, 2.8605572879314423e-06)
    moment_first = normal_values(key_list[11], (SLOTS, BLOCK, BLOCK), (P_ALL ** -0.5), 0.00390625, ((0, 32),), jnp.float32)
    moment_second = jnp.clip(jnp.exp(math.log(3.1783972076482314e-07) - 1.3862944 * jax.random.uniform(key_list[12], (SLOTS, BLOCK, BLOCK), jnp.float32) ** levels(key_list[12], (SLOTS, BLOCK, BLOCK), ((0, 32),), -0.2, 0.2)), 7.945993019120579e-08, 3.1783972076482314e-07)
    left_stat = draw_left_stat(jax.random.fold_in(key_list[17], 71), 0)
    right_stat = draw_right_stat(jax.random.fold_in(key_list[17], 71), 0)
    left_basis = draw_left_basis(jax.random.fold_in(key_list[17], 71), 0)
    right_basis = draw_right_basis(jax.random.fold_in(key_list[17], 71), 0)
    return dict(tokens=tokens, cotangent=cotangent, lengths=lengths, owners=owners, w_qkv=w_qkv, w_out=w_out, w_up=w_up, w_down=w_down, norm_gains=norm_gains, gain_first=gain_first, gain_second=gain_second, moment_first=moment_first, moment_second=moment_second, left_stat=left_stat, right_stat=right_stat, left_basis=left_basis, right_basis=right_basis)


eps_norm = 1e-05
eps_adam = 1e-08
decay_rate = 0.5
clip_bound = 1.0
weight_decay = 0.01
gain_rate = 1.0
neg_large = -1e+30
highest = lax.Precision.HIGHEST

@jax.custom_vjp
def low(v):
    return lax.optimization_barrier(v.astype(jnp.bfloat16)).astype(jnp.float32)

@jax.custom_vjp
def low_back(v):
    return v

def low_keep(v):
    return (low(v), None)

def low_pass(kept, grad):
    return (grad,)

def back_keep(v):
    return (v, None)

def back_low(kept, grad):
    return (low(grad),)
low.defvjp(low_keep, low_pass)
low_back.defvjp(back_keep, back_low)

def dense(left, right):
    return jnp.dot(left, right, precision=highest)

def layer_norm(values, gain):
    center = values - lax.optimization_barrier(jnp.mean(values, -1, keepdims=True))
    spread = lax.optimization_barrier(jnp.mean(center * center, -1, keepdims=True))
    return center * lax.rsqrt(spread + eps_norm) * gain

def head_attention(visible, parts):
    queries, keyset, valueset = parts
    scores = low_back(dense(queries, keyset.T) * HEAD ** (-0.5))
    scores = jnp.where(visible[None, :], scores, neg_large)
    topmost = lax.optimization_barrier(jnp.max(scores, -1, keepdims=True))
    expo_vals = jnp.exp(scores - topmost)
    attn_probs = expo_vals / lax.optimization_barrier(jnp.sum(expo_vals, -1, keepdims=True))
    return dense(low(attn_probs), valueset)

def scene_forward(params, scene_data):
    w_attn, w_proj, w_hidden, w_back, gain_one, gain_two = params
    scene_tok, length = scene_data
    visible = jnp.arange(SEQ, dtype=jnp.int32) < length
    normed = low(layer_norm(scene_tok, gain_one))
    packed = low(low_back(dense(normed, w_attn)))
    head_split = packed.reshape(SEQ, 3, HEADS, HEAD).transpose(1, 2, 0, 3)
    mixed = lax.map(jax.checkpoint(partial(head_attention, visible)), (head_split[0], head_split[1], head_split[2]))
    merged = low(low_back(mixed.transpose(1, 0, 2).reshape(SEQ, D)))
    middle = scene_tok + low_back(dense(merged, w_proj))
    second_in = low(layer_norm(middle, gain_two))
    hidden = low_back(dense(second_in, w_hidden))
    active = low(jax.nn.gelu(hidden, approximate=True))
    return middle + dense(active, w_back)

def to_matrix(layout):
    return layout.reshape(layout.shape[0] * layout.shape[1], layout.shape[2])

def to_blocks(matrix):
    rows_n, cols_n = matrix.shape
    return matrix.reshape(rows_n // BLOCK, BLOCK, cols_n // BLOCK, BLOCK).transpose(0, 2, 1, 3).reshape(-1, BLOCK, BLOCK)

def from_blocks(blocks, rows_n, cols_n):
    return blocks.reshape(rows_n // BLOCK, cols_n // BLOCK, BLOCK, BLOCK).transpose(0, 2, 1, 3).reshape(rows_n // BLOCK, BLOCK, cols_n)

def slot_table(owners):
    order = jnp.arange(owners.shape[0], dtype=jnp.int32)
    earlier = (owners[None, :] == owners[:, None]) & (order[None, :] < order[:, None])
    return (owners * CAP + lax.optimization_barrier(jnp.sum(earlier.astype(jnp.int32), 1))).astype(jnp.int32)

def batched(spec, left, right):
    return jnp.einsum(spec, left, right, precision=highest)

def renew_basis(stat, basis):
    turned = batched('sij,sjk->sik', stat, basis)
    gram_matrix = batched('sji,sjk->sik', turned, turned)
    factor_low = jnp.linalg.cholesky(gram_matrix)
    solved = jax.scipy.linalg.solve_triangular(factor_low, turned.transpose(0, 2, 1), lower=True)
    return solved.transpose(0, 2, 1)

def soap_update(gradient, first_old, second_old, left_old, right_old, left_base, right_base):
    left_new = decay_rate * left_old + (1.0 - decay_rate) * batched('sij,skj->sik', gradient, gradient)
    right_new = decay_rate * right_old + (1.0 - decay_rate) * batched('sji,sjk->sik', gradient, gradient)
    turned = batched('sji,sjk->sik', left_base, batched('sij,sjk->sik', gradient, right_base))
    first_new = decay_rate * first_old + (1.0 - decay_rate) * turned
    second_new = decay_rate * second_old + (1.0 - decay_rate) * turned * turned
    correct = 1.0 - decay_rate ** STEP
    direction = first_new / correct / (jnp.sqrt(second_new / correct) + eps_adam)
    restored = batched('sij,sjk->sik', left_base, batched('sij,skj->sik', direction, right_base))
    return (restored, first_new, second_new, left_new, right_new, renew_basis(left_new, left_base), renew_basis(right_new, right_base))

def reference(tokens, cotangent, lengths, owners, w_qkv, w_out, w_up, w_down, norm_gains, gain_first, gain_second, moment_first, moment_second, left_stat, right_stat, left_basis, right_basis):
    masters = (w_qkv, w_out, w_up, w_down)
    matrices = tuple((to_matrix(layout) for layout in masters))

    def forward_all(inputs, matrix_set, gain_pairs):
        gain_low = low(gain_pairs)
        params = tuple((low(matrix) for matrix in matrix_set)) + (gain_low[0], gain_low[1])

        def scene_step(carry, scene_data):
            return (carry, jax.checkpoint(scene_forward)(params, scene_data))
        _, results = lax.scan(scene_step, None, (inputs.reshape(SCENES, SEQ, D), lengths))
        return results.reshape(TOKENS, D)
    block_out, pullback = jax.vjp(forward_all, tokens.astype(jnp.float32), matrices, norm_gains)
    grad_in, grad_mats, grad_gains = pullback(cotangent.astype(jnp.float32))
    total_squares = jnp.sum(grad_gains * grad_gains) + sum((jnp.sum(matrix * matrix) for matrix in grad_mats))
    grad_norm = jnp.sqrt(total_squares)
    factor = jnp.minimum(1.0, clip_bound / grad_norm)
    blocks = jnp.concatenate([to_blocks(matrix) for matrix in grad_mats], 0) * factor
    slots = slot_table(owners)
    slot_grads = jnp.zeros((SLOTS, BLOCK, BLOCK), jnp.float32).at[slots].set(blocks)
    restored, first_new, second_new, left_new, right_new, left_turn, right_turn = soap_update(slot_grads, moment_first, moment_second, left_stat, right_stat, left_basis, right_basis)
    back_blocks = restored[slots]
    fan_list = (2 * D, max(1, D * 16 // SEQ), D, FF)
    updated = []
    offset = 0
    for master, matrix, fan_in in zip(masters, matrices, fan_list):
        rows_n, cols_n = matrix.shape
        piece_count = rows_n // BLOCK * (cols_n // BLOCK)
        direction = from_blocks(back_blocks[offset:offset + piece_count], rows_n, cols_n)
        updated.append(master - fan_in ** (-0.5) * (direction + weight_decay * master))
        offset += piece_count
    clipped = grad_gains * factor
    gain_one_new = decay_rate * gain_first + (1.0 - decay_rate) * clipped
    gain_two_new = decay_rate * gain_second + (1.0 - decay_rate) * clipped * clipped
    correct = 1.0 - decay_rate ** STEP
    gain_values = norm_gains - gain_rate * (gain_one_new / correct) / (jnp.sqrt(gain_two_new / correct) + eps_adam)
    return (block_out.astype(jnp.bfloat16), grad_in.astype(jnp.bfloat16), grad_norm, updated[0], updated[1], updated[2], updated[3], gain_values, gain_one_new, gain_two_new, first_new, second_new, left_new, right_new, left_turn, right_turn)
```

```python
from functools import partial

import jax
import jax.numpy as jnp
from jax import lax
from jax.experimental import pallas as pl
from jax.experimental.pallas import tpu as pltpu
from jax.sharding import PartitionSpec as P

FF = 4096
HEADS = 16
HEAD = 64
BLOCK = 256
STEP = 10


eps_norm = 1e-05
eps_adam = 1e-08
decay_rate = 0.5
clip_bound = 1.0
weight_decay = 0.01
gain_rate = 1.0
neg_large = -1e30
highest = lax.Precision.HIGHEST
float32 = jnp.float32
bfloat16 = jnp.bfloat16
PAIR = 2 * HEAD
NT = (((1,), (1,)), ((), ()))
TN = (((0,), (0,)), ((), ()))
VMEM_LIMIT = 48 * 2**20


def shortened(shard):
    return jax.tree.map(lambda a: a.astype(jnp.bfloat16) if a.dtype == jnp.float32 else a, shard)


def normalize(values):
    center = values - jnp.mean(values, -1, keepdims=True)
    inverse = lax.rsqrt(jnp.mean(center * center, -1, keepdims=True) + eps_norm)
    return (center * inverse, inverse)


def norm_backward(d_result, normed, inverse, gain):
    scaled = d_result * gain
    d_gain = jnp.sum(d_result * normed, 0)
    d_input = inverse * (
        scaled
        - jnp.mean(scaled, -1, keepdims=True)
        - normed * jnp.mean(scaled * normed, -1, keepdims=True)
    )
    return (d_input, d_gain)


def as_layout(matrix):
    return matrix.reshape(matrix.shape[0] // BLOCK, BLOCK, matrix.shape[1])


def to_pieces(shard):
    band_count, band_rows, col_count = shard.shape
    return (
        shard.reshape(band_count, band_rows, col_count // BLOCK, BLOCK)
        .transpose(0, 2, 1, 3)
        .reshape(-1, band_rows, BLOCK)
    )


def from_pieces(pieces, band_count, col_count):
    band_rows = pieces.shape[1]
    return (
        pieces.reshape(band_count, col_count // BLOCK, band_rows, BLOCK)
        .transpose(0, 2, 1, 3)
        .reshape(band_count, band_rows, col_count)
    )


def one_head(matrix, head):
    lane = lax.broadcasted_iota(jnp.int32, matrix.shape, 1)
    return jnp.where(lane // HEAD == head, matrix, jnp.zeros_like(matrix))


def hide(scores, start, safe, length):
    if start + scores.shape[0] <= safe:
        return scores
    position = start + lax.broadcasted_iota(jnp.int32, scores.shape, 0)
    return jnp.where(position < length, scores, neg_large)


def attend_kernel(safe, chunk, length_ref, q_ref, k_ref, v_ref, o_ref, log_ref, vt_ref, s_ref):
    seq_len = k_ref.shape[0]
    length = length_ref[0]

    @pl.when(pl.program_id(1) == 0)
    def _():
        vt_ref[...] = v_ref[...].T

    outs = []
    for head in range(2):
        queries = one_head(q_ref[...], head) * bfloat16(HEAD**-0.5)
        topmost = None
        for at in range(0, seq_len, chunk):
            scores = lax.dot_general(
                k_ref[at : at + chunk, :], queries, NT, preferred_element_type=float32
            )
            scores = hide(scores, at, safe, length)
            s_ref[head, at : at + chunk, :] = scores
            top = jnp.max(scores, 0, keepdims=True)
            topmost = top if topmost is None else jnp.maximum(topmost, top)
        totals = jnp.zeros_like(topmost)
        mixed = jnp.zeros((HEAD, q_ref.shape[0]), float32)
        for at in range(0, seq_len, chunk):
            expo = jnp.exp(s_ref[head, at : at + chunk, :] - topmost)
            totals += jnp.sum(expo, 0, keepdims=True)
            mixed += jnp.dot(
                vt_ref[head * HEAD : (head + 1) * HEAD, at : at + chunk],
                expo.astype(bfloat16),
                preferred_element_type=float32,
            )
        outs.append(mixed * (1.0 / totals))
        log_ref[0, head : head + 1, :] = topmost + jnp.log(totals)
    o_ref[...] = jnp.concatenate(outs, 0).T.astype(bfloat16)


def attend(lengths, scene, safe, rows=1024, chunk=512):
    seq_len, width = scene.shape[0], scene.shape[1] // 3
    pairs = width // PAIR
    return pl.pallas_call(
        partial(attend_kernel, safe, chunk),
        grid=(pairs, seq_len // rows),
        in_specs=[
            pl.BlockSpec(memory_space=pltpu.SMEM),
            pl.BlockSpec((rows, PAIR), lambda p, i: (i, p)),
            pl.BlockSpec((seq_len, PAIR), lambda p, i: (0, pairs + p)),
            pl.BlockSpec((seq_len, PAIR), lambda p, i: (0, 2 * pairs + p)),
        ],
        out_specs=[
            pl.BlockSpec((rows, PAIR), lambda p, i: (i, p)),
            pl.BlockSpec((1, 2, rows), lambda p, i: (p, 0, i)),
        ],
        out_shape=[
            jax.ShapeDtypeStruct((seq_len, width), bfloat16),
            jax.ShapeDtypeStruct((pairs, 2, seq_len), float32),
        ],
        scratch_shapes=[
            pltpu.VMEM((PAIR, seq_len), bfloat16),
            pltpu.VMEM((2, seq_len, rows), float32),
        ],
        compiler_params=pltpu.CompilerParams(vmem_limit_bytes=VMEM_LIMIT),
        cost_estimate=pl.CostEstimate(
            flops=4 * pairs * 2 * 4 * seq_len * seq_len * HEAD,
            bytes_accessed=8 * seq_len * width,
            transcendentals=0,
        ),
    )(lengths, scene, scene, scene)


def attend_backward_kernel(
    safe, chunk, length_ref, q_ref, k_ref, v_ref, o_ref, do_ref, log_ref, dq_ref, dk_ref, dv_ref, kt_ref, dk_sum, dv_sum
):
    seq_len = k_ref.shape[0]
    length = length_ref[0]

    @pl.when(pl.program_id(1) == 0)
    def _():
        kt_ref[...] = k_ref[...].T
        dk_sum[...] = jnp.zeros_like(dk_sum)
        dv_sum[...] = jnp.zeros_like(dv_sum)

    products = (o_ref[...].astype(float32) * do_ref[...].astype(float32)).T
    turned = []
    for head in range(2):
        lanes = slice(head * HEAD, (head + 1) * HEAD)
        queries = one_head(q_ref[...], head) * bfloat16(HEAD**-0.5)
        d_mixed = one_head(do_ref[...], head)
        inner = jnp.sum(products[lanes, :], 0, keepdims=True)
        log_total = log_ref[0, head : head + 1, :]
        d_queries = jnp.zeros((HEAD, q_ref.shape[0]), float32)
        for at in range(0, seq_len, chunk):
            part = slice(at, at + chunk)
            scores = lax.dot_general(k_ref[part, :], queries, NT, preferred_element_type=float32)
            probs = jnp.exp(hide(scores, at, safe, length) - log_total)
            d_probs = lax.dot_general(v_ref[part, :], d_mixed, NT, preferred_element_type=float32)
            dv_sum[part, :] += jnp.dot(
                probs.astype(bfloat16), d_mixed, preferred_element_type=float32
            )
            d_scores = (probs * (d_probs - inner)).astype(bfloat16)
            dk_sum[part, :] += jnp.dot(d_scores, queries, preferred_element_type=float32)
            d_queries += jnp.dot(kt_ref[lanes, part], d_scores, preferred_element_type=float32)
        turned.append(d_queries * HEAD**-0.5)
    dq_ref[...] = jnp.concatenate(turned, 0).T.astype(bfloat16)

    @pl.when(pl.program_id(1) == pl.num_programs(1) - 1)
    def _():
        dk_ref[...] = dk_sum[...].astype(bfloat16)
        dv_ref[...] = dv_sum[...].astype(bfloat16)


def attend_backward(lengths, scene, mixed, d_mixed, log_totals, safe, rows=512, chunk=1024):
    seq_len, width = mixed.shape
    pairs = width // PAIR
    tile = pl.BlockSpec((rows, PAIR), lambda p, i: (i, p))
    full = pl.BlockSpec((seq_len, PAIR), lambda p, i: (0, p))
    return pl.pallas_call(
        partial(attend_backward_kernel, safe, chunk),
        grid=(pairs, seq_len // rows),
        in_specs=[
            pl.BlockSpec(memory_space=pltpu.SMEM),
            tile,
            pl.BlockSpec((seq_len, PAIR), lambda p, i: (0, pairs + p)),
            pl.BlockSpec((seq_len, PAIR), lambda p, i: (0, 2 * pairs + p)),
            tile,
            tile,
            pl.BlockSpec((1, 2, rows), lambda p, i: (p, 0, i)),
        ],
        out_specs=[tile, full, full],
        out_shape=[jax.ShapeDtypeStruct((seq_len, width), bfloat16)] * 3,
        scratch_shapes=[
            pltpu.VMEM((PAIR, seq_len), bfloat16),
            pltpu.VMEM((seq_len, PAIR), float32),
            pltpu.VMEM((seq_len, PAIR), float32),
        ],
        compiler_params=pltpu.CompilerParams(vmem_limit_bytes=VMEM_LIMIT),
        cost_estimate=pl.CostEstimate(
            flops=4 * pairs * 2 * 10 * seq_len * seq_len * HEAD,
            bytes_accessed=16 * seq_len * width,
            transcendentals=0,
        ),
    )(lengths, scene, scene, scene, mixed, d_mixed, log_totals)


def exact(left, right, dims=(((1,), (0,)), ((), ()))):
    return lax.dot_general(left, right, dims, precision=highest, preferred_element_type=float32)


def soap_kernel(
    g_ref, first_ref, second_ref, ls_ref, rs_ref, lb_ref, rb_ref,
    back_ref, first_out, second_out, ls_out, rs_out, gram_ref, turn_ref,
):
    gradient = g_ref[0].astype(float32)
    left_base, right_base = lb_ref[0], rb_ref[0]
    left_new = decay_rate * ls_ref[0] + (1.0 - decay_rate) * exact(gradient, gradient, NT)
    right_new = decay_rate * rs_ref[0] + (1.0 - decay_rate) * exact(gradient, gradient, TN)
    ls_out[0] = left_new
    rs_out[0] = right_new
    turned = exact(left_base, exact(gradient, right_base), TN)
    first_new = decay_rate * first_ref[0] + (1.0 - decay_rate) * turned
    second_new = decay_rate * second_ref[0] + (1.0 - decay_rate) * turned * turned
    first_out[0] = first_new
    second_out[0] = second_new
    correct = 1.0 - decay_rate**STEP
    direction = first_new / correct / (jnp.sqrt(second_new / correct) + eps_adam)
    back_ref[0] = exact(left_base, exact(direction, right_base, NT)).astype(back_ref.dtype)
    for side, stat, base in ((0, left_new, left_base), (1, right_new, right_base)):
        turn = exact(stat, base).T
        turn_ref[0, side] = turn
        gram_ref[0, side] = exact(turn, turn, NT)


def soap_update(gradient, first_old, second_old, left_old, right_old, left_base, right_base):
    slots, order, _ = gradient.shape
    one = pl.BlockSpec((1, order, order), lambda s: (s, 0, 0))
    two = pl.BlockSpec((1, 2, order, order), lambda s: (s, 0, 0, 0))
    single = jax.ShapeDtypeStruct((slots, order, order), float32)
    double = jax.ShapeDtypeStruct((slots, 2, order, order), float32)
    return pl.pallas_call(
        soap_kernel,
        grid=(slots,),
        in_specs=[one] * 7,
        out_specs=[one] * 5 + [two] * 2,
        out_shape=[jax.ShapeDtypeStruct((slots, order, order), bfloat16)] + [single] * 4 + [double] * 2,
        compiler_params=pltpu.CompilerParams(vmem_limit_bytes=VMEM_LIMIT),
        cost_estimate=pl.CostEstimate(
            flops=slots * 120 * order**3, bytes_accessed=slots * 60 * order**2, transcendentals=0
        ),
    )(gradient, first_old, second_old, left_old, right_old, left_base, right_base)


def renew_kernel(rows, gram_ref, turn_ref, q_ref, x_ref, u_ref):
    count, order = gram_ref.shape[0], gram_ref.shape[1]
    eye = (
        lax.broadcasted_iota(jnp.int32, (rows, rows), 0)
        == lax.broadcasted_iota(jnp.int32, (rows, rows), 1)
    ).astype(float32)
    sublane = lax.broadcasted_iota(jnp.int32, (1, 8, 1), 1)
    for low in range(0, order, rows):
        part = slice(low, low + rows)

        def panel(at, carry, low=low, part=part):
            row = jnp.concatenate([gram_ref[at, part, :], turn_ref[at, part, :]], 1)
            if low:
                row = row - exact(u_ref[at, :low, part], u_ref[at, :low, :], TN)
            u_ref[at, part, :] = row
            x_ref[at] = jnp.concatenate([row[:, part], eye], 1)
            return carry

        lax.fori_loop(0, count, panel, 0, unroll=2)
        for j in range(rows):
            tile = j // 8 * 8
            row = x_ref[:, j : j + 1, :]
            row = row * (1.0 / row[:, :, j : j + 1])
            top = x_ref[:, tile : tile + 8, :]
            below = jnp.where(sublane > j - tile, top[:, :, j : j + 1], 0.0)
            x_ref[:, tile : tile + 8, :] = top - below * row
            if tile + 8 < rows:
                rest = x_ref[:, tile + 8 :, :]
                x_ref[:, tile + 8 :, :] = rest - rest[:, :, j : j + 1] * row

        def solve(at, carry, part=part):
            both = x_ref[at]
            diagonal = jnp.sum(both[:, :rows] * eye, 1, keepdims=True)
            u_ref[at, part, :] = exact(both[:, rows:] * lax.rsqrt(diagonal), u_ref[at, part, :])
            return carry

        lax.fori_loop(0, count, solve, 0, unroll=2)

    def turn_back(at, carry):
        q_ref[at] = u_ref[at, :, order:].T
        return carry

    lax.fori_loop(0, count, turn_back, 0)


def renew_bases(gram, turn, rows=64):
    count, order, _ = gram.shape
    return pl.pallas_call(
        partial(renew_kernel, rows),
        out_shape=jax.ShapeDtypeStruct(gram.shape, float32),
        in_specs=[pl.BlockSpec(memory_space=pltpu.VMEM)] * 2,
        out_specs=pl.BlockSpec(memory_space=pltpu.VMEM),
        scratch_shapes=[
            pltpu.VMEM((count, rows, 2 * rows), float32),
            pltpu.VMEM((count, order, 2 * order), float32),
        ],
        compiler_params=pltpu.CompilerParams(vmem_limit_bytes=VMEM_LIMIT),
        cost_estimate=pl.CostEstimate(
            flops=count * 200 * order**3, bytes_accessed=count * 12 * order**2, transcendentals=0
        ),
    )(gram, turn)


def exchange(groups):
    return lax.all_to_all(groups, "narrow", split_axis=0, concat_axis=0, tiled=True)


def scattered(layout, dimension):
    return lax.psum_scatter(
        layout.astype(bfloat16), ("wide", "narrow"), scatter_dimension=dimension, tiled=True
    ).astype(float32)


def unpack(gathered):
    matrices = [
        layout.reshape(layout.shape[0] * layout.shape[1], layout.shape[2])
        for layout in gathered[:4]
    ]
    return (matrices, gathered[4].astype(jnp.float32))


def global_norm(squares):
    return jnp.sqrt(lax.psum(squares, ("wide", "narrow")))


def body(
    tokens,
    cotangent,
    lengths,
    owners,
    w_qkv,
    w_out,
    w_up,
    w_down,
    norm_gains,
    gain_first,
    gain_second,
    moment_first,
    moment_second,
    left_stat,
    right_stat,
    left_basis,
    right_basis,
):
    tok_rows, width = tokens.shape
    narrow_count = lax.axis_size("narrow")
    device_count = lax.axis_size("wide") * narrow_count
    seq_len = tok_rows * narrow_count
    cap_slots = moment_first.shape[0]
    masters = (w_qkv, w_out, w_up, w_down)
    lowered = tuple((layout.astype(jnp.bfloat16) for layout in masters)) + (
        norm_gains.astype(jnp.bfloat16),
    )
    weight_list, gain_pair = unpack(
        jax.tree.map(
            lambda part, own: part.astype(own.dtype),
            lax.all_gather(shortened(lowered), ("wide", "narrow"), axis=1, tiled=True),
            lowered,
        )
    )
    w_attn, w_proj, w_hidden, w_back = weight_list
    inputs = tokens.astype(jnp.float32)
    normed_one, inverse_one = normalize(inputs)
    act_one = (normed_one * gain_pair[0]).astype(jnp.bfloat16)
    head_width = width // narrow_count
    safe = seq_len - tok_rows
    w_groups = w_attn.reshape(width, 3, narrow_count, head_width)
    packed = jnp.einsum("td,dkge->gtke", act_one, w_groups, preferred_element_type=jnp.float32)
    packed = packed.astype(jnp.bfloat16).reshape(narrow_count, tok_rows, 3 * head_width)
    scene = exchange(packed).reshape(seq_len, 3 * head_width)
    mixed, log_totals = attend(lengths, scene, safe)
    merged = exchange(mixed.reshape(narrow_count, tok_rows, head_width))
    merged = merged.transpose(1, 0, 2).reshape(tok_rows, width)
    middle = inputs + jnp.dot(merged, w_proj, preferred_element_type=jnp.float32)
    normed_two, inverse_two = normalize(middle)
    act_two = (normed_two * gain_pair[1]).astype(jnp.bfloat16)
    hidden = jnp.dot(act_two, w_hidden, preferred_element_type=jnp.float32)
    active = jax.nn.gelu(hidden, approximate=True).astype(jnp.bfloat16)
    block_out = (middle + jnp.dot(active, w_back, preferred_element_type=jnp.float32)).astype(
        jnp.bfloat16
    )
    d_back = jnp.einsum("tf,td->fd", active, cotangent, preferred_element_type=jnp.float32)
    d_active = jnp.einsum("td,fd->tf", cotangent, w_back, preferred_element_type=jnp.float32)
    _, gelu_pull = jax.vjp(partial(jax.nn.gelu, approximate=True), hidden)
    d_hidden = gelu_pull(d_active)[0].astype(jnp.bfloat16)
    d_w_hidden = jnp.einsum("td,tf->df", act_two, d_hidden, preferred_element_type=jnp.float32)
    d_act_two = jnp.einsum("tf,df->td", d_hidden, w_hidden, preferred_element_type=jnp.float32)
    d_norm_two, d_gain_two = norm_backward(d_act_two, normed_two, inverse_two, gain_pair[1])
    d_middle = cotangent.astype(jnp.float32) + d_norm_two
    mlp_sums = (scattered(as_layout(d_w_hidden), 1), scattered(as_layout(d_back), 1))
    d_branch = d_middle.astype(jnp.bfloat16)
    d_proj = jnp.einsum("td,te->de", merged, d_branch, preferred_element_type=jnp.float32)
    d_merged = jnp.einsum("te,de->td", d_branch, w_proj, preferred_element_type=jnp.float32).astype(
        jnp.bfloat16
    )
    d_mixed = d_merged.reshape(tok_rows, narrow_count, head_width).transpose(1, 0, 2)
    d_mixed = exchange(d_mixed).reshape(seq_len, head_width)
    d_scene = jnp.concatenate(attend_backward(lengths, scene, mixed, d_mixed, log_totals, safe), 1)
    d_packed = exchange(d_scene.reshape(narrow_count, tok_rows, 3 * head_width))
    d_attn = jnp.einsum("td,gtc->gdc", act_one, d_packed, preferred_element_type=jnp.float32)
    d_act_one = jnp.einsum(
        "gtke,dkge->td",
        d_packed.reshape(narrow_count, tok_rows, 3, head_width),
        w_groups,
        preferred_element_type=jnp.float32,
    )
    d_norm_one, d_gain_one = norm_backward(d_act_one, normed_one, inverse_one, gain_pair[0])
    grad_tokens = (d_middle + d_norm_one).astype(jnp.bfloat16)
    attn_sum = scattered(d_attn.reshape(narrow_count, -1, BLOCK, 3 * head_width), 2)
    band_rows = attn_sum.shape[2]
    attn_sum = attn_sum.reshape(narrow_count, -1, band_rows, 3, head_width)
    attn_sum = attn_sum.transpose(1, 2, 3, 0, 4).reshape(-1, band_rows, 3 * width)
    attn_sums = (
        attn_sum,
        scattered(as_layout(d_proj), 1),
        lax.psum_scatter(
            jnp.stack([d_gain_one, d_gain_two]), ("wide", "narrow"), scatter_dimension=1, tiled=True
        ),
    )
    grad_shards = (attn_sums[0], attn_sums[1], mlp_sums[0], mlp_sums[1])
    gain_grad = attn_sums[2]
    local_squares = jnp.sum(gain_grad * gain_grad) + sum(
        (jnp.sum(shard * shard) for shard in grad_shards)
    )
    pieces = jnp.concatenate([to_pieces(shard) for shard in grad_shards], 0)
    block_count = pieces.shape[0]
    order = lax.iota(jnp.int32, block_count)
    earlier = (owners[None, :] == owners[:, None]) & (order[None, :] < order[:, None])
    slots = owners * cap_slots + jnp.sum(earlier.astype(jnp.int32), 1)
    routing = (slots[None, :] == lax.iota(jnp.int32, device_count * cap_slots)[:, None]).astype(
        jnp.float32
    )
    routing = routing.reshape(device_count, cap_slots, block_count)
    grad_norm = global_norm(local_squares)
    factor = jnp.minimum(1.0, clip_bound / grad_norm)
    outgoing = pieces * factor
    arrived = lax.all_to_all(
        jnp.einsum("okb,bxy->koxy", routing, outgoing, precision=highest).astype(jnp.bfloat16),
        ("wide", "narrow"),
        split_axis=1,
        concat_axis=1,
        tiled=True,
    ).astype(jnp.float32)
    slot_grads = arrived.reshape(cap_slots, BLOCK, BLOCK)
    restored, first_new, second_new, left_new, right_new, gram, turn = soap_update(
        slot_grads, moment_first, moment_second, left_stat, right_stat, left_basis, right_basis
    )
    square = (-1, BLOCK, BLOCK)
    bases = renew_bases(gram.reshape(square), turn.reshape(square))
    bases = bases.reshape(cap_slots, 2, BLOCK, BLOCK)
    left_turn, right_turn = bases[:, 0], bases[:, 1]
    returned = lax.all_to_all(
        shortened(restored.reshape(cap_slots, device_count, -1, BLOCK)),
        ("wide", "narrow"),
        split_axis=1,
        concat_axis=1,
        tiled=True,
    )
    back_pieces = jnp.einsum("okb,koxy->bxy", routing, returned, precision=highest)
    fan_list = (2 * width, max(1, width * 16 // seq_len), width, FF)
    updated = []
    offset = 0
    for master, fan_in in zip(masters, fan_list):
        band_count, band_rows, col_count = master.shape
        piece_count = band_count * (col_count // BLOCK)
        direction = from_pieces(back_pieces[offset : offset + piece_count], band_count, col_count)
        updated.append(master - fan_in ** (-0.5) * (direction + weight_decay * master))
        offset += piece_count
    clipped = gain_grad * factor
    gain_one_new = decay_rate * gain_first + (1.0 - decay_rate) * clipped
    gain_two_new = decay_rate * gain_second + (1.0 - decay_rate) * clipped * clipped
    correct = 1.0 - decay_rate**STEP
    gain_values = norm_gains - gain_rate * (gain_one_new / correct) / (
        jnp.sqrt(gain_two_new / correct) + eps_adam
    )
    return (
        block_out,
        grad_tokens,
        grad_norm,
        updated[0],
        updated[1],
        updated[2],
        updated[3],
        gain_values,
        gain_one_new,
        gain_two_new,
        first_new,
        second_new,
        left_new,
        right_new,
        left_turn,
        right_turn,
    )


def solution(mesh):
    in_specs = (
        P(("wide", "narrow"), None),
        P(("wide", "narrow"), None),
        P("wide"),
        P(),
        P(None, ("wide", "narrow"), None),
        P(None, ("wide", "narrow"), None),
        P(None, ("wide", "narrow"), None),
        P(None, ("wide", "narrow"), None),
        P(None, ("wide", "narrow")),
        P(None, ("wide", "narrow")),
        P(None, ("wide", "narrow")),
        P(("wide", "narrow"), None, None),
        P(("wide", "narrow"), None, None),
        P(("wide", "narrow"), None, None),
        P(("wide", "narrow"), None, None),
        P(("wide", "narrow"), None, None),
        P(("wide", "narrow"), None, None),
    )
    out_specs = (
        P(("wide", "narrow"), None),
        P(("wide", "narrow"), None),
        P(),
        P(None, ("wide", "narrow"), None),
        P(None, ("wide", "narrow"), None),
        P(None, ("wide", "narrow"), None),
        P(None, ("wide", "narrow"), None),
        P(None, ("wide", "narrow")),
        P(None, ("wide", "narrow")),
        P(None, ("wide", "narrow")),
        P(("wide", "narrow"), None, None),
        P(("wide", "narrow"), None, None),
        P(("wide", "narrow"), None, None),
        P(("wide", "narrow"), None, None),
        P(("wide", "narrow"), None, None),
        P(("wide", "narrow"), None, None),
    )
    return jax.shard_map(body, mesh=mesh, in_specs=in_specs, out_specs=out_specs, check_vma=False)
```

```python
from functools import partial

import jax
import jax.numpy as jnp
from jax import lax
from jax.experimental import pallas as pl
from jax.experimental.pallas import tpu as pltpu
from jax.sharding import PartitionSpec as P

FF = 4096
HEADS = 16
HEAD = 64
BLOCK = 256
STEP = 10


eps_norm = 1e-05
eps_adam = 1e-08
decay_rate = 0.5
clip_bound = 1.0
weight_decay = 0.01
gain_rate = 1.0
neg_large = -1e30
highest = lax.Precision.HIGHEST
float32 = jnp.float32
bfloat16 = jnp.bfloat16
PAIR = 2 * HEAD
NT = (((1,), (1,)), ((), ()))
TN = (((0,), (0,)), ((), ()))
MESH = pl.DeviceIdType.MESH
VMEM_LIMIT = 48 * 2**20
AHEAD = 4


def shortened(shard):
    return jax.tree.map(lambda a: a.astype(jnp.bfloat16) if a.dtype == jnp.float32 else a, shard)


def normalize(values):
    center = values - jnp.mean(values, -1, keepdims=True)
    inverse = lax.rsqrt(jnp.mean(center * center, -1, keepdims=True) + eps_norm)
    return (center * inverse, inverse)


def norm_backward(d_result, normed, inverse, gain):
    scaled = d_result * gain
    d_gain = jnp.sum(d_result * normed, 0)
    d_input = inverse * (
        scaled
        - jnp.mean(scaled, -1, keepdims=True)
        - normed * jnp.mean(scaled * normed, -1, keepdims=True)
    )
    return (d_input, d_gain)


def from_pieces(pieces, band_count, col_count):
    band_rows = pieces.shape[1]
    return (
        pieces.reshape(band_count, col_count // BLOCK, band_rows, BLOCK)
        .transpose(0, 2, 1, 3)
        .reshape(band_count, band_rows, col_count)
    )


def one_head(matrix, head):
    lane = lax.broadcasted_iota(jnp.int32, matrix.shape, 1)
    return jnp.where(lane // HEAD == head, matrix, jnp.zeros_like(matrix))


def hide(scores, start, safe, length):
    if start + scores.shape[0] <= safe:
        return scores
    position = start + lax.broadcasted_iota(jnp.int32, scores.shape, 0)
    return jnp.where(position < length, scores, neg_large)


def attend_kernel(safe, chunk, length_ref, q_ref, k_ref, v_ref, o_ref, log_ref, vt_ref, s_ref):
    seq_len = k_ref.shape[0]
    length = length_ref[0]

    @pl.when(pl.program_id(1) == 0)
    def _():
        vt_ref[...] = v_ref[...].T

    outs = []
    for head in range(2):
        queries = one_head(q_ref[...], head) * bfloat16(HEAD**-0.5)
        topmost = None
        for at in range(0, seq_len, chunk):
            scores = lax.dot_general(
                k_ref[at : at + chunk, :], queries, NT, preferred_element_type=float32
            )
            scores = hide(scores, at, safe, length)
            s_ref[head, at : at + chunk, :] = scores
            top = jnp.max(scores, 0, keepdims=True)
            topmost = top if topmost is None else jnp.maximum(topmost, top)
        totals = jnp.zeros_like(topmost)
        mixed = jnp.zeros((HEAD, q_ref.shape[0]), float32)
        for at in range(0, seq_len, chunk):
            expo = jnp.exp(s_ref[head, at : at + chunk, :] - topmost)
            totals += jnp.sum(expo, 0, keepdims=True)
            mixed += jnp.dot(
                vt_ref[head * HEAD : (head + 1) * HEAD, at : at + chunk],
                expo.astype(bfloat16),
                preferred_element_type=float32,
            )
        outs.append(mixed * (1.0 / totals))
        log_ref[0, head : head + 1, :] = topmost + jnp.log(totals)
    o_ref[...] = jnp.concatenate(outs, 0).T.astype(bfloat16)


def attend(lengths, scene, safe, rows=1024, chunk=512):
    seq_len, width = scene.shape[0], scene.shape[1] // 3
    pairs = width // PAIR
    return pl.pallas_call(
        partial(attend_kernel, safe, chunk),
        grid=(pairs, seq_len // rows),
        in_specs=[
            pl.BlockSpec(memory_space=pltpu.SMEM),
            pl.BlockSpec((rows, PAIR), lambda p, i: (i, p)),
            pl.BlockSpec((seq_len, PAIR), lambda p, i: (0, pairs + p)),
            pl.BlockSpec((seq_len, PAIR), lambda p, i: (0, 2 * pairs + p)),
        ],
        out_specs=[
            pl.BlockSpec((rows, PAIR), lambda p, i: (i, p)),
            pl.BlockSpec((1, 2, rows), lambda p, i: (p, 0, i)),
        ],
        out_shape=[
            jax.ShapeDtypeStruct((seq_len, width), bfloat16),
            jax.ShapeDtypeStruct((pairs, 2, seq_len), float32),
        ],
        scratch_shapes=[
            pltpu.VMEM((PAIR, seq_len), bfloat16),
            pltpu.VMEM((2, seq_len, rows), float32),
        ],
        compiler_params=pltpu.CompilerParams(vmem_limit_bytes=VMEM_LIMIT),
        cost_estimate=pl.CostEstimate(
            flops=4 * pairs * 2 * 4 * seq_len * seq_len * HEAD,
            bytes_accessed=8 * seq_len * width,
            transcendentals=0,
        ),
    )(lengths, scene, scene, scene)


def attend_backward_kernel(
    safe, chunk, length_ref, q_ref, k_ref, v_ref, o_ref, do_ref, log_ref, dq_ref, dk_ref, dv_ref, kt_ref, dk_sum, dv_sum
):
    seq_len = k_ref.shape[0]
    length = length_ref[0]

    @pl.when(pl.program_id(1) == 0)
    def _():
        kt_ref[...] = k_ref[...].T
        dk_sum[...] = jnp.zeros_like(dk_sum)
        dv_sum[...] = jnp.zeros_like(dv_sum)

    products = (o_ref[...].astype(float32) * do_ref[...].astype(float32)).T
    turned = []
    for head in range(2):
        lanes = slice(head * HEAD, (head + 1) * HEAD)
        queries = one_head(q_ref[...], head) * bfloat16(HEAD**-0.5)
        d_mixed = one_head(do_ref[...], head)
        inner = jnp.sum(products[lanes, :], 0, keepdims=True)
        log_total = log_ref[0, head : head + 1, :]
        d_queries = jnp.zeros((HEAD, q_ref.shape[0]), float32)
        for at in range(0, seq_len, chunk):
            part = slice(at, at + chunk)
            scores = lax.dot_general(k_ref[part, :], queries, NT, preferred_element_type=float32)
            probs = jnp.exp(hide(scores, at, safe, length) - log_total)
            d_probs = lax.dot_general(v_ref[part, :], d_mixed, NT, preferred_element_type=float32)
            dv_sum[part, :] += jnp.dot(
                probs.astype(bfloat16), d_mixed, preferred_element_type=float32
            )
            d_scores = (probs * (d_probs - inner)).astype(bfloat16)
            dk_sum[part, :] += jnp.dot(d_scores, queries, preferred_element_type=float32)
            d_queries += jnp.dot(kt_ref[lanes, part], d_scores, preferred_element_type=float32)
        turned.append(d_queries * HEAD**-0.5)
    dq_ref[...] = jnp.concatenate(turned, 0).T.astype(bfloat16)

    @pl.when(pl.program_id(1) == pl.num_programs(1) - 1)
    def _():
        dk_ref[...] = dk_sum[...].astype(bfloat16)
        dv_ref[...] = dv_sum[...].astype(bfloat16)


def attend_backward(lengths, scene, mixed, d_mixed, log_totals, safe, rows=512, chunk=1024):
    seq_len, width = mixed.shape
    pairs = width // PAIR
    tile = pl.BlockSpec((rows, PAIR), lambda p, i: (i, p))
    full = pl.BlockSpec((seq_len, PAIR), lambda p, i: (0, p))
    return pl.pallas_call(
        partial(attend_backward_kernel, safe, chunk),
        grid=(pairs, seq_len // rows),
        in_specs=[
            pl.BlockSpec(memory_space=pltpu.SMEM),
            tile,
            pl.BlockSpec((seq_len, PAIR), lambda p, i: (0, pairs + p)),
            pl.BlockSpec((seq_len, PAIR), lambda p, i: (0, 2 * pairs + p)),
            tile,
            tile,
            pl.BlockSpec((1, 2, rows), lambda p, i: (p, 0, i)),
        ],
        out_specs=[tile, full, full],
        out_shape=[jax.ShapeDtypeStruct((seq_len, width), bfloat16)] * 3,
        scratch_shapes=[
            pltpu.VMEM((PAIR, seq_len), bfloat16),
            pltpu.VMEM((seq_len, PAIR), float32),
            pltpu.VMEM((seq_len, PAIR), float32),
        ],
        compiler_params=pltpu.CompilerParams(vmem_limit_bytes=VMEM_LIMIT),
        cost_estimate=pl.CostEstimate(
            flops=4 * pairs * 2 * 10 * seq_len * seq_len * HEAD,
            bytes_accessed=16 * seq_len * width,
            transcendentals=0,
        ),
    )(lengths, scene, scene, scene, mixed, d_mixed, log_totals)


def exact(left, right, dims=(((1,), (0,)), ((), ()))):
    return lax.dot_general(left, right, dims, precision=highest, preferred_element_type=float32)


def soap_kernel(
    factor_ref, g_ref, first_ref, second_ref, ls_ref, rs_ref, lb_ref, rb_ref,
    back_ref, first_out, second_out, ls_out, rs_out, gram_ref, turn_ref,
):
    gradient = factor_ref[0, 0] * g_ref[0].astype(float32)
    left_base, right_base = lb_ref[0], rb_ref[0]
    left_new = decay_rate * ls_ref[0] + (1.0 - decay_rate) * exact(gradient, gradient, NT)
    right_new = decay_rate * rs_ref[0] + (1.0 - decay_rate) * exact(gradient, gradient, TN)
    ls_out[0] = left_new
    rs_out[0] = right_new
    turned = exact(left_base, exact(gradient, right_base), TN)
    first_new = decay_rate * first_ref[0] + (1.0 - decay_rate) * turned
    second_new = decay_rate * second_ref[0] + (1.0 - decay_rate) * turned * turned
    first_out[0] = first_new
    second_out[0] = second_new
    correct = 1.0 - decay_rate**STEP
    direction = first_new / correct / (jnp.sqrt(second_new / correct) + eps_adam)
    back_ref[0] = exact(left_base, exact(direction, right_base, NT)).astype(back_ref.dtype)
    for side, stat, base in ((0, left_new, left_base), (1, right_new, right_base)):
        turn = exact(stat, base).T
        turn_ref[0, side] = turn
        gram_ref[0, side] = exact(turn, turn, NT)


def soap_update(factor, gradient, first_old, second_old, left_old, right_old, left_base, right_base):
    slots, order, _ = gradient.shape
    one = pl.BlockSpec((1, order, order), lambda s: (s, 0, 0))
    two = pl.BlockSpec((1, 2, order, order), lambda s: (s, 0, 0, 0))
    single = jax.ShapeDtypeStruct((slots, order, order), float32)
    double = jax.ShapeDtypeStruct((slots, 2, order, order), float32)
    return pl.pallas_call(
        soap_kernel,
        grid=(slots,),
        in_specs=[pl.BlockSpec(memory_space=pltpu.SMEM)] + [one] * 7,
        out_specs=[one] * 5 + [two] * 2,
        out_shape=[jax.ShapeDtypeStruct((slots, order, order), bfloat16)] + [single] * 4 + [double] * 2,
        compiler_params=pltpu.CompilerParams(vmem_limit_bytes=VMEM_LIMIT),
        cost_estimate=pl.CostEstimate(
            flops=slots * 120 * order**3, bytes_accessed=slots * 60 * order**2, transcendentals=0
        ),
    )(factor.reshape(1, 1), gradient, first_old, second_old, left_old, right_old, left_base, right_base)


def renew_kernel(rows, gram_ref, turn_ref, q_ref, x_ref, u_ref):
    count, order = gram_ref.shape[0], gram_ref.shape[1]
    eye = (
        lax.broadcasted_iota(jnp.int32, (rows, rows), 0)
        == lax.broadcasted_iota(jnp.int32, (rows, rows), 1)
    ).astype(float32)
    sublane = lax.broadcasted_iota(jnp.int32, (1, 8, 1), 1)
    for low in range(0, order, rows):
        part = slice(low, low + rows)

        def panel(at, carry, low=low, part=part):
            row = jnp.concatenate([gram_ref[at, part, :], turn_ref[at, part, :]], 1)
            if low:
                row = row - exact(u_ref[at, :low, part], u_ref[at, :low, :], TN)
            u_ref[at, part, :] = row
            x_ref[at] = jnp.concatenate([row[:, part], eye], 1)
            return carry

        lax.fori_loop(0, count, panel, 0, unroll=2)
        for j in range(rows):
            tile = j // 8 * 8
            row = x_ref[:, j : j + 1, :]
            row = row * (1.0 / row[:, :, j : j + 1])
            top = x_ref[:, tile : tile + 8, :]
            below = jnp.where(sublane > j - tile, top[:, :, j : j + 1], 0.0)
            x_ref[:, tile : tile + 8, :] = top - below * row
            if tile + 8 < rows:
                rest = x_ref[:, tile + 8 :, :]
                x_ref[:, tile + 8 :, :] = rest - rest[:, :, j : j + 1] * row

        def solve(at, carry, part=part):
            both = x_ref[at]
            diagonal = jnp.sum(both[:, :rows] * eye, 1, keepdims=True)
            u_ref[at, part, :] = exact(both[:, rows:] * lax.rsqrt(diagonal), u_ref[at, part, :])
            return carry

        lax.fori_loop(0, count, solve, 0, unroll=2)

    def turn_back(at, carry):
        q_ref[at] = u_ref[at, :, order:].T
        return carry

    lax.fori_loop(0, count, turn_back, 0)


def renew_bases(gram, turn, rows=64):
    count, order, _ = gram.shape
    return pl.pallas_call(
        partial(renew_kernel, rows),
        out_shape=jax.ShapeDtypeStruct(gram.shape, float32),
        in_specs=[pl.BlockSpec(memory_space=pltpu.VMEM)] * 2,
        out_specs=pl.BlockSpec(memory_space=pltpu.VMEM),
        scratch_shapes=[
            pltpu.VMEM((count, rows, 2 * rows), float32),
            pltpu.VMEM((count, order, 2 * order), float32),
        ],
        compiler_params=pltpu.CompilerParams(vmem_limit_bytes=VMEM_LIMIT),
        cost_estimate=pl.CostEstimate(
            flops=count * 200 * order**3, bytes_accessed=count * 12 * order**2, transcendentals=0
        ),
    )(gram, turn)


def exchange(groups):
    return lax.all_to_all(groups, "narrow", split_axis=0, concat_axis=0, tiled=True)


def partner(bit, narrow_bits):
    axis, step = ("narrow", 1 << bit) if bit < narrow_bits else ("wide", 1 << (bit - narrow_bits))
    place = lax.axis_index(axis)
    mine = lax.rem(place // step, 2)
    return {axis: place + step - 2 * step * mine}, mine


def greet(peers):
    barrier = pltpu.get_barrier_semaphore()
    for device, _ in peers:
        pl.semaphore_signal(barrier, inc=1, device_id=device, device_id_type=MESH)
    pl.semaphore_wait(barrier, len(peers))


def mesh_bits():
    narrow_bits = lax.axis_size("narrow").bit_length() - 1
    return narrow_bits + lax.axis_size("wide").bit_length() - 1, narrow_bits


def reduce_kernel(bits, narrow_bits, plans, chunks, count, *refs):
    sources, outs, scratch = refs[:count], refs[count : 2 * count], refs[2 * count :]
    held = scratch[:count]
    arrived = [scratch[count * (1 + s) : count * (2 + s)] for s in range(bits)]
    load_sem, send_sem, recv_sem = scratch[count * (1 + bits) :]
    peers = [partner(b, narrow_bits) for b in range(bits)]
    greet(peers)
    first = plans[0][0]
    order_of_dims = list(reversed(range(bits)))
    whole = slice(None)

    def within(order, stage, current):
        return tuple(
            peers[b][1] if b in order[:stage] else current if b == order[stage] else whole
            for b in order_of_dims
            if b != first
        )

    def of_source(value):
        return tuple(value if b == first else whole for b in order_of_dims)

    def rows_of(chunk):
        at, row, rows, colour = chunks[chunk]
        return at, plans[colour], (pl.ds(row, rows), whole)

    def send(chunk, stage):
        at, order, part = rows_of(chunk)
        device, mine = peers[order[stage]]
        if stage == 0:
            source = sources[at].at[of_source(1 - mine) + part]
        else:
            source = held[at].at[within(order, stage, 1 - mine) + part]
        return pltpu.make_async_remote_copy(
            src_ref=source,
            dst_ref=arrived[stage][at].at[(whole,) * (bits - 1 - stage) + part],
            send_sem=send_sem.at[chunk, stage],
            recv_sem=recv_sem.at[chunk, stage],
            device_id=device,
            device_id_type=MESH,
        )

    def load(chunk):
        at, order, part = rows_of(chunk)
        return pltpu.make_async_copy(
            sources[at].at[of_source(peers[first][1]) + part],
            held[at].at[(whole,) * (bits - 1) + part],
            load_sem.at[chunk],
        )

    def begin(chunk):
        send(chunk, 0).start()
        load(chunk).start()

    def finish(chunk, stage):
        at, order, part = rows_of(chunk)
        if stage == 0:
            load(chunk).wait()
        send(chunk, stage).wait_recv()
        left = bits - 1 - stage
        keep = within(order, stage, peers[order[stage]][1])
        if left == 0:
            own = held[at][keep + part].astype(float32)
            outs[at][part] = own + arrived[stage][at][part].astype(float32)
            return
        free = [i for i, k in enumerate(keep) if isinstance(k, slice)]

        def add(m, carry):
            which = tuple(m // (1 << (left - 1 - i)) % 2 for i in range(left))
            spot = list(keep)
            for i, f in enumerate(free):
                spot[f] = which[i]
            spot = tuple(spot) + part
            held[at][spot] = held[at][spot] + arrived[stage][at][which + part]
            return carry

        lax.fori_loop(0, 1 << left, add, 0)
        send(chunk, stage + 1).start()

    total = len(chunks)
    for chunk in range(min(AHEAD, total)):
        begin(chunk)
    for step in range(total + 2 * bits):
        for stage in reversed(range(bits)):
            chunk = step - 2 * stage
            if 0 <= chunk < total:
                finish(chunk, stage)
                if stage == 0 and chunk + AHEAD < total:
                    begin(chunk + AHEAD)
    for chunk in range(total):
        for stage in range(bits):
            send(chunk, stage).wait_send()


def reduce_to_shards(parts, pieces, collective_id):
    bits, narrow_bits = mesh_bits()
    shapes = [part.shape[1:] for part in parts]
    kinds = [part.dtype for part in parts]
    chunks = []
    for at, (shape, cut) in enumerate(zip(shapes, pieces)):
        rows = shape[0] // cut
        chunks += [(at, row, rows, len(chunks) % 2) for row in range(0, shape[0], rows)]
        chunks = [(a, r, n, i % 2) for i, (a, r, n, _) in enumerate(chunks)]
    later = tuple(range(3, bits))
    plans = ((0, 2, 1) + later, (0, 1, 2) + later)
    sizes = [bits - 1] + [bits - 1 - stage for stage in range(bits)]
    scratch = [
        pltpu.VMEM((2,) * size + shape, kind)
        for size in sizes
        for shape, kind in zip(shapes, kinds)
    ]
    total = len(chunks)
    scratch += [
        pltpu.SemaphoreType.DMA((total,)),
        pltpu.SemaphoreType.DMA((total, bits)),
        pltpu.SemaphoreType.DMA((total, bits)),
    ]
    return pl.pallas_call(
        partial(reduce_kernel, bits, narrow_bits, plans, tuple(chunks), len(parts)),
        out_shape=[jax.ShapeDtypeStruct(shape, float32) for shape in shapes],
        in_specs=[pl.BlockSpec(memory_space=pl.ANY)] * len(parts),
        out_specs=[pl.BlockSpec(memory_space=pltpu.VMEM)] * len(parts),
        scratch_shapes=scratch,
        compiler_params=pltpu.CompilerParams(
            collective_id=collective_id, has_side_effects=True, vmem_limit_bytes=58 * 2**20
        ),
        cost_estimate=pl.CostEstimate(flops=10**8, bytes_accessed=4 * 10**8, transcendentals=0),
    )(*(part.reshape((2,) * bits + shape) for part, shape in zip(parts, shapes)))


def total_kernel(bits, narrow_bits, own_ref, sum_ref, arrived, send_sem, recv_sem):
    peers = [partner(b, narrow_bits) for b in range(bits)]
    greet(peers)
    sum_ref[...] = own_ref[...]
    for stage in range(bits):
        copy = pltpu.make_async_remote_copy(
            src_ref=sum_ref,
            dst_ref=arrived.at[stage],
            send_sem=send_sem.at[stage],
            recv_sem=recv_sem.at[stage],
            device_id=peers[stage][0],
            device_id_type=MESH,
        )
        copy.start()
        copy.wait()
        sum_ref[...] = sum_ref[...] + arrived[stage]


def total_of(value, collective_id):
    bits, narrow_bits = mesh_bits()
    tile = (8, 128)
    return pl.pallas_call(
        partial(total_kernel, bits, narrow_bits),
        out_shape=jax.ShapeDtypeStruct(tile, float32),
        in_specs=[pl.BlockSpec(memory_space=pltpu.VMEM)],
        out_specs=pl.BlockSpec(memory_space=pltpu.VMEM),
        scratch_shapes=[
            pltpu.VMEM((bits,) + tile, float32),
            pltpu.SemaphoreType.DMA((bits,)),
            pltpu.SemaphoreType.DMA((bits,)),
        ],
        compiler_params=pltpu.CompilerParams(collective_id=collective_id, has_side_effects=True),
    )(jnp.broadcast_to(value, tile))[0, 0]


def weight_grad_kernel(columns, band_rows, left_ref, right_ref, out_ref):
    left = left_ref[...].T
    for at in range(0, len(columns), 2):
        blocks = []
        for group, start in columns[at : at + 2]:
            block = jnp.dot(
                left, right_ref[group, :, start : start + BLOCK], preferred_element_type=float32
            )
            blocks.append(block.astype(bfloat16).reshape(-1, band_rows, BLOCK))
        out_ref[:, at * band_rows : (at + 2) * band_rows, :] = jnp.concatenate(blocks, 1)


def weight_grad(left, right, columns, device_count):
    tok_rows, height = left.shape
    band_rows = BLOCK // device_count
    bands, wide = height // BLOCK, len(columns)
    if band_rows % 8:
        product = jnp.einsum("td,gte->dge", left, right, preferred_element_type=float32)
        product = jnp.concatenate(
            [product[:, group, start : start + BLOCK] for group, start in columns], 1
        )
        product = product.astype(bfloat16).reshape(bands, device_count, band_rows, wide, BLOCK)
        return product.transpose(1, 0, 3, 2, 4).reshape(device_count, -1, BLOCK)
    return pl.pallas_call(
        partial(weight_grad_kernel, columns, band_rows),
        grid=(bands,),
        in_specs=[
            pl.BlockSpec((tok_rows, BLOCK), lambda i: (0, i)),
            pl.BlockSpec(right.shape, lambda i: (0, 0, 0)),
        ],
        out_specs=pl.BlockSpec((device_count, wide * band_rows, BLOCK), lambda i: (0, i, 0)),
        out_shape=jax.ShapeDtypeStruct((device_count, bands * wide * band_rows, BLOCK), bfloat16),
        compiler_params=pltpu.CompilerParams(vmem_limit_bytes=VMEM_LIMIT),
        cost_estimate=pl.CostEstimate(
            flops=2 * tok_rows * bands * wide * BLOCK**2,
            bytes_accessed=2 * (tok_rows * (height + wide * BLOCK) + bands * wide * BLOCK**2),
            transcendentals=0,
        ),
    )(left, right)


def unpack(gathered):
    matrices = [
        layout.reshape(layout.shape[0] * layout.shape[1], layout.shape[2])
        for layout in gathered[:4]
    ]
    return (matrices, gathered[4].astype(jnp.float32))


def body(
    tokens,
    cotangent,
    lengths,
    owners,
    w_qkv,
    w_out,
    w_up,
    w_down,
    norm_gains,
    gain_first,
    gain_second,
    moment_first,
    moment_second,
    left_stat,
    right_stat,
    left_basis,
    right_basis,
):
    tok_rows, width = tokens.shape
    narrow_count = lax.axis_size("narrow")
    device_count = lax.axis_size("wide") * narrow_count
    seq_len = tok_rows * narrow_count
    cap_slots = moment_first.shape[0]
    masters = (w_qkv, w_out, w_up, w_down)
    lowered = tuple((layout.astype(jnp.bfloat16) for layout in masters)) + (
        norm_gains.astype(jnp.bfloat16),
    )
    weight_list, gain_pair = unpack(
        jax.tree.map(
            lambda part, own: part.astype(own.dtype),
            lax.all_gather(shortened(lowered), ("wide", "narrow"), axis=1, tiled=True),
            lowered,
        )
    )
    w_attn, w_proj, w_hidden, w_back = weight_list
    inputs = tokens.astype(jnp.float32)
    normed_one, inverse_one = normalize(inputs)
    act_one = (normed_one * gain_pair[0]).astype(jnp.bfloat16)
    head_width = width // narrow_count
    safe = seq_len - tok_rows
    w_groups = w_attn.reshape(width, 3, narrow_count, head_width)
    packed = jnp.einsum("td,dkge->gtke", act_one, w_groups, preferred_element_type=jnp.float32)
    packed = packed.astype(jnp.bfloat16).reshape(narrow_count, tok_rows, 3 * head_width)
    scene = exchange(packed).reshape(seq_len, 3 * head_width)
    mixed, log_totals = attend(lengths, scene, safe)
    merged = exchange(mixed.reshape(narrow_count, tok_rows, head_width))
    merged = merged.transpose(1, 0, 2).reshape(tok_rows, width)
    middle = inputs + jnp.dot(merged, w_proj, preferred_element_type=jnp.float32)
    normed_two, inverse_two = normalize(middle)
    act_two = (normed_two * gain_pair[1]).astype(jnp.bfloat16)
    hidden = jnp.dot(act_two, w_hidden, preferred_element_type=jnp.float32)
    active = jax.nn.gelu(hidden, approximate=True).astype(jnp.bfloat16)
    block_out = (middle + jnp.dot(active, w_back, preferred_element_type=jnp.float32)).astype(
        jnp.bfloat16
    )
    plain = lambda size: tuple((0, start) for start in range(0, size, BLOCK))
    d_back = weight_grad(active, cotangent[None], plain(width), device_count)
    d_active = jnp.einsum("td,fd->tf", cotangent, w_back, preferred_element_type=jnp.float32)
    _, gelu_pull = jax.vjp(partial(jax.nn.gelu, approximate=True), hidden)
    d_hidden = gelu_pull(d_active)[0].astype(jnp.bfloat16)
    d_w_hidden = weight_grad(act_two, d_hidden[None], plain(FF), device_count)
    d_act_two = jnp.einsum("tf,df->td", d_hidden, w_hidden, preferred_element_type=jnp.float32)
    d_norm_two, d_gain_two = norm_backward(d_act_two, normed_two, inverse_two, gain_pair[1])
    d_middle = cotangent.astype(jnp.float32) + d_norm_two
    d_branch = d_middle.astype(jnp.bfloat16)
    d_proj = weight_grad(merged, d_branch[None], plain(width), device_count)
    d_merged = jnp.einsum("te,de->td", d_branch, w_proj, preferred_element_type=jnp.float32).astype(
        jnp.bfloat16
    )
    d_mixed = d_merged.reshape(tok_rows, narrow_count, head_width).transpose(1, 0, 2)
    d_mixed = exchange(d_mixed).reshape(seq_len, head_width)
    d_scene = jnp.concatenate(attend_backward(lengths, scene, mixed, d_mixed, log_totals, safe), 1)
    d_packed = exchange(d_scene.reshape(narrow_count, tok_rows, 3 * head_width))
    grouped = tuple(
        (group, third * head_width + start)
        for third in range(3)
        for group in range(narrow_count)
        for start in range(0, head_width, BLOCK)
    )
    d_attn = weight_grad(act_one, d_packed, grouped, device_count)
    d_act_one = jnp.einsum(
        "gtke,dkge->td",
        d_packed.reshape(narrow_count, tok_rows, 3, head_width),
        w_groups,
        preferred_element_type=jnp.float32,
    )
    d_norm_one, d_gain_one = norm_backward(d_act_one, normed_one, inverse_one, gain_pair[0])
    grad_tokens = (d_middle + d_norm_one).astype(jnp.bfloat16)
    share = width // device_count
    gain_parts = jnp.stack([d_gain_one, d_gain_two]).reshape(2, device_count, share)
    gain_parts = jnp.pad(gain_parts.transpose(1, 0, 2), ((0, 0), (0, 6), (0, 128 - share)))
    *grad_shards, gain_grad = reduce_to_shards(
        (d_attn, d_proj, d_w_hidden, d_back, gain_parts), (6, 2, 8, 8, 1), 1
    )
    gain_grad = gain_grad[:2, :share]
    band_rows = BLOCK // device_count
    local_squares = jnp.sum(gain_grad * gain_grad) + sum(
        (jnp.sum(shard * shard) for shard in grad_shards)
    )
    pieces = jnp.concatenate(grad_shards, 0).reshape(-1, band_rows, BLOCK)
    block_count = pieces.shape[0]
    order = lax.iota(jnp.int32, block_count)
    earlier = (owners[None, :] == owners[:, None]) & (order[None, :] < order[:, None])
    slots = owners * cap_slots + jnp.sum(earlier.astype(jnp.int32), 1)
    routing = (slots[None, :] == lax.iota(jnp.int32, device_count * cap_slots)[:, None]).astype(
        jnp.float32
    )
    routing = routing.reshape(device_count, cap_slots, block_count)
    grad_norm = jnp.sqrt(total_of(local_squares, 2))
    factor = jnp.minimum(1.0, clip_bound / grad_norm)
    arrived = lax.all_to_all(
        jnp.einsum("okb,bxy->koxy", routing, pieces, precision=highest).astype(jnp.bfloat16),
        ("wide", "narrow"),
        split_axis=1,
        concat_axis=1,
        tiled=True,
    )
    slot_grads = arrived.reshape(cap_slots, BLOCK, BLOCK)
    restored, first_new, second_new, left_new, right_new, gram, turn = soap_update(
        factor, slot_grads, moment_first, moment_second, left_stat, right_stat, left_basis, right_basis
    )
    square = (-1, BLOCK, BLOCK)
    bases = renew_bases(gram.reshape(square), turn.reshape(square))
    bases = bases.reshape(cap_slots, 2, BLOCK, BLOCK)
    left_turn, right_turn = bases[:, 0], bases[:, 1]
    returned = lax.all_to_all(
        shortened(restored.reshape(cap_slots, device_count, -1, BLOCK)),
        ("wide", "narrow"),
        split_axis=1,
        concat_axis=1,
        tiled=True,
    )
    back_pieces = jnp.einsum("okb,koxy->bxy", routing, returned, precision=highest)
    fan_list = (2 * width, max(1, width * 16 // seq_len), width, FF)
    updated = []
    offset = 0
    for master, fan_in in zip(masters, fan_list):
        band_count, band_rows, col_count = master.shape
        piece_count = band_count * (col_count // BLOCK)
        direction = from_pieces(back_pieces[offset : offset + piece_count], band_count, col_count)
        updated.append(master - fan_in ** (-0.5) * (direction + weight_decay * master))
        offset += piece_count
    clipped = gain_grad * factor
    gain_one_new = decay_rate * gain_first + (1.0 - decay_rate) * clipped
    gain_two_new = decay_rate * gain_second + (1.0 - decay_rate) * clipped * clipped
    correct = 1.0 - decay_rate**STEP
    gain_values = norm_gains - gain_rate * (gain_one_new / correct) / (
        jnp.sqrt(gain_two_new / correct) + eps_adam
    )
    return (
        block_out,
        grad_tokens,
        grad_norm,
        updated[0],
        updated[1],
        updated[2],
        updated[3],
        gain_values,
        gain_one_new,
        gain_two_new,
        first_new,
        second_new,
        left_new,
        right_new,
        left_turn,
        right_turn,
    )


def solution(mesh):
    in_specs = (
        P(("wide", "narrow"), None),
        P(("wide", "narrow"), None),
        P("wide"),
        P(),
        P(None, ("wide", "narrow"), None),
        P(None, ("wide", "narrow"), None),
        P(None, ("wide", "narrow"), None),
        P(None, ("wide", "narrow"), None),
        P(None, ("wide", "narrow")),
        P(None, ("wide", "narrow")),
        P(None, ("wide", "narrow")),
        P(("wide", "narrow"), None, None),
        P(("wide", "narrow"), None, None),
        P(("wide", "narrow"), None, None),
        P(("wide", "narrow"), None, None),
        P(("wide", "narrow"), None, None),
        P(("wide", "narrow"), None, None),
    )
    out_specs = (
        P(("wide", "narrow"), None),
        P(("wide", "narrow"), None),
        P(),
        P(None, ("wide", "narrow"), None),
        P(None, ("wide", "narrow"), None),
        P(None, ("wide", "narrow"), None),
        P(None, ("wide", "narrow"), None),
        P(None, ("wide", "narrow")),
        P(None, ("wide", "narrow")),
        P(None, ("wide", "narrow")),
        P(("wide", "narrow"), None, None),
        P(("wide", "narrow"), None, None),
        P(("wide", "narrow"), None, None),
        P(("wide", "narrow"), None, None),
        P(("wide", "narrow"), None, None),
        P(("wide", "narrow"), None, None),
    )
    return jax.shard_map(body, mesh=mesh, in_specs=in_specs, out_specs=out_specs, check_vma=False)
```

```python
from functools import partial

import jax
import jax.numpy as jnp
from jax import lax
from jax.experimental import pallas as pl
from jax.experimental.pallas import tpu as pltpu
from jax.sharding import PartitionSpec as P

FF = 4096
HEADS = 16
HEAD = 64
BLOCK = 256
STEP = 10


eps_norm = 1e-05
eps_adam = 1e-08
decay_rate = 0.5
clip_bound = 1.0
weight_decay = 0.01
gain_rate = 1.0
neg_large = -1e30
highest = lax.Precision.HIGHEST
float32 = jnp.float32
bfloat16 = jnp.bfloat16
PAIR = 2 * HEAD
NT = (((1,), (1,)), ((), ()))
TN = (((0,), (0,)), ((), ()))
MESH = pl.DeviceIdType.MESH
VMEM_LIMIT = 48 * 2**20
AHEAD = 4
SKEW = 3


def shortened(shard):
    return jax.tree.map(lambda a: a.astype(jnp.bfloat16) if a.dtype == jnp.float32 else a, shard)


def normalize(values):
    center = values - jnp.mean(values, -1, keepdims=True)
    inverse = lax.rsqrt(jnp.mean(center * center, -1, keepdims=True) + eps_norm)
    return (center * inverse, inverse)


def norm_backward(d_result, normed, inverse, gain):
    scaled = d_result * gain
    d_gain = jnp.sum(d_result * normed, 0)
    d_input = inverse * (
        scaled
        - jnp.mean(scaled, -1, keepdims=True)
        - normed * jnp.mean(scaled * normed, -1, keepdims=True)
    )
    return (d_input, d_gain)


def from_pieces(pieces, band_count, col_count):
    band_rows = pieces.shape[1]
    return (
        pieces.reshape(band_count, col_count // BLOCK, band_rows, BLOCK)
        .transpose(0, 2, 1, 3)
        .reshape(band_count, band_rows, col_count)
    )


def one_head(matrix, head):
    lane = lax.broadcasted_iota(jnp.int32, matrix.shape, 1)
    return jnp.where(lane // HEAD == head, matrix, jnp.zeros_like(matrix))


def hide(scores, start, safe, length):
    if start + scores.shape[0] <= safe:
        return scores
    position = start + lax.broadcasted_iota(jnp.int32, scores.shape, 0)
    return jnp.where(position < length, scores, neg_large)


def attend_kernel(safe, chunk, length_ref, q_ref, k_ref, v_ref, o_ref, log_ref, vt_ref, s_ref):
    seq_len = k_ref.shape[0]
    length = length_ref[0]

    @pl.when(pl.program_id(1) == 0)
    def _():
        vt_ref[...] = v_ref[...].T

    outs = []
    for head in range(2):
        queries = one_head(q_ref[...], head) * bfloat16(HEAD**-0.5)
        topmost = None
        for at in range(0, seq_len, chunk):
            scores = lax.dot_general(
                k_ref[at : at + chunk, :], queries, NT, preferred_element_type=float32
            )
            scores = hide(scores, at, safe, length)
            s_ref[head, at : at + chunk, :] = scores
            top = jnp.max(scores, 0, keepdims=True)
            topmost = top if topmost is None else jnp.maximum(topmost, top)
        totals = jnp.zeros_like(topmost)
        mixed = jnp.zeros((HEAD, q_ref.shape[0]), float32)
        for at in range(0, seq_len, chunk):
            expo = jnp.exp(s_ref[head, at : at + chunk, :] - topmost)
            totals += jnp.sum(expo, 0, keepdims=True)
            mixed += jnp.dot(
                vt_ref[head * HEAD : (head + 1) * HEAD, at : at + chunk],
                expo.astype(bfloat16),
                preferred_element_type=float32,
            )
        outs.append(mixed * (1.0 / totals))
        log_ref[0, head : head + 1, :] = topmost + jnp.log(totals)
    o_ref[...] = jnp.concatenate(outs, 0).T.astype(bfloat16)


def attend(lengths, scene, safe, rows=1024, chunk=512):
    seq_len, width = scene.shape[0], scene.shape[1] // 3
    pairs = width // PAIR
    return pl.pallas_call(
        partial(attend_kernel, safe, chunk),
        grid=(pairs, seq_len // rows),
        in_specs=[
            pl.BlockSpec(memory_space=pltpu.SMEM),
            pl.BlockSpec((rows, PAIR), lambda p, i: (i, p)),
            pl.BlockSpec((seq_len, PAIR), lambda p, i: (0, pairs + p)),
            pl.BlockSpec((seq_len, PAIR), lambda p, i: (0, 2 * pairs + p)),
        ],
        out_specs=[
            pl.BlockSpec((rows, PAIR), lambda p, i: (i, p)),
            pl.BlockSpec((1, 2, rows), lambda p, i: (p, 0, i)),
        ],
        out_shape=[
            jax.ShapeDtypeStruct((seq_len, width), bfloat16),
            jax.ShapeDtypeStruct((pairs, 2, seq_len), float32),
        ],
        scratch_shapes=[
            pltpu.VMEM((PAIR, seq_len), bfloat16),
            pltpu.VMEM((2, seq_len, rows), float32),
        ],
        compiler_params=pltpu.CompilerParams(vmem_limit_bytes=VMEM_LIMIT),
        cost_estimate=pl.CostEstimate(
            flops=4 * pairs * 2 * 4 * seq_len * seq_len * HEAD,
            bytes_accessed=8 * seq_len * width,
            transcendentals=0,
        ),
    )(lengths, scene, scene, scene)


def attend_backward_kernel(
    safe, chunk, length_ref, q_ref, k_ref, v_ref, o_ref, do_ref, log_ref, out_ref, kt_ref, dk_sum, dv_sum
):
    seq_len = k_ref.shape[0]
    length = length_ref[0]

    @pl.when(pl.program_id(1) == 0)
    def _():
        kt_ref[...] = k_ref[...].T
        dk_sum[...] = jnp.zeros_like(dk_sum)
        dv_sum[...] = jnp.zeros_like(dv_sum)

    products = (o_ref[...].astype(float32) * do_ref[...].astype(float32)).T
    turned = []
    for head in range(2):
        lanes = slice(head * HEAD, (head + 1) * HEAD)
        queries = one_head(q_ref[...], head) * bfloat16(HEAD**-0.5)
        d_mixed = one_head(do_ref[...], head)
        inner = jnp.sum(products[lanes, :], 0, keepdims=True)
        log_total = log_ref[0, head : head + 1, :]
        d_queries = jnp.zeros((HEAD, q_ref.shape[0]), float32)
        for at in range(0, seq_len, chunk):
            part = slice(at, at + chunk)
            scores = lax.dot_general(k_ref[part, :], queries, NT, preferred_element_type=float32)
            probs = jnp.exp(hide(scores, at, safe, length) - log_total)
            d_probs = lax.dot_general(v_ref[part, :], d_mixed, NT, preferred_element_type=float32)
            dv_sum[part, :] += jnp.dot(
                probs.astype(bfloat16), d_mixed, preferred_element_type=float32
            )
            d_scores = (probs * (d_probs - inner)).astype(bfloat16)
            dk_sum[part, :] += jnp.dot(d_scores, queries, preferred_element_type=float32)
            d_queries += jnp.dot(kt_ref[lanes, part], d_scores, preferred_element_type=float32)
        turned.append(d_queries * HEAD**-0.5)
    rows = q_ref.shape[0]
    here = pl.ds(pl.multiple_of(pl.program_id(1) * rows, rows), rows)
    out_ref[here, :PAIR] = jnp.concatenate(turned, 0).T.astype(bfloat16)

    @pl.when(pl.program_id(1) == pl.num_programs(1) - 1)
    def _():
        out_ref[:, PAIR : 2 * PAIR] = dk_sum[...].astype(bfloat16)
        out_ref[:, 2 * PAIR :] = dv_sum[...].astype(bfloat16)


def attend_backward(lengths, scene, mixed, d_mixed, log_totals, safe, rows=512, chunk=1024):
    seq_len, width = mixed.shape
    pairs = width // PAIR
    tile = pl.BlockSpec((rows, PAIR), lambda p, i: (i, p))
    return pl.pallas_call(
        partial(attend_backward_kernel, safe, chunk),
        grid=(pairs, seq_len // rows),
        in_specs=[
            pl.BlockSpec(memory_space=pltpu.SMEM),
            tile,
            pl.BlockSpec((seq_len, PAIR), lambda p, i: (0, pairs + p)),
            pl.BlockSpec((seq_len, PAIR), lambda p, i: (0, 2 * pairs + p)),
            tile,
            tile,
            pl.BlockSpec((1, 2, rows), lambda p, i: (p, 0, i)),
        ],
        out_specs=pl.BlockSpec((seq_len, 3 * PAIR), lambda p, i: (0, p)),
        out_shape=jax.ShapeDtypeStruct((seq_len, 3 * width), bfloat16),
        scratch_shapes=[
            pltpu.VMEM((PAIR, seq_len), bfloat16),
            pltpu.VMEM((seq_len, PAIR), float32),
            pltpu.VMEM((seq_len, PAIR), float32),
        ],
        compiler_params=pltpu.CompilerParams(vmem_limit_bytes=VMEM_LIMIT),
        cost_estimate=pl.CostEstimate(
            flops=4 * pairs * 2 * 10 * seq_len * seq_len * HEAD,
            bytes_accessed=16 * seq_len * width,
            transcendentals=0,
        ),
    )(lengths, scene, scene, scene, mixed, d_mixed, log_totals)


def project_kernel(acts_ref, wq_ref, wk_ref, wv_ref, *out_refs):
    thirds = (wq_ref, wk_ref, wv_ref)
    halves = len(out_refs)
    weights = jnp.concatenate(
        [third[:, h * PAIR : (h + 1) * PAIR] for h in range(halves) for third in thirds], 1
    )
    result = jnp.dot(acts_ref[...], weights, preferred_element_type=float32).astype(bfloat16)
    for h, out_ref in enumerate(out_refs):
        out_ref[0] = result[:, h * 3 * PAIR : (h + 1) * 3 * PAIR]


def project(acts, weights, groups):
    tok_rows, width = acts.shape
    head_width = width // groups
    halves = head_width // PAIR

    def third(k):
        return pl.BlockSpec((width, head_width), lambda g: (0, k * groups + g))

    return pl.pallas_call(
        project_kernel,
        grid=(groups,),
        in_specs=[pl.BlockSpec((tok_rows, width), lambda g: (0, 0)), third(0), third(1), third(2)],
        out_specs=[pl.BlockSpec((1, tok_rows, 3 * PAIR), lambda g: (g, 0, 0))] * halves,
        out_shape=[jax.ShapeDtypeStruct((groups, tok_rows, 3 * PAIR), bfloat16)] * halves,
        compiler_params=pltpu.CompilerParams(vmem_limit_bytes=VMEM_LIMIT),
        cost_estimate=pl.CostEstimate(
            flops=6 * tok_rows * width**2, bytes_accessed=6 * width**2 + 8 * tok_rows * width,
            transcendentals=0,
        ),
    )(acts, weights, weights, weights)


def project_back_kernel(halves, *refs):
    grads, (wq_ref, wk_ref, wv_ref, out_ref) = refs[:halves], refs[halves:]
    thirds = (wq_ref, wk_ref, wv_ref)
    weights = jnp.concatenate(
        [third[:, h * PAIR : (h + 1) * PAIR] for h in range(halves) for third in thirds], 1
    )
    rows = jnp.concatenate([grad[0] for grad in grads], 1)
    result = lax.dot_general(rows, weights, NT, preferred_element_type=float32)

    @pl.when(pl.program_id(0) == 0)
    def _():
        out_ref[...] = result

    @pl.when(pl.program_id(0) > 0)
    def _():
        out_ref[...] += result


def project_back(grads, weights):
    groups, tok_rows, _ = grads[0].shape
    width = weights.shape[0]
    head_width = width // groups

    def third(k):
        return pl.BlockSpec((width, head_width), lambda g: (0, k * groups + g))

    return pl.pallas_call(
        partial(project_back_kernel, len(grads)),
        grid=(groups,),
        in_specs=[pl.BlockSpec((1, tok_rows, 3 * PAIR), lambda g: (g, 0, 0))] * len(grads)
        + [third(0), third(1), third(2)],
        out_specs=pl.BlockSpec((tok_rows, width), lambda g: (0, 0)),
        out_shape=jax.ShapeDtypeStruct((tok_rows, width), float32),
        compiler_params=pltpu.CompilerParams(vmem_limit_bytes=VMEM_LIMIT),
        cost_estimate=pl.CostEstimate(
            flops=6 * tok_rows * width**2, bytes_accessed=6 * width**2 + 10 * tok_rows * width,
            transcendentals=0,
        ),
    )(*grads, weights, weights, weights)


def exact(left, right, dims=(((1,), (0,)), ((), ()))):
    return lax.dot_general(left, right, dims, precision=highest, preferred_element_type=float32)


def soap_kernel(
    factor_ref, g_ref, first_ref, second_ref, ls_ref, rs_ref, lb_ref, rb_ref,
    back_ref, first_out, second_out, ls_out, rs_out, gram_ref, turn_ref,
):
    gradient = factor_ref[0, 0] * g_ref[0].astype(float32)
    left_base, right_base = lb_ref[0], rb_ref[0]
    left_new = decay_rate * ls_ref[0] + (1.0 - decay_rate) * exact(gradient, gradient, NT)
    right_new = decay_rate * rs_ref[0] + (1.0 - decay_rate) * exact(gradient, gradient, TN)
    ls_out[0] = left_new
    rs_out[0] = right_new
    turned = exact(left_base, exact(gradient, right_base), TN)
    first_new = decay_rate * first_ref[0] + (1.0 - decay_rate) * turned
    second_new = decay_rate * second_ref[0] + (1.0 - decay_rate) * turned * turned
    first_out[0] = first_new
    second_out[0] = second_new
    correct = 1.0 - decay_rate**STEP
    direction = first_new / correct / (jnp.sqrt(second_new / correct) + eps_adam)
    back_ref[0] = exact(left_base, exact(direction, right_base, NT)).astype(back_ref.dtype)
    for side, stat, base in ((0, left_new, left_base), (1, right_new, right_base)):
        turn = exact(stat, base).T
        turn_ref[0, side] = turn
        gram_ref[0, side] = exact(turn, turn, NT)


def soap_update(factor, gradient, first_old, second_old, left_old, right_old, left_base, right_base):
    slots, order, _ = gradient.shape
    one = pl.BlockSpec((1, order, order), lambda s: (s, 0, 0))
    two = pl.BlockSpec((1, 2, order, order), lambda s: (s, 0, 0, 0))
    single = jax.ShapeDtypeStruct((slots, order, order), float32)
    double = jax.ShapeDtypeStruct((slots, 2, order, order), float32)
    return pl.pallas_call(
        soap_kernel,
        grid=(slots,),
        in_specs=[pl.BlockSpec(memory_space=pltpu.SMEM)] + [one] * 7,
        out_specs=[one] * 5 + [two] * 2,
        out_shape=[jax.ShapeDtypeStruct((slots, order, order), bfloat16)] + [single] * 4 + [double] * 2,
        compiler_params=pltpu.CompilerParams(vmem_limit_bytes=VMEM_LIMIT),
        cost_estimate=pl.CostEstimate(
            flops=slots * 120 * order**3, bytes_accessed=slots * 60 * order**2, transcendentals=0
        ),
    )(factor.reshape(1, 1), gradient, first_old, second_old, left_old, right_old, left_base, right_base)


def renew_kernel(rows, gram_ref, turn_ref, q_ref, x_ref, u_ref):
    count, order = gram_ref.shape[0], gram_ref.shape[1]
    eye = (
        lax.broadcasted_iota(jnp.int32, (rows, rows), 0)
        == lax.broadcasted_iota(jnp.int32, (rows, rows), 1)
    ).astype(float32)
    sublane = lax.broadcasted_iota(jnp.int32, (1, 8, 1), 1)
    for low in range(0, order, rows):
        part = slice(low, low + rows)

        def panel(at, carry, low=low, part=part):
            row = jnp.concatenate([gram_ref[at, part, :], turn_ref[at, part, :]], 1)
            if low:
                row = row - exact(u_ref[at, :low, part], u_ref[at, :low, :], TN)
            u_ref[at, part, :] = row
            x_ref[at] = jnp.concatenate([row[:, part], eye], 1)
            return carry

        lax.fori_loop(0, count, panel, 0, unroll=2)
        for j in range(rows):
            tile = j // 8 * 8
            row = x_ref[:, j : j + 1, :]
            row = row * (1.0 / row[:, :, j : j + 1])
            top = x_ref[:, tile : tile + 8, :]
            below = jnp.where(sublane > j - tile, top[:, :, j : j + 1], 0.0)
            x_ref[:, tile : tile + 8, :] = top - below * row
            if tile + 8 < rows:
                rest = x_ref[:, tile + 8 :, :]
                x_ref[:, tile + 8 :, :] = rest - rest[:, :, j : j + 1] * row

        def solve(at, carry, part=part):
            both = x_ref[at]
            diagonal = jnp.sum(both[:, :rows] * eye, 1, keepdims=True)
            u_ref[at, part, :] = exact(both[:, rows:] * lax.rsqrt(diagonal), u_ref[at, part, :])
            return carry

        lax.fori_loop(0, count, solve, 0, unroll=2)

    def turn_back(at, carry):
        q_ref[at] = u_ref[at, :, order:].T
        return carry

    lax.fori_loop(0, count, turn_back, 0)


def renew_bases(gram, turn, rows=64):
    count, order, _ = gram.shape
    return pl.pallas_call(
        partial(renew_kernel, rows),
        out_shape=jax.ShapeDtypeStruct(gram.shape, float32),
        in_specs=[pl.BlockSpec(memory_space=pltpu.VMEM)] * 2,
        out_specs=pl.BlockSpec(memory_space=pltpu.VMEM),
        scratch_shapes=[
            pltpu.VMEM((count, rows, 2 * rows), float32),
            pltpu.VMEM((count, order, 2 * order), float32),
        ],
        compiler_params=pltpu.CompilerParams(vmem_limit_bytes=VMEM_LIMIT),
        cost_estimate=pl.CostEstimate(
            flops=count * 200 * order**3, bytes_accessed=count * 12 * order**2, transcendentals=0
        ),
    )(gram, turn)


def exchange(groups):
    return lax.all_to_all(groups, "narrow", split_axis=0, concat_axis=0, tiled=True)


def partner(bit, narrow_bits):
    axis, step = ("narrow", 1 << bit) if bit < narrow_bits else ("wide", 1 << (bit - narrow_bits))
    place = lax.axis_index(axis)
    mine = lax.rem(place // step, 2)
    return {axis: place + step - 2 * step * mine}, mine


def greet(peers):
    barrier = pltpu.get_barrier_semaphore()
    for device, _ in peers:
        pl.semaphore_signal(barrier, inc=1, device_id=device, device_id_type=MESH)
    pl.semaphore_wait(barrier, len(peers))


def mesh_bits():
    narrow_bits = lax.axis_size("narrow").bit_length() - 1
    return narrow_bits + lax.axis_size("wide").bit_length() - 1, narrow_bits


def reduce_kernel(bits, narrow_bits, plans, chunks, count, *refs):
    sources, outs, scratch = refs[:count], refs[count : 2 * count], refs[2 * count :]
    held = scratch[:count]
    arrived = [scratch[count * (1 + s) : count * (2 + s)] for s in range(bits)]
    load_sem, send_sem, recv_sem = scratch[count * (1 + bits) :]
    peers = [partner(b, narrow_bits) for b in range(bits)]
    greet(peers)
    first = plans[0][0]
    order_of_dims = list(reversed(range(bits)))
    whole = slice(None)

    def within(order, stage, current):
        return tuple(
            peers[b][1] if b in order[:stage] else current if b == order[stage] else whole
            for b in order_of_dims
            if b != first
        )

    def of_source(value):
        return tuple(value if b == first else whole for b in order_of_dims)

    def rows_of(chunk):
        at, row, rows, colour = chunks[chunk]
        return at, plans[colour], (pl.ds(row, rows), whole)

    def send(chunk, stage):
        at, order, part = rows_of(chunk)
        device, mine = peers[order[stage]]
        if stage == 0:
            source = sources[at].at[of_source(1 - mine) + part]
        else:
            source = held[at].at[within(order, stage, 1 - mine) + part]
        return pltpu.make_async_remote_copy(
            src_ref=source,
            dst_ref=arrived[stage][at].at[(whole,) * (bits - 1 - stage) + part],
            send_sem=send_sem.at[chunk, stage],
            recv_sem=recv_sem.at[chunk, stage],
            device_id=device,
            device_id_type=MESH,
        )

    def load(chunk):
        at, order, part = rows_of(chunk)
        return pltpu.make_async_copy(
            sources[at].at[of_source(peers[first][1]) + part],
            held[at].at[(whole,) * (bits - 1) + part],
            load_sem.at[chunk],
        )

    def begin(chunk):
        send(chunk, 0).start()
        load(chunk).start()

    def finish(chunk, stage):
        at, order, part = rows_of(chunk)
        if stage == 0:
            load(chunk).wait()
        send(chunk, stage).wait_recv()
        left = bits - 1 - stage
        keep = within(order, stage, peers[order[stage]][1])
        if left == 0:
            own = held[at][keep + part].astype(float32)
            outs[at][part] = own + arrived[stage][at][part].astype(float32)
            return
        free = [i for i, k in enumerate(keep) if isinstance(k, slice)]

        def add(m, carry):
            which = tuple(m // (1 << (left - 1 - i)) % 2 for i in range(left))
            spot = list(keep)
            for i, f in enumerate(free):
                spot[f] = which[i]
            spot = tuple(spot) + part
            held[at][spot] = held[at][spot] + arrived[stage][at][which + part]
            return carry

        lax.fori_loop(0, 1 << left, add, 0)
        send(chunk, stage + 1).start()

    total = len(chunks)
    for chunk in range(min(AHEAD, total)):
        begin(chunk)
    for step in range(total + 2 * bits):
        for stage in reversed(range(bits)):
            chunk = step - 2 * stage
            if 0 <= chunk < total:
                finish(chunk, stage)
                if stage == 0 and chunk + AHEAD < total:
                    begin(chunk + AHEAD)
    for chunk in range(total):
        for stage in range(bits):
            send(chunk, stage).wait_send()


def reduce_to_shards(parts, pieces, collective_id):
    bits, narrow_bits = mesh_bits()
    shapes = [part.shape[1:] for part in parts]
    kinds = [part.dtype for part in parts]
    chunks = []
    for at, (shape, cut) in enumerate(zip(shapes, pieces)):
        rows = shape[0] // cut
        chunks += [(at, row, rows, len(chunks) % 2) for row in range(0, shape[0], rows)]
        chunks = [(a, r, n, i % 2) for i, (a, r, n, _) in enumerate(chunks)]
    later = tuple(range(3, bits))
    plans = ((0, 2, 1) + later, (0, 1, 2) + later)
    sizes = [bits - 1] + [bits - 1 - stage for stage in range(bits)]
    scratch = [
        pltpu.VMEM((2,) * size + shape, kind)
        for size in sizes
        for shape, kind in zip(shapes, kinds)
    ]
    total = len(chunks)
    scratch += [
        pltpu.SemaphoreType.DMA((total,)),
        pltpu.SemaphoreType.DMA((total, bits)),
        pltpu.SemaphoreType.DMA((total, bits)),
    ]
    return pl.pallas_call(
        partial(reduce_kernel, bits, narrow_bits, plans, tuple(chunks), len(parts)),
        out_shape=[jax.ShapeDtypeStruct(shape, float32) for shape in shapes],
        in_specs=[pl.BlockSpec(memory_space=pl.ANY)] * len(parts),
        out_specs=[pl.BlockSpec(memory_space=pltpu.VMEM)] * len(parts),
        scratch_shapes=scratch,
        compiler_params=pltpu.CompilerParams(
            collective_id=collective_id, has_side_effects=True, vmem_limit_bytes=58 * 2**20
        ),
        cost_estimate=pl.CostEstimate(flops=10**8, bytes_accessed=4 * 10**8, transcendentals=0),
    )(*(part.reshape((2,) * bits + shape) for part, shape in zip(parts, shapes)))


def gather_kernel(bits, narrow_bits, plans, chunks, count, *refs):
    sources, outs = refs[:count], refs[count : 2 * count]
    own_sem, send_sem, recv_sem = refs[2 * count :]
    peers = [partner(b, narrow_bits) for b in range(bits)]
    greet(peers)
    dims = list(reversed(range(bits)))

    def place(chunk, stage):
        at, band, bands, col, cols, colour = chunks[chunk]
        done = plans[colour][:stage]
        index = tuple(slice(None) if b in done else peers[b][1] for b in dims)
        return outs[at].at[(pl.ds(band, bands),) + index + (slice(None), pl.ds(col, cols))]

    def own(chunk):
        at, band, bands, col, cols, colour = chunks[chunk]
        return sources[at].at[pl.ds(band, bands), :, pl.ds(col, cols)]

    def send(chunk, stage):
        colour = chunks[chunk][-1]
        target = place(chunk, stage)
        return pltpu.make_async_remote_copy(
            src_ref=target if stage else own(chunk),
            dst_ref=target,
            send_sem=send_sem.at[chunk, stage],
            recv_sem=recv_sem.at[chunk, stage],
            device_id=peers[plans[colour][stage]][0],
            device_id_type=MESH,
        )

    def keep(chunk):
        return pltpu.make_async_copy(own(chunk), place(chunk, 0), own_sem.at[chunk])

    total = len(chunks)
    for chunk in range(total):
        send(chunk, 0).start()
        keep(chunk).start()
    for step in range(total + SKEW * bits):
        for stage in reversed(range(bits)):
            chunk = step - SKEW * stage
            if 0 <= chunk < total:
                if stage == 0:
                    keep(chunk).wait()
                send(chunk, stage).wait_recv()
                if stage + 1 < bits:
                    send(chunk, stage + 1).start()
    for chunk in range(total):
        for stage in range(bits):
            send(chunk, stage).wait_send()


def gather_bands(parts, pieces, collective_id):
    bits, narrow_bits = mesh_bits()
    chunks = []
    for at, (part, (cut, cut_cols)) in enumerate(zip(parts, pieces)):
        bands, cols = part.shape[0] // cut, part.shape[2] // cut_cols
        for band in range(0, part.shape[0], bands):
            for col in range(0, part.shape[2], cols):
                chunks.append((at, band, bands, col, cols, len(chunks) % 2))
    later = tuple(reversed(range(3, bits)))
    plans = (later + (1, 2, 0), later + (2, 1, 0))
    total = len(chunks)
    results = pl.pallas_call(
        partial(gather_kernel, bits, narrow_bits, plans, tuple(chunks), len(parts)),
        out_shape=[
            jax.ShapeDtypeStruct(part.shape[:1] + (2,) * bits + part.shape[1:], part.dtype)
            for part in parts
        ],
        in_specs=[pl.BlockSpec(memory_space=pl.ANY)] * len(parts),
        out_specs=[pl.BlockSpec(memory_space=pl.ANY)] * len(parts),
        scratch_shapes=[
            pltpu.SemaphoreType.DMA((total,)),
            pltpu.SemaphoreType.DMA((total, bits)),
            pltpu.SemaphoreType.DMA((total, bits)),
        ],
        compiler_params=pltpu.CompilerParams(collective_id=collective_id, has_side_effects=True),
        cost_estimate=pl.CostEstimate(flops=0, bytes_accessed=10**8, transcendentals=0),
    )(*parts)
    return [
        result.reshape(part.shape[:1] + (1 << bits,) + part.shape[1:])
        for result, part in zip(results, parts)
    ]


def total_kernel(bits, narrow_bits, own_ref, sum_ref, arrived, send_sem, recv_sem):
    peers = [partner(b, narrow_bits) for b in range(bits)]
    greet(peers)
    sum_ref[...] = own_ref[...]
    for stage in range(bits):
        copy = pltpu.make_async_remote_copy(
            src_ref=sum_ref,
            dst_ref=arrived.at[stage],
            send_sem=send_sem.at[stage],
            recv_sem=recv_sem.at[stage],
            device_id=peers[stage][0],
            device_id_type=MESH,
        )
        copy.start()
        copy.wait()
        sum_ref[...] = sum_ref[...] + arrived[stage]


def total_of(value, collective_id):
    bits, narrow_bits = mesh_bits()
    tile = (8, 128)
    return pl.pallas_call(
        partial(total_kernel, bits, narrow_bits),
        out_shape=jax.ShapeDtypeStruct(tile, float32),
        in_specs=[pl.BlockSpec(memory_space=pltpu.VMEM)],
        out_specs=pl.BlockSpec(memory_space=pltpu.VMEM),
        scratch_shapes=[
            pltpu.VMEM((bits,) + tile, float32),
            pltpu.SemaphoreType.DMA((bits,)),
            pltpu.SemaphoreType.DMA((bits,)),
        ],
        compiler_params=pltpu.CompilerParams(collective_id=collective_id, has_side_effects=True),
    )(jnp.broadcast_to(value, tile))[0, 0]


def weight_grad_kernel(columns, band_rows, left_ref, *refs):
    right_refs, out_ref = refs[:-1], refs[-1]
    left = left_ref[...].T
    for at in range(0, len(columns), 2):
        blocks = []
        for spots in columns[at : at + 2]:
            right = [right_refs[i][g, :, start : start + size] for i, g, start, size in spots]
            right = right[0] if len(right) == 1 else jnp.concatenate(right, 1)
            block = jnp.dot(left, right, preferred_element_type=float32)
            blocks.append(block.astype(bfloat16).reshape(-1, band_rows, BLOCK))
        out_ref[:, at * band_rows : (at + 2) * band_rows, :] = jnp.concatenate(blocks, 1)


def weight_grad(left, rights, columns, device_count):
    tok_rows, height = left.shape
    band_rows = BLOCK // device_count
    bands, wide = height // BLOCK, len(columns)
    if band_rows % 8:
        right = [rights[i][g, :, start : start + n] for spots in columns for i, g, start, n in spots]
        right = jnp.concatenate(right, 1)
        product = jnp.einsum("td,te->de", left, right, preferred_element_type=float32)
        product = product.astype(bfloat16).reshape(bands, device_count, band_rows, wide, BLOCK)
        return product.transpose(1, 0, 3, 2, 4).reshape(device_count, -1, BLOCK)
    return pl.pallas_call(
        partial(weight_grad_kernel, columns, band_rows),
        grid=(bands,),
        in_specs=[
            pl.BlockSpec((tok_rows, BLOCK), lambda i: (0, i)),
        ]
        + [pl.BlockSpec(right.shape, lambda i: (0, 0, 0)) for right in rights],
        out_specs=pl.BlockSpec((device_count, wide * band_rows, BLOCK), lambda i: (0, i, 0)),
        out_shape=jax.ShapeDtypeStruct((device_count, bands * wide * band_rows, BLOCK), bfloat16),
        compiler_params=pltpu.CompilerParams(vmem_limit_bytes=VMEM_LIMIT),
        cost_estimate=pl.CostEstimate(
            flops=2 * tok_rows * bands * wide * BLOCK**2,
            bytes_accessed=2 * (tok_rows * (height + wide * BLOCK) + bands * wide * BLOCK**2),
            transcendentals=0,
        ),
    )(left, *rights)


def body(
    tokens,
    cotangent,
    lengths,
    owners,
    w_qkv,
    w_out,
    w_up,
    w_down,
    norm_gains,
    gain_first,
    gain_second,
    moment_first,
    moment_second,
    left_stat,
    right_stat,
    left_basis,
    right_basis,
):
    tok_rows, width = tokens.shape
    narrow_count = lax.axis_size("narrow")
    device_count = lax.axis_size("wide") * narrow_count
    seq_len = tok_rows * narrow_count
    cap_slots = moment_first.shape[0]
    masters = (w_qkv, w_out, w_up, w_down)
    lowered = tuple((layout.astype(jnp.bfloat16) for layout in masters)) + (
        norm_gains.astype(jnp.bfloat16),
    )
    share = norm_gains.shape[1]
    gains_low = jnp.pad(lowered[4], ((0, 6), (0, 128 - share)))[None]
    w_attn, gain_pair = gather_bands((lowered[0], gains_low), ((4, 2), (1, 1)), 3)
    w_attn = w_attn.reshape(width, 3 * width)
    gain_pair = gain_pair[0, :, :2, :share].transpose(1, 0, 2).reshape(2, width)
    gain_pair = gain_pair.astype(jnp.float32)
    w_proj, w_hidden, w_back = (
        gathered.reshape(-1, gathered.shape[2])
        for gathered in lax.all_gather(lowered[1:4], ("wide", "narrow"), axis=1, tiled=True)
    )
    inputs = tokens.astype(jnp.float32)
    normed_one, inverse_one = normalize(inputs)
    act_one = (normed_one * gain_pair[0]).astype(jnp.bfloat16)
    head_width = width // narrow_count
    safe = seq_len - tok_rows
    halves = head_width // PAIR
    scenes = [
        exchange(part).reshape(seq_len, 3 * PAIR)
        for part in project(act_one, w_attn, narrow_count)
    ]
    attended = [attend(lengths, scene, safe) for scene in scenes]
    merged = [exchange(o.reshape(narrow_count, tok_rows, PAIR)) for o, _ in attended]
    merged = jnp.concatenate(
        [merged[half][group] for group in range(narrow_count) for half in range(halves)], 1
    )
    middle = inputs + jnp.dot(merged, w_proj, preferred_element_type=jnp.float32)
    normed_two, inverse_two = normalize(middle)
    act_two = (normed_two * gain_pair[1]).astype(jnp.bfloat16)
    hidden = jnp.dot(act_two, w_hidden, preferred_element_type=jnp.float32)
    active = jax.nn.gelu(hidden, approximate=True).astype(jnp.bfloat16)
    block_out = (middle + jnp.dot(active, w_back, preferred_element_type=jnp.float32)).astype(
        jnp.bfloat16
    )
    plain = lambda size: tuple(((0, 0, start, BLOCK),) for start in range(0, size, BLOCK))
    d_back = weight_grad(active, [cotangent[None]], plain(width), device_count)
    d_active = jnp.einsum("td,fd->tf", cotangent, w_back, preferred_element_type=jnp.float32)
    _, gelu_pull = jax.vjp(partial(jax.nn.gelu, approximate=True), hidden)
    d_hidden = gelu_pull(d_active)[0].astype(jnp.bfloat16)
    d_w_hidden = weight_grad(act_two, [d_hidden[None]], plain(FF), device_count)
    d_act_two = jnp.einsum("tf,df->td", d_hidden, w_hidden, preferred_element_type=jnp.float32)
    d_norm_two, d_gain_two = norm_backward(d_act_two, normed_two, inverse_two, gain_pair[1])
    d_middle = cotangent.astype(jnp.float32) + d_norm_two
    d_branch = d_middle.astype(jnp.bfloat16)
    d_proj = weight_grad(merged, [d_branch[None]], plain(width), device_count)
    d_merged = jnp.einsum("te,de->td", d_branch, w_proj, preferred_element_type=jnp.float32).astype(
        jnp.bfloat16
    )
    d_mixed = d_merged.reshape(tok_rows, narrow_count, halves, PAIR).transpose(2, 1, 0, 3)
    d_mixed = [exchange(d_mixed[half]).reshape(seq_len, PAIR) for half in range(halves)]
    d_scenes = [
        attend_backward(lengths, scene, mixed, d_mixed_one, log_total, safe)
        for scene, (mixed, log_total), d_mixed_one in zip(scenes, attended, d_mixed)
    ]
    d_packed = [exchange(d.reshape(narrow_count, tok_rows, 3 * PAIR)) for d in d_scenes]
    grouped = tuple(
        tuple((half, group, third * PAIR, PAIR) for half in range(halves))
        for third in range(3)
        for group in range(narrow_count)
    )
    d_attn = weight_grad(act_one, d_packed, grouped, device_count)
    d_act_one = project_back(d_packed, w_attn)
    d_norm_one, d_gain_one = norm_backward(d_act_one, normed_one, inverse_one, gain_pair[0])
    grad_tokens = (d_middle + d_norm_one).astype(jnp.bfloat16)
    gain_parts = jnp.stack([d_gain_one, d_gain_two]).reshape(2, device_count, share)
    gain_parts = jnp.pad(gain_parts.transpose(1, 0, 2), ((0, 0), (0, 6), (0, 128 - share)))
    *grad_shards, gain_grad = reduce_to_shards(
        (d_attn, d_proj, d_w_hidden, d_back, gain_parts), (6, 2, 8, 8, 1), 1
    )
    gain_grad = gain_grad[:2, :share]
    band_rows = BLOCK // device_count
    local_squares = jnp.sum(gain_grad * gain_grad) + sum(
        (jnp.sum(shard * shard) for shard in grad_shards)
    )
    pieces = jnp.concatenate(grad_shards, 0).reshape(-1, band_rows, BLOCK)
    block_count = pieces.shape[0]
    order = lax.iota(jnp.int32, block_count)
    earlier = (owners[None, :] == owners[:, None]) & (order[None, :] < order[:, None])
    slots = owners * cap_slots + jnp.sum(earlier.astype(jnp.int32), 1)
    routing = (slots[None, :] == lax.iota(jnp.int32, device_count * cap_slots)[:, None]).astype(
        jnp.float32
    )
    routing = routing.reshape(device_count, cap_slots, block_count)
    grad_norm = jnp.sqrt(total_of(local_squares, 2))
    factor = jnp.minimum(1.0, clip_bound / grad_norm)
    arrived = lax.all_to_all(
        jnp.einsum("okb,bxy->koxy", routing, pieces, precision=highest).astype(jnp.bfloat16),
        ("wide", "narrow"),
        split_axis=1,
        concat_axis=1,
        tiled=True,
    )
    slot_grads = arrived.reshape(cap_slots, BLOCK, BLOCK)
    restored, first_new, second_new, left_new, right_new, gram, turn = soap_update(
        factor, slot_grads, moment_first, moment_second, left_stat, right_stat, left_basis, right_basis
    )
    square = (-1, BLOCK, BLOCK)
    bases = renew_bases(gram.reshape(square), turn.reshape(square))
    bases = bases.reshape(cap_slots, 2, BLOCK, BLOCK)
    left_turn, right_turn = bases[:, 0], bases[:, 1]
    returned = lax.all_to_all(
        shortened(restored.reshape(cap_slots, device_count, -1, BLOCK)),
        ("wide", "narrow"),
        split_axis=1,
        concat_axis=1,
        tiled=True,
    )
    back_pieces = jnp.einsum("okb,koxy->bxy", routing, returned, precision=highest)
    fan_list = (2 * width, max(1, width * 16 // seq_len), width, FF)
    updated = []
    offset = 0
    for master, fan_in in zip(masters, fan_list):
        band_count, band_rows, col_count = master.shape
        piece_count = band_count * (col_count // BLOCK)
        direction = from_pieces(back_pieces[offset : offset + piece_count], band_count, col_count)
        updated.append(master - fan_in ** (-0.5) * (direction + weight_decay * master))
        offset += piece_count
    clipped = gain_grad * factor
    gain_one_new = decay_rate * gain_first + (1.0 - decay_rate) * clipped
    gain_two_new = decay_rate * gain_second + (1.0 - decay_rate) * clipped * clipped
    correct = 1.0 - decay_rate**STEP
    gain_values = norm_gains - gain_rate * (gain_one_new / correct) / (
        jnp.sqrt(gain_two_new / correct) + eps_adam
    )
    return (
        block_out,
        grad_tokens,
        grad_norm,
        updated[0],
        updated[1],
        updated[2],
        updated[3],
        gain_values,
        gain_one_new,
        gain_two_new,
        first_new,
        second_new,
        left_new,
        right_new,
        left_turn,
        right_turn,
    )


def solution(mesh):
    in_specs = (
        P(("wide", "narrow"), None),
        P(("wide", "narrow"), None),
        P("wide"),
        P(),
        P(None, ("wide", "narrow"), None),
        P(None, ("wide", "narrow"), None),
        P(None, ("wide", "narrow"), None),
        P(None, ("wide", "narrow"), None),
        P(None, ("wide", "narrow")),
        P(None, ("wide", "narrow")),
        P(None, ("wide", "narrow")),
        P(("wide", "narrow"), None, None),
        P(("wide", "narrow"), None, None),
        P(("wide", "narrow"), None, None),
        P(("wide", "narrow"), None, None),
        P(("wide", "narrow"), None, None),
        P(("wide", "narrow"), None, None),
    )
    out_specs = (
        P(("wide", "narrow"), None),
        P(("wide", "narrow"), None),
        P(),
        P(None, ("wide", "narrow"), None),
        P(None, ("wide", "narrow"), None),
        P(None, ("wide", "narrow"), None),
        P(None, ("wide", "narrow"), None),
        P(None, ("wide", "narrow")),
        P(None, ("wide", "narrow")),
        P(None, ("wide", "narrow")),
        P(("wide", "narrow"), None, None),
        P(("wide", "narrow"), None, None),
        P(("wide", "narrow"), None, None),
        P(("wide", "narrow"), None, None),
        P(("wide", "narrow"), None, None),
        P(("wide", "narrow"), None, None),
    )
    return jax.shard_map(body, mesh=mesh, in_specs=in_specs, out_specs=out_specs, check_vma=False)
```

```python
from functools import partial

import jax
import jax.numpy as jnp
from jax import lax
from jax.experimental import pallas as pl
from jax.experimental.pallas import tpu as pltpu
from jax.sharding import PartitionSpec as P

FF = 4096
HEADS = 16
HEAD = 64
BLOCK = 256
STEP = 10


eps_norm = 1e-05
eps_adam = 1e-08
decay_rate = 0.5
clip_bound = 1.0
weight_decay = 0.01
gain_rate = 1.0
neg_large = -1e30
highest = lax.Precision.HIGHEST
float32 = jnp.float32
bfloat16 = jnp.bfloat16
PAIR = 2 * HEAD
NT = (((1,), (1,)), ((), ()))
TN = (((0,), (0,)), ((), ()))
MESH = pl.DeviceIdType.MESH
VMEM_LIMIT = 48 * 2**20
AHEAD = 4
SKEW = 3
PACE = 0.9
DELAY = 1.0


def shortened(shard):
    return jax.tree.map(lambda a: a.astype(jnp.bfloat16) if a.dtype == jnp.float32 else a, shard)


def normalize(values):
    center = values - jnp.mean(values, -1, keepdims=True)
    inverse = lax.rsqrt(jnp.mean(center * center, -1, keepdims=True) + eps_norm)
    return (center * inverse, inverse)


def norm_backward(d_result, normed, inverse, gain):
    scaled = d_result * gain
    d_gain = jnp.sum(d_result * normed, 0)
    d_input = inverse * (
        scaled
        - jnp.mean(scaled, -1, keepdims=True)
        - normed * jnp.mean(scaled * normed, -1, keepdims=True)
    )
    return (d_input, d_gain)


def from_pieces(pieces, band_count, col_count):
    band_rows = pieces.shape[1]
    return (
        pieces.reshape(band_count, col_count // BLOCK, band_rows, BLOCK)
        .transpose(0, 2, 1, 3)
        .reshape(band_count, band_rows, col_count)
    )


def one_head(matrix, head):
    lane = lax.broadcasted_iota(jnp.int32, matrix.shape, 1)
    return jnp.where(lane // HEAD == head, matrix, jnp.zeros_like(matrix))


def hide(scores, start, safe, length):
    if start + scores.shape[0] <= safe:
        return scores
    position = start + lax.broadcasted_iota(jnp.int32, scores.shape, 0)
    return jnp.where(position < length, scores, neg_large)


def attend_kernel(safe, chunk, length_ref, q_ref, k_ref, v_ref, o_ref, log_ref, vt_ref, s_ref):
    seq_len = k_ref.shape[0]
    length = length_ref[0]

    @pl.when(pl.program_id(1) == 0)
    def _():
        vt_ref[...] = v_ref[...].T

    outs = []
    for head in range(2):
        queries = one_head(q_ref[...], head) * bfloat16(HEAD**-0.5)
        topmost = None
        for at in range(0, seq_len, chunk):
            scores = lax.dot_general(
                k_ref[at : at + chunk, :], queries, NT, preferred_element_type=float32
            )
            scores = hide(scores, at, safe, length)
            s_ref[head, at : at + chunk, :] = scores
            top = jnp.max(scores, 0, keepdims=True)
            topmost = top if topmost is None else jnp.maximum(topmost, top)
        totals = jnp.zeros_like(topmost)
        mixed = jnp.zeros((HEAD, q_ref.shape[0]), float32)
        for at in range(0, seq_len, chunk):
            expo = jnp.exp(s_ref[head, at : at + chunk, :] - topmost)
            totals += jnp.sum(expo, 0, keepdims=True)
            mixed += jnp.dot(
                vt_ref[head * HEAD : (head + 1) * HEAD, at : at + chunk],
                expo.astype(bfloat16),
                preferred_element_type=float32,
            )
        outs.append(mixed * (1.0 / totals))
        log_ref[0, head : head + 1, :] = topmost + jnp.log(totals)
    o_ref[...] = jnp.concatenate(outs, 0).T.astype(bfloat16)


def attend(lengths, scene, safe, rows=1024, chunk=512):
    seq_len, width = scene.shape[0], scene.shape[1] // 3
    pairs = width // PAIR
    return pl.pallas_call(
        partial(attend_kernel, safe, chunk),
        grid=(pairs, seq_len // rows),
        in_specs=[
            pl.BlockSpec(memory_space=pltpu.SMEM),
            pl.BlockSpec((rows, PAIR), lambda p, i: (i, p)),
            pl.BlockSpec((seq_len, PAIR), lambda p, i: (0, pairs + p)),
            pl.BlockSpec((seq_len, PAIR), lambda p, i: (0, 2 * pairs + p)),
        ],
        out_specs=[
            pl.BlockSpec((rows, PAIR), lambda p, i: (i, p)),
            pl.BlockSpec((1, 2, rows), lambda p, i: (p, 0, i)),
        ],
        out_shape=[
            jax.ShapeDtypeStruct((seq_len, width), bfloat16),
            jax.ShapeDtypeStruct((pairs, 2, seq_len), float32),
        ],
        scratch_shapes=[
            pltpu.VMEM((PAIR, seq_len), bfloat16),
            pltpu.VMEM((2, seq_len, rows), float32),
        ],
        compiler_params=pltpu.CompilerParams(vmem_limit_bytes=VMEM_LIMIT),
        cost_estimate=pl.CostEstimate(
            flops=4 * pairs * 2 * 4 * seq_len * seq_len * HEAD,
            bytes_accessed=8 * seq_len * width,
            transcendentals=0,
        ),
    )(lengths, scene, scene, scene)


def attend_backward_kernel(safe, chunk, plan, slots, length_ref, q_ref, k_ref, v_ref, o_ref, do_ref, log_ref, *refs):
    count = plan[4]
    sources, out_ref, outs = refs[:count], refs[count], refs[count + 1 : 2 * count + 1]
    kt_ref, dk_sum, dv_sum = refs[2 * count + 1 : 2 * count + 4]
    peers, begin, finish, drain = reduce_steps(*plan[:4], sources, outs, refs[2 * count + 4 :])
    total = len(plan[3])
    seq_len = k_ref.shape[0]
    length = length_ref[0]
    step = pl.program_id(0)

    def move(chunk, stage):
        finish(chunk, stage)
        if stage == 0 and chunk + AHEAD < total:
            begin(chunk + AHEAD)

    def move_at(head):
        for at in range(head, len(slots) - 1, 2):
            if slots[at]:

                @pl.when(step == at // 2)
                def _(at=at):
                    for chunk, stage in slots[at]:
                        move(chunk, stage)

    @pl.when(step == 0)
    def _():
        greet(peers)
        for chunk in range(min(AHEAD, total)):
            begin(chunk)
        kt_ref[...] = k_ref[...].T
        dk_sum[...] = jnp.zeros_like(dk_sum)
        dv_sum[...] = jnp.zeros_like(dv_sum)

    products = (o_ref[...].astype(float32) * do_ref[...].astype(float32)).T
    turned = []
    for head in range(2):
        move_at(head)
        lanes = slice(head * HEAD, (head + 1) * HEAD)
        queries = one_head(q_ref[...], head) * bfloat16(HEAD**-0.5)
        d_mixed = one_head(do_ref[...], head)
        inner = jnp.sum(products[lanes, :], 0, keepdims=True)
        log_total = log_ref[0, head : head + 1, :]
        d_queries = jnp.zeros((HEAD, q_ref.shape[0]), float32)
        for at in range(0, seq_len, chunk):
            part = slice(at, at + chunk)
            scores = lax.dot_general(k_ref[part, :], queries, NT, preferred_element_type=float32)
            probs = jnp.exp(hide(scores, at, safe, length) - log_total)
            d_probs = lax.dot_general(v_ref[part, :], d_mixed, NT, preferred_element_type=float32)
            dv_sum[part, :] += jnp.dot(
                probs.astype(bfloat16), d_mixed, preferred_element_type=float32
            )
            d_scores = (probs * (d_probs - inner)).astype(bfloat16)
            dk_sum[part, :] += jnp.dot(d_scores, queries, preferred_element_type=float32)
            d_queries += jnp.dot(kt_ref[lanes, part], d_scores, preferred_element_type=float32)
        turned.append(d_queries * HEAD**-0.5)
    rows = q_ref.shape[0]
    here = pl.ds(pl.multiple_of(step * rows, rows), rows)
    out_ref[here, :PAIR] = jnp.concatenate(turned, 0).T.astype(bfloat16)

    @pl.when(step == pl.num_programs(0) - 1)
    def _():
        out_ref[:, PAIR : 2 * PAIR] = dk_sum[...].astype(bfloat16)
        out_ref[:, 2 * PAIR :] = dv_sum[...].astype(bfloat16)
        for chunk, stage in slots[-1]:
            move(chunk, stage)
        drain()


def attend_backward(
    lengths, scene, mixed, d_mixed, log_totals, safe, parts, pieces, collective_id, rows=512, chunk=1024
):
    seq_len = scene.shape[0]
    bits, narrow_bits, plans, chunks, halved, outs, scratch = reduce_plan(parts, pieces)
    steps = seq_len // rows
    slots = reduce_slots(len(chunks), bits, 2 * steps, PACE, DELAY)
    tile = pl.BlockSpec((rows, PAIR), lambda i: (i, 0))
    return pl.pallas_call(
        partial(
            attend_backward_kernel,
            safe,
            chunk,
            (bits, narrow_bits, plans, chunks, len(parts)),
            slots,
        ),
        grid=(steps,),
        in_specs=[
            pl.BlockSpec(memory_space=pltpu.SMEM),
            tile,
            pl.BlockSpec((seq_len, PAIR), lambda i: (0, 1)),
            pl.BlockSpec((seq_len, PAIR), lambda i: (0, 2)),
            tile,
            tile,
            pl.BlockSpec((1, 2, rows), lambda i: (0, 0, i)),
        ]
        + [pl.BlockSpec(memory_space=pl.ANY)] * len(parts),
        out_specs=[pl.BlockSpec((seq_len, 3 * PAIR), lambda i: (0, 0))]
        + [pl.BlockSpec(out.shape, lambda i: (0, 0)) for out in outs],
        out_shape=[jax.ShapeDtypeStruct((seq_len, 3 * PAIR), bfloat16)] + outs,
        scratch_shapes=[
            pltpu.VMEM((PAIR, seq_len), bfloat16),
            pltpu.VMEM((seq_len, PAIR), float32),
            pltpu.VMEM((seq_len, PAIR), float32),
        ]
        + scratch,
        compiler_params=pltpu.CompilerParams(
            collective_id=collective_id, has_side_effects=True, vmem_limit_bytes=58 * 2**20
        ),
        cost_estimate=pl.CostEstimate(
            flops=4 * 2 * 10 * seq_len * seq_len * HEAD,
            bytes_accessed=16 * seq_len * PAIR,
            transcendentals=0,
        ),
    )(lengths, scene, scene, scene, mixed, d_mixed, log_totals, *halved)


def project_kernel(acts_ref, wq_ref, wk_ref, wv_ref, *out_refs):
    thirds = (wq_ref, wk_ref, wv_ref)
    halves = len(out_refs)
    weights = jnp.concatenate(
        [third[:, h * PAIR : (h + 1) * PAIR] for h in range(halves) for third in thirds], 1
    )
    result = jnp.dot(acts_ref[...], weights, preferred_element_type=float32).astype(bfloat16)
    for h, out_ref in enumerate(out_refs):
        out_ref[0] = result[:, h * 3 * PAIR : (h + 1) * 3 * PAIR]


def project(acts, weights, groups):
    tok_rows, width = acts.shape
    head_width = width // groups
    halves = head_width // PAIR

    def third(k):
        return pl.BlockSpec((width, head_width), lambda g: (0, k * groups + g))

    return pl.pallas_call(
        project_kernel,
        grid=(groups,),
        in_specs=[pl.BlockSpec((tok_rows, width), lambda g: (0, 0)), third(0), third(1), third(2)],
        out_specs=[pl.BlockSpec((1, tok_rows, 3 * PAIR), lambda g: (g, 0, 0))] * halves,
        out_shape=[jax.ShapeDtypeStruct((groups, tok_rows, 3 * PAIR), bfloat16)] * halves,
        compiler_params=pltpu.CompilerParams(vmem_limit_bytes=VMEM_LIMIT),
        cost_estimate=pl.CostEstimate(
            flops=6 * tok_rows * width**2, bytes_accessed=6 * width**2 + 8 * tok_rows * width,
            transcendentals=0,
        ),
    )(acts, weights, weights, weights)


def project_back_kernel(halves, *refs):
    grads, (wq_ref, wk_ref, wv_ref, out_ref) = refs[:halves], refs[halves:]
    thirds = (wq_ref, wk_ref, wv_ref)
    weights = jnp.concatenate(
        [third[:, h * PAIR : (h + 1) * PAIR] for h in range(halves) for third in thirds], 1
    )
    rows = jnp.concatenate([grad[0] for grad in grads], 1)
    result = lax.dot_general(rows, weights, NT, preferred_element_type=float32)

    @pl.when(pl.program_id(0) == 0)
    def _():
        out_ref[...] = result

    @pl.when(pl.program_id(0) > 0)
    def _():
        out_ref[...] += result


def project_back(grads, weights):
    groups, tok_rows, _ = grads[0].shape
    width = weights.shape[0]
    head_width = width // groups

    def third(k):
        return pl.BlockSpec((width, head_width), lambda g: (0, k * groups + g))

    return pl.pallas_call(
        partial(project_back_kernel, len(grads)),
        grid=(groups,),
        in_specs=[pl.BlockSpec((1, tok_rows, 3 * PAIR), lambda g: (g, 0, 0))] * len(grads)
        + [third(0), third(1), third(2)],
        out_specs=pl.BlockSpec((tok_rows, width), lambda g: (0, 0)),
        out_shape=jax.ShapeDtypeStruct((tok_rows, width), float32),
        compiler_params=pltpu.CompilerParams(vmem_limit_bytes=VMEM_LIMIT),
        cost_estimate=pl.CostEstimate(
            flops=6 * tok_rows * width**2, bytes_accessed=6 * width**2 + 10 * tok_rows * width,
            transcendentals=0,
        ),
    )(*grads, weights, weights, weights)


def exact(left, right, dims=(((1,), (0,)), ((), ()))):
    return lax.dot_general(left, right, dims, precision=highest, preferred_element_type=float32)


def soap_kernel(
    factor_ref, g_ref, first_ref, second_ref, ls_ref, rs_ref, lb_ref, rb_ref,
    back_ref, first_out, second_out, ls_out, rs_out, gram_ref, turn_ref,
):
    gradient = factor_ref[0, 0] * g_ref[0].astype(float32)
    left_base, right_base = lb_ref[0], rb_ref[0]
    left_new = decay_rate * ls_ref[0] + (1.0 - decay_rate) * exact(gradient, gradient, NT)
    right_new = decay_rate * rs_ref[0] + (1.0 - decay_rate) * exact(gradient, gradient, TN)
    ls_out[0] = left_new
    rs_out[0] = right_new
    turned = exact(left_base, exact(gradient, right_base), TN)
    first_new = decay_rate * first_ref[0] + (1.0 - decay_rate) * turned
    second_new = decay_rate * second_ref[0] + (1.0 - decay_rate) * turned * turned
    first_out[0] = first_new
    second_out[0] = second_new
    correct = 1.0 - decay_rate**STEP
    direction = first_new / correct / (jnp.sqrt(second_new / correct) + eps_adam)
    back_ref[0] = exact(left_base, exact(direction, right_base, NT)).astype(back_ref.dtype)
    for side, stat, base in ((0, left_new, left_base), (1, right_new, right_base)):
        turn = exact(stat, base).T
        turn_ref[0, side] = turn
        gram_ref[0, side] = exact(turn, turn, NT)


def soap_update(factor, gradient, first_old, second_old, left_old, right_old, left_base, right_base):
    slots, order, _ = gradient.shape
    one = pl.BlockSpec((1, order, order), lambda s: (s, 0, 0))
    two = pl.BlockSpec((1, 2, order, order), lambda s: (s, 0, 0, 0))
    single = jax.ShapeDtypeStruct((slots, order, order), float32)
    double = jax.ShapeDtypeStruct((slots, 2, order, order), float32)
    return pl.pallas_call(
        soap_kernel,
        grid=(slots,),
        in_specs=[pl.BlockSpec(memory_space=pltpu.SMEM)] + [one] * 7,
        out_specs=[one] * 5 + [two] * 2,
        out_shape=[jax.ShapeDtypeStruct((slots, order, order), bfloat16)] + [single] * 4 + [double] * 2,
        compiler_params=pltpu.CompilerParams(vmem_limit_bytes=VMEM_LIMIT),
        cost_estimate=pl.CostEstimate(
            flops=slots * 120 * order**3, bytes_accessed=slots * 60 * order**2, transcendentals=0
        ),
    )(factor.reshape(1, 1), gradient, first_old, second_old, left_old, right_old, left_base, right_base)


def renew_kernel(rows, gram_ref, turn_ref, q_ref, x_ref, u_ref):
    count, order = gram_ref.shape[0], gram_ref.shape[1]
    eye = (
        lax.broadcasted_iota(jnp.int32, (rows, rows), 0)
        == lax.broadcasted_iota(jnp.int32, (rows, rows), 1)
    ).astype(float32)
    sublane = lax.broadcasted_iota(jnp.int32, (1, 8, 1), 1)
    for low in range(0, order, rows):
        part = slice(low, low + rows)

        def panel(at, carry, low=low, part=part):
            row = jnp.concatenate([gram_ref[at, part, :], turn_ref[at, part, :]], 1)
            if low:
                row = row - exact(u_ref[at, :low, part], u_ref[at, :low, :], TN)
            u_ref[at, part, :] = row
            x_ref[at] = jnp.concatenate([row[:, part], eye], 1)
            return carry

        lax.fori_loop(0, count, panel, 0, unroll=2)
        for j in range(rows):
            tile = j // 8 * 8
            row = x_ref[:, j : j + 1, :]
            row = row * (1.0 / row[:, :, j : j + 1])
            top = x_ref[:, tile : tile + 8, :]
            below = jnp.where(sublane > j - tile, top[:, :, j : j + 1], 0.0)
            x_ref[:, tile : tile + 8, :] = top - below * row
            if tile + 8 < rows:
                rest = x_ref[:, tile + 8 :, :]
                x_ref[:, tile + 8 :, :] = rest - rest[:, :, j : j + 1] * row

        def solve(at, carry, part=part):
            both = x_ref[at]
            diagonal = jnp.sum(both[:, :rows] * eye, 1, keepdims=True)
            u_ref[at, part, :] = exact(both[:, rows:] * lax.rsqrt(diagonal), u_ref[at, part, :])
            return carry

        lax.fori_loop(0, count, solve, 0, unroll=2)

    def turn_back(at, carry):
        q_ref[at] = u_ref[at, :, order:].T
        return carry

    lax.fori_loop(0, count, turn_back, 0)


def renew_bases(gram, turn, rows=64):
    count, order, _ = gram.shape
    return pl.pallas_call(
        partial(renew_kernel, rows),
        out_shape=jax.ShapeDtypeStruct(gram.shape, float32),
        in_specs=[pl.BlockSpec(memory_space=pltpu.VMEM)] * 2,
        out_specs=pl.BlockSpec(memory_space=pltpu.VMEM),
        scratch_shapes=[
            pltpu.VMEM((count, rows, 2 * rows), float32),
            pltpu.VMEM((count, order, 2 * order), float32),
        ],
        compiler_params=pltpu.CompilerParams(vmem_limit_bytes=VMEM_LIMIT),
        cost_estimate=pl.CostEstimate(
            flops=count * 200 * order**3, bytes_accessed=count * 12 * order**2, transcendentals=0
        ),
    )(gram, turn)


def exchange(groups):
    return lax.all_to_all(groups, "narrow", split_axis=0, concat_axis=0, tiled=True)


def partner(bit, narrow_bits):
    axis, step = ("narrow", 1 << bit) if bit < narrow_bits else ("wide", 1 << (bit - narrow_bits))
    place = lax.axis_index(axis)
    mine = lax.rem(place // step, 2)
    return {axis: place + step - 2 * step * mine}, mine


def greet(peers):
    barrier = pltpu.get_barrier_semaphore()
    for device, _ in peers:
        pl.semaphore_signal(barrier, inc=1, device_id=device, device_id_type=MESH)
    pl.semaphore_wait(barrier, len(peers))


def mesh_bits():
    narrow_bits = lax.axis_size("narrow").bit_length() - 1
    return narrow_bits + lax.axis_size("wide").bit_length() - 1, narrow_bits


def reduce_steps(bits, narrow_bits, plans, chunks, sources, outs, scratch):
    count = len(sources)
    held = scratch[:count]
    arrived = [scratch[count * (1 + s) : count * (2 + s)] for s in range(bits)]
    load_sem, send_sem, recv_sem = scratch[count * (1 + bits) :]
    peers = [partner(b, narrow_bits) for b in range(bits)]
    first = plans[0][0]
    order_of_dims = list(reversed(range(bits)))
    whole = slice(None)

    def within(order, stage, current):
        return tuple(
            peers[b][1] if b in order[:stage] else current if b == order[stage] else whole
            for b in order_of_dims
            if b != first
        )

    def of_source(value):
        return tuple(value if b == first else whole for b in order_of_dims)

    def rows_of(chunk):
        at, row, rows, colour = chunks[chunk]
        return at, plans[colour], (pl.ds(row, rows), whole)

    def send(chunk, stage):
        at, order, part = rows_of(chunk)
        device, mine = peers[order[stage]]
        if stage == 0:
            source = sources[at].at[of_source(1 - mine) + part]
        else:
            source = held[at].at[within(order, stage, 1 - mine) + part]
        return pltpu.make_async_remote_copy(
            src_ref=source,
            dst_ref=arrived[stage][at].at[(whole,) * (bits - 1 - stage) + part],
            send_sem=send_sem.at[chunk, stage],
            recv_sem=recv_sem.at[chunk, stage],
            device_id=device,
            device_id_type=MESH,
        )

    def load(chunk):
        at, order, part = rows_of(chunk)
        return pltpu.make_async_copy(
            sources[at].at[of_source(peers[first][1]) + part],
            held[at].at[(whole,) * (bits - 1) + part],
            load_sem.at[chunk],
        )

    def begin(chunk):
        send(chunk, 0).start()
        load(chunk).start()

    def finish(chunk, stage):
        at, order, part = rows_of(chunk)
        if stage == 0:
            load(chunk).wait()
        send(chunk, stage).wait_recv()
        left = bits - 1 - stage
        keep = within(order, stage, peers[order[stage]][1])
        if left == 0:
            own = held[at][keep + part].astype(float32)
            outs[at][part] = own + arrived[stage][at][part].astype(float32)
            return
        free = [i for i, k in enumerate(keep) if isinstance(k, slice)]

        def add(m, carry):
            which = tuple(m // (1 << (left - 1 - i)) % 2 for i in range(left))
            spot = list(keep)
            for i, f in enumerate(free):
                spot[f] = which[i]
            spot = tuple(spot) + part
            held[at][spot] = held[at][spot] + arrived[stage][at][which + part]
            return carry

        lax.fori_loop(0, 1 << left, add, 0)
        send(chunk, stage + 1).start()

    def drain():
        for chunk in range(len(chunks)):
            for stage in range(bits):
                send(chunk, stage).wait_send()

    return peers, begin, finish, drain


def reduce_kernel(bits, narrow_bits, plans, chunks, count, *refs):
    peers, begin, finish, drain = reduce_steps(
        bits, narrow_bits, plans, chunks, refs[:count], refs[count : 2 * count], refs[2 * count :]
    )
    greet(peers)
    total = len(chunks)
    for chunk in range(min(AHEAD, total)):
        begin(chunk)
    for step in range(total + 2 * bits):
        for stage in reversed(range(bits)):
            chunk = step - 2 * stage
            if 0 <= chunk < total:
                finish(chunk, stage)
                if stage == 0 and chunk + AHEAD < total:
                    begin(chunk + AHEAD)
    drain()


def reduce_slots(chunks, bits, slots, pace, delay):
    table = [[] for _ in range(slots + 1)]
    done = sorted(
        (chunk * pace + (stage + 1) * delay, -stage, chunk, stage)
        for chunk in range(chunks)
        for stage in range(bits)
    )
    for when, _, chunk, stage in done:
        table[min(int(when), slots)].append((chunk, stage))
    return table


def reduce_plan(parts, pieces):
    bits, narrow_bits = mesh_bits()
    shapes = [part.shape[1:] for part in parts]
    kinds = [part.dtype for part in parts]
    chunks = []
    for at, (shape, cut) in enumerate(zip(shapes, pieces)):
        rows = shape[0] // cut
        for row in range(0, shape[0], rows):
            chunks.append((at, row, rows, len(chunks) % 2))
    later = tuple(range(3, bits))
    plans = ((0, 2, 1) + later, (0, 1, 2) + later)
    sizes = [bits - 1] + [bits - 1 - stage for stage in range(bits)]
    scratch = [
        pltpu.VMEM((2,) * size + shape, kind)
        for size in sizes
        for shape, kind in zip(shapes, kinds)
    ]
    total = len(chunks)
    scratch += [
        pltpu.SemaphoreType.DMA((total,)),
        pltpu.SemaphoreType.DMA((total, bits)),
        pltpu.SemaphoreType.DMA((total, bits)),
    ]
    outs = [jax.ShapeDtypeStruct(shape, float32) for shape in shapes]
    halved = [part.reshape((2,) * bits + shape) for part, shape in zip(parts, shapes)]
    return bits, narrow_bits, plans, tuple(chunks), halved, outs, scratch


def reduce_to_shards(parts, pieces, collective_id):
    bits, narrow_bits, plans, chunks, halved, outs, scratch = reduce_plan(parts, pieces)
    return pl.pallas_call(
        partial(reduce_kernel, bits, narrow_bits, plans, chunks, len(parts)),
        out_shape=outs,
        in_specs=[pl.BlockSpec(memory_space=pl.ANY)] * len(parts),
        out_specs=[pl.BlockSpec(memory_space=pltpu.VMEM)] * len(parts),
        scratch_shapes=scratch,
        compiler_params=pltpu.CompilerParams(
            collective_id=collective_id, has_side_effects=True, vmem_limit_bytes=58 * 2**20
        ),
        cost_estimate=pl.CostEstimate(flops=10**8, bytes_accessed=4 * 10**8, transcendentals=0),
    )(*halved)


def gather_kernel(bits, narrow_bits, plans, chunks, count, *refs):
    sources, outs = refs[:count], refs[count : 2 * count]
    own_sem, send_sem, recv_sem = refs[2 * count :]
    peers = [partner(b, narrow_bits) for b in range(bits)]
    greet(peers)
    dims = list(reversed(range(bits)))

    def place(chunk, stage):
        at, band, bands, col, cols, colour = chunks[chunk]
        done = plans[colour][:stage]
        index = tuple(slice(None) if b in done else peers[b][1] for b in dims)
        return outs[at].at[(pl.ds(band, bands),) + index + (slice(None), pl.ds(col, cols))]

    def own(chunk):
        at, band, bands, col, cols, colour = chunks[chunk]
        return sources[at].at[pl.ds(band, bands), :, pl.ds(col, cols)]

    def send(chunk, stage):
        colour = chunks[chunk][-1]
        target = place(chunk, stage)
        return pltpu.make_async_remote_copy(
            src_ref=target if stage else own(chunk),
            dst_ref=target,
            send_sem=send_sem.at[chunk, stage],
            recv_sem=recv_sem.at[chunk, stage],
            device_id=peers[plans[colour][stage]][0],
            device_id_type=MESH,
        )

    def keep(chunk):
        return pltpu.make_async_copy(own(chunk), place(chunk, 0), own_sem.at[chunk])

    total = len(chunks)
    for chunk in range(total):
        send(chunk, 0).start()
        keep(chunk).start()
    for step in range(total + SKEW * bits):
        for stage in reversed(range(bits)):
            chunk = step - SKEW * stage
            if 0 <= chunk < total:
                if stage == 0:
                    keep(chunk).wait()
                send(chunk, stage).wait_recv()
                if stage + 1 < bits:
                    send(chunk, stage + 1).start()
    for chunk in range(total):
        for stage in range(bits):
            send(chunk, stage).wait_send()


def gather_bands(parts, pieces, collective_id):
    bits, narrow_bits = mesh_bits()
    chunks = []
    for at, (part, (cut, cut_cols)) in enumerate(zip(parts, pieces)):
        bands, cols = part.shape[0] // cut, part.shape[2] // cut_cols
        for band in range(0, part.shape[0], bands):
            for col in range(0, part.shape[2], cols):
                chunks.append((at, band, bands, col, cols, len(chunks) % 2))
    later = tuple(reversed(range(3, bits)))
    plans = (later + (1, 2, 0), later + (2, 1, 0))
    total = len(chunks)
    results = pl.pallas_call(
        partial(gather_kernel, bits, narrow_bits, plans, tuple(chunks), len(parts)),
        out_shape=[
            jax.ShapeDtypeStruct(part.shape[:1] + (2,) * bits + part.shape[1:], part.dtype)
            for part in parts
        ],
        in_specs=[pl.BlockSpec(memory_space=pl.ANY)] * len(parts),
        out_specs=[pl.BlockSpec(memory_space=pl.ANY)] * len(parts),
        scratch_shapes=[
            pltpu.SemaphoreType.DMA((total,)),
            pltpu.SemaphoreType.DMA((total, bits)),
            pltpu.SemaphoreType.DMA((total, bits)),
        ],
        compiler_params=pltpu.CompilerParams(collective_id=collective_id, has_side_effects=True),
        cost_estimate=pl.CostEstimate(flops=0, bytes_accessed=10**8, transcendentals=0),
    )(*parts)
    return [
        result.reshape(part.shape[:1] + (1 << bits,) + part.shape[1:])
        for result, part in zip(results, parts)
    ]


def total_kernel(bits, narrow_bits, own_ref, sum_ref, arrived, send_sem, recv_sem):
    peers = [partner(b, narrow_bits) for b in range(bits)]
    greet(peers)
    sum_ref[...] = own_ref[...]
    for stage in range(bits):
        copy = pltpu.make_async_remote_copy(
            src_ref=sum_ref,
            dst_ref=arrived.at[stage],
            send_sem=send_sem.at[stage],
            recv_sem=recv_sem.at[stage],
            device_id=peers[stage][0],
            device_id_type=MESH,
        )
        copy.start()
        copy.wait()
        sum_ref[...] = sum_ref[...] + arrived[stage]


def total_of(value, collective_id):
    bits, narrow_bits = mesh_bits()
    tile = (8, 128)
    return pl.pallas_call(
        partial(total_kernel, bits, narrow_bits),
        out_shape=jax.ShapeDtypeStruct(tile, float32),
        in_specs=[pl.BlockSpec(memory_space=pltpu.VMEM)],
        out_specs=pl.BlockSpec(memory_space=pltpu.VMEM),
        scratch_shapes=[
            pltpu.VMEM((bits,) + tile, float32),
            pltpu.SemaphoreType.DMA((bits,)),
            pltpu.SemaphoreType.DMA((bits,)),
        ],
        compiler_params=pltpu.CompilerParams(collective_id=collective_id, has_side_effects=True),
    )(jnp.broadcast_to(value, tile))[0, 0]


def weight_grad_kernel(columns, band_rows, left_ref, *refs):
    right_refs, out_ref = refs[:-1], refs[-1]
    left = left_ref[...].T
    for at in range(0, len(columns), 2):
        blocks = []
        for spots in columns[at : at + 2]:
            right = [right_refs[i][g, :, start : start + size] for i, g, start, size in spots]
            right = right[0] if len(right) == 1 else jnp.concatenate(right, 1)
            block = jnp.dot(left, right, preferred_element_type=float32)
            blocks.append(block.astype(bfloat16).reshape(-1, band_rows, BLOCK))
        out_ref[:, at * band_rows : (at + 2) * band_rows, :] = jnp.concatenate(blocks, 1)


def weight_grad(left, rights, columns, device_count):
    tok_rows, height = left.shape
    band_rows = BLOCK // device_count
    bands, wide = height // BLOCK, len(columns)
    if band_rows % 8:
        right = [rights[i][g, :, start : start + n] for spots in columns for i, g, start, n in spots]
        right = jnp.concatenate(right, 1)
        product = jnp.einsum("td,te->de", left, right, preferred_element_type=float32)
        product = product.astype(bfloat16).reshape(bands, device_count, band_rows, wide, BLOCK)
        return product.transpose(1, 0, 3, 2, 4).reshape(device_count, -1, BLOCK)
    return pl.pallas_call(
        partial(weight_grad_kernel, columns, band_rows),
        grid=(bands,),
        in_specs=[
            pl.BlockSpec((tok_rows, BLOCK), lambda i: (0, i)),
        ]
        + [pl.BlockSpec(right.shape, lambda i: (0, 0, 0)) for right in rights],
        out_specs=pl.BlockSpec((device_count, wide * band_rows, BLOCK), lambda i: (0, i, 0)),
        out_shape=jax.ShapeDtypeStruct((device_count, bands * wide * band_rows, BLOCK), bfloat16),
        compiler_params=pltpu.CompilerParams(vmem_limit_bytes=VMEM_LIMIT),
        cost_estimate=pl.CostEstimate(
            flops=2 * tok_rows * bands * wide * BLOCK**2,
            bytes_accessed=2 * (tok_rows * (height + wide * BLOCK) + bands * wide * BLOCK**2),
            transcendentals=0,
        ),
    )(left, *rights)


def body(
    tokens,
    cotangent,
    lengths,
    owners,
    w_qkv,
    w_out,
    w_up,
    w_down,
    norm_gains,
    gain_first,
    gain_second,
    moment_first,
    moment_second,
    left_stat,
    right_stat,
    left_basis,
    right_basis,
):
    tok_rows, width = tokens.shape
    narrow_count = lax.axis_size("narrow")
    device_count = lax.axis_size("wide") * narrow_count
    seq_len = tok_rows * narrow_count
    cap_slots = moment_first.shape[0]
    masters = (w_qkv, w_out, w_up, w_down)
    lowered = tuple((layout.astype(jnp.bfloat16) for layout in masters)) + (
        norm_gains.astype(jnp.bfloat16),
    )
    share = norm_gains.shape[1]
    gains_low = jnp.pad(lowered[4], ((0, 6), (0, 128 - share)))[None]
    w_attn, gain_pair = gather_bands((lowered[0], gains_low), ((4, 2), (1, 1)), 3)
    w_attn = w_attn.reshape(width, 3 * width)
    gain_pair = gain_pair[0, :, :2, :share].transpose(1, 0, 2).reshape(2, width)
    gain_pair = gain_pair.astype(jnp.float32)
    w_proj, w_hidden, w_back = (
        gathered.reshape(-1, gathered.shape[2])
        for gathered in lax.all_gather(lowered[1:4], ("wide", "narrow"), axis=1, tiled=True)
    )
    inputs = tokens.astype(jnp.float32)
    normed_one, inverse_one = normalize(inputs)
    act_one = (normed_one * gain_pair[0]).astype(jnp.bfloat16)
    head_width = width // narrow_count
    safe = seq_len - tok_rows
    halves = head_width // PAIR
    scenes = [
        exchange(part).reshape(seq_len, 3 * PAIR)
        for part in project(act_one, w_attn, narrow_count)
    ]
    attended = [attend(lengths, scene, safe) for scene in scenes]
    merged = [exchange(o.reshape(narrow_count, tok_rows, PAIR)) for o, _ in attended]
    merged = jnp.concatenate(
        [merged[half][group] for group in range(narrow_count) for half in range(halves)], 1
    )
    middle = inputs + jnp.dot(merged, w_proj, preferred_element_type=jnp.float32)
    normed_two, inverse_two = normalize(middle)
    act_two = (normed_two * gain_pair[1]).astype(jnp.bfloat16)
    hidden = jnp.dot(act_two, w_hidden, preferred_element_type=jnp.float32)
    active = jax.nn.gelu(hidden, approximate=True).astype(jnp.bfloat16)
    block_out = (middle + jnp.dot(active, w_back, preferred_element_type=jnp.float32)).astype(
        jnp.bfloat16
    )
    plain = lambda size: tuple(((0, 0, start, BLOCK),) for start in range(0, size, BLOCK))
    d_back = weight_grad(active, [cotangent[None]], plain(width), device_count)
    d_active = jnp.einsum("td,fd->tf", cotangent, w_back, preferred_element_type=jnp.float32)
    _, gelu_pull = jax.vjp(partial(jax.nn.gelu, approximate=True), hidden)
    d_hidden = gelu_pull(d_active)[0].astype(jnp.bfloat16)
    d_w_hidden = weight_grad(act_two, [d_hidden[None]], plain(FF), device_count)
    d_act_two = jnp.einsum("tf,df->td", d_hidden, w_hidden, preferred_element_type=jnp.float32)
    d_norm_two, d_gain_two = norm_backward(d_act_two, normed_two, inverse_two, gain_pair[1])
    d_middle = cotangent.astype(jnp.float32) + d_norm_two
    d_branch = d_middle.astype(jnp.bfloat16)
    d_proj = weight_grad(merged, [d_branch[None]], plain(width), device_count)
    d_merged = jnp.einsum("te,de->td", d_branch, w_proj, preferred_element_type=jnp.float32).astype(
        jnp.bfloat16
    )
    d_mixed = d_merged.reshape(tok_rows, narrow_count, halves, PAIR).transpose(2, 1, 0, 3)
    d_mixed = [exchange(d_mixed[half]).reshape(seq_len, PAIR) for half in range(halves)]
    ready = (((d_w_hidden, d_proj), (8, 2)), ((d_back,), (8,)))
    d_scenes, summed = [], []
    for half in range(halves):
        mixed, log_total = attended[half]
        parts, cuts = ready[half]
        d_scene, *sums = attend_backward(
            lengths, scenes[half], mixed, d_mixed[half], log_total, safe, parts, cuts, 4 + half
        )
        d_scenes.append(d_scene)
        summed.append(sums)
    d_packed = [exchange(d.reshape(narrow_count, tok_rows, 3 * PAIR)) for d in d_scenes]
    grouped = tuple(
        tuple((half, group, third * PAIR, PAIR) for half in range(halves))
        for third in range(3)
        for group in range(narrow_count)
    )
    d_attn = weight_grad(act_one, d_packed, grouped, device_count)
    d_act_one = project_back(d_packed, w_attn)
    d_norm_one, d_gain_one = norm_backward(d_act_one, normed_one, inverse_one, gain_pair[0])
    grad_tokens = (d_middle + d_norm_one).astype(jnp.bfloat16)
    gain_parts = jnp.stack([d_gain_one, d_gain_two]).reshape(2, device_count, share)
    gain_parts = jnp.pad(gain_parts.transpose(1, 0, 2), ((0, 0), (0, 6), (0, 128 - share)))
    attn_sum, gain_grad = reduce_to_shards((d_attn, gain_parts), (6, 1), 1)
    (hidden_sum, proj_sum), (back_sum,) = summed
    grad_shards = (attn_sum, proj_sum, hidden_sum, back_sum)
    gain_grad = gain_grad[:2, :share]
    band_rows = BLOCK // device_count
    local_squares = jnp.sum(gain_grad * gain_grad) + sum(
        (jnp.sum(shard * shard) for shard in grad_shards)
    )
    pieces = jnp.concatenate(grad_shards, 0).reshape(-1, band_rows, BLOCK)
    block_count = pieces.shape[0]
    order = lax.iota(jnp.int32, block_count)
    earlier = (owners[None, :] == owners[:, None]) & (order[None, :] < order[:, None])
    slots = owners * cap_slots + jnp.sum(earlier.astype(jnp.int32), 1)
    routing = (slots[None, :] == lax.iota(jnp.int32, device_count * cap_slots)[:, None]).astype(
        jnp.float32
    )
    routing = routing.reshape(device_count, cap_slots, block_count)
    grad_norm = jnp.sqrt(total_of(local_squares, 2))
    factor = jnp.minimum(1.0, clip_bound / grad_norm)
    arrived = lax.all_to_all(
        jnp.einsum("okb,bxy->koxy", routing, pieces, precision=highest).astype(jnp.bfloat16),
        ("wide", "narrow"),
        split_axis=1,
        concat_axis=1,
        tiled=True,
    )
    slot_grads = arrived.reshape(cap_slots, BLOCK, BLOCK)
    restored, first_new, second_new, left_new, right_new, gram, turn = soap_update(
        factor, slot_grads, moment_first, moment_second, left_stat, right_stat, left_basis, right_basis
    )
    square = (-1, BLOCK, BLOCK)
    bases = renew_bases(gram.reshape(square), turn.reshape(square))
    bases = bases.reshape(cap_slots, 2, BLOCK, BLOCK)
    left_turn, right_turn = bases[:, 0], bases[:, 1]
    returned = lax.all_to_all(
        shortened(restored.reshape(cap_slots, device_count, -1, BLOCK)),
        ("wide", "narrow"),
        split_axis=1,
        concat_axis=1,
        tiled=True,
    )
    back_pieces = jnp.einsum("okb,koxy->bxy", routing, returned, precision=highest)
    fan_list = (2 * width, max(1, width * 16 // seq_len), width, FF)
    updated = []
    offset = 0
    for master, fan_in in zip(masters, fan_list):
        band_count, band_rows, col_count = master.shape
        piece_count = band_count * (col_count // BLOCK)
        direction = from_pieces(back_pieces[offset : offset + piece_count], band_count, col_count)
        updated.append(master - fan_in ** (-0.5) * (direction + weight_decay * master))
        offset += piece_count
    clipped = gain_grad * factor
    gain_one_new = decay_rate * gain_first + (1.0 - decay_rate) * clipped
    gain_two_new = decay_rate * gain_second + (1.0 - decay_rate) * clipped * clipped
    correct = 1.0 - decay_rate**STEP
    gain_values = norm_gains - gain_rate * (gain_one_new / correct) / (
        jnp.sqrt(gain_two_new / correct) + eps_adam
    )
    return (
        block_out,
        grad_tokens,
        grad_norm,
        updated[0],
        updated[1],
        updated[2],
        updated[3],
        gain_values,
        gain_one_new,
        gain_two_new,
        first_new,
        second_new,
        left_new,
        right_new,
        left_turn,
        right_turn,
    )


def solution(mesh):
    in_specs = (
        P(("wide", "narrow"), None),
        P(("wide", "narrow"), None),
        P("wide"),
        P(),
        P(None, ("wide", "narrow"), None),
        P(None, ("wide", "narrow"), None),
        P(None, ("wide", "narrow"), None),
        P(None, ("wide", "narrow"), None),
        P(None, ("wide", "narrow")),
        P(None, ("wide", "narrow")),
        P(None, ("wide", "narrow")),
        P(("wide", "narrow"), None, None),
        P(("wide", "narrow"), None, None),
        P(("wide", "narrow"), None, None),
        P(("wide", "narrow"), None, None),
        P(("wide", "narrow"), None, None),
        P(("wide", "narrow"), None, None),
    )
    out_specs = (
        P(("wide", "narrow"), None),
        P(("wide", "narrow"), None),
        P(),
        P(None, ("wide", "narrow"), None),
        P(None, ("wide", "narrow"), None),
        P(None, ("wide", "narrow"), None),
        P(None, ("wide", "narrow"), None),
        P(None, ("wide", "narrow")),
        P(None, ("wide", "narrow")),
        P(None, ("wide", "narrow")),
        P(("wide", "narrow"), None, None),
        P(("wide", "narrow"), None, None),
        P(("wide", "narrow"), None, None),
        P(("wide", "narrow"), None, None),
        P(("wide", "narrow"), None, None),
        P(("wide", "narrow"), None, None),
    )
    return jax.shard_map(body, mesh=mesh, in_specs=in_specs, out_specs=out_specs, check_vma=False)
```

```python
from functools import partial

import jax
import jax.numpy as jnp
from jax import lax
from jax.experimental import pallas as pl
from jax.experimental.pallas import tpu as pltpu
from jax.sharding import PartitionSpec as P

FF = 4096
HEADS = 16
HEAD = 64
BLOCK = 256
STEP = 10


eps_norm = 1e-05
eps_adam = 1e-08
decay_rate = 0.5
clip_bound = 1.0
weight_decay = 0.01
gain_rate = 1.0
neg_large = -1e30
highest = lax.Precision.HIGHEST
float32 = jnp.float32
bfloat16 = jnp.bfloat16
PAIR = 2 * HEAD
NT = (((1,), (1,)), ((), ()))
TN = (((0,), (0,)), ((), ()))
MESH = pl.DeviceIdType.MESH
VMEM_LIMIT = 48 * 2**20
AHEAD = 8
SKEW = 3
ORDERS = ((0, 2, 1, None), (0, 1, 2, None), (0, 2, None, 1))
PACE = 3.7
DELAY = 12.0
GATHER_PACE = 10.0
GATHER_DELAY = 20.0


def shortened(shard):
    return jax.tree.map(lambda a: a.astype(jnp.bfloat16) if a.dtype == jnp.float32 else a, shard)


def normalize(values):
    center = values - jnp.mean(values, -1, keepdims=True)
    inverse = lax.rsqrt(jnp.mean(center * center, -1, keepdims=True) + eps_norm)
    return (center * inverse, inverse)


def norm_backward(d_result, normed, inverse, gain):
    scaled = d_result * gain
    d_gain = jnp.sum(d_result * normed, 0)
    d_input = inverse * (
        scaled
        - jnp.mean(scaled, -1, keepdims=True)
        - normed * jnp.mean(scaled * normed, -1, keepdims=True)
    )
    return (d_input, d_gain)


def from_pieces(pieces, band_count, col_count):
    band_rows = pieces.shape[1]
    return (
        pieces.reshape(band_count, col_count // BLOCK, band_rows, BLOCK)
        .transpose(0, 2, 1, 3)
        .reshape(band_count, band_rows, col_count)
    )


def one_head(matrix, head):
    lane = lax.broadcasted_iota(jnp.int32, matrix.shape, 1)
    return jnp.where(lane // HEAD == head, matrix, jnp.zeros_like(matrix))


def hide(scores, start, safe, length):
    if start + scores.shape[0] <= safe:
        return scores
    position = start + lax.broadcasted_iota(jnp.int32, scores.shape, 0)
    return jnp.where(position < length, scores, neg_large)


def project_kernel(acts_ref, wq_ref, wk_ref, wv_ref, *out_refs):
    thirds = (wq_ref, wk_ref, wv_ref)
    halves = len(out_refs)
    weights = jnp.concatenate(
        [third[:, h * PAIR : (h + 1) * PAIR] for h in range(halves) for third in thirds], 1
    )
    result = jnp.dot(acts_ref[...], weights, preferred_element_type=float32).astype(bfloat16)
    for h, out_ref in enumerate(out_refs):
        out_ref[0] = result[:, h * 3 * PAIR : (h + 1) * 3 * PAIR]


def project(acts, weights, groups):
    tok_rows, width = acts.shape
    head_width = width // groups
    halves = head_width // PAIR

    def third(k):
        return pl.BlockSpec((width, head_width), lambda g: (0, k * groups + g))

    return pl.pallas_call(
        project_kernel,
        grid=(groups,),
        in_specs=[pl.BlockSpec((tok_rows, width), lambda g: (0, 0)), third(0), third(1), third(2)],
        out_specs=[pl.BlockSpec((1, tok_rows, 3 * PAIR), lambda g: (g, 0, 0))] * halves,
        out_shape=[jax.ShapeDtypeStruct((groups, tok_rows, 3 * PAIR), bfloat16)] * halves,
        compiler_params=pltpu.CompilerParams(vmem_limit_bytes=VMEM_LIMIT),
        cost_estimate=pl.CostEstimate(
            flops=6 * tok_rows * width**2, bytes_accessed=6 * width**2 + 8 * tok_rows * width,
            transcendentals=0,
        ),
    )(acts, weights, weights, weights)


def project_back_kernel(halves, *refs):
    grads, (wq_ref, wk_ref, wv_ref, out_ref) = refs[:halves], refs[halves:]
    thirds = (wq_ref, wk_ref, wv_ref)
    weights = jnp.concatenate(
        [third[:, h * PAIR : (h + 1) * PAIR] for h in range(halves) for third in thirds], 1
    )
    rows = jnp.concatenate([grad[0] for grad in grads], 1)
    result = lax.dot_general(rows, weights, NT, preferred_element_type=float32)

    @pl.when(pl.program_id(0) == 0)
    def _():
        out_ref[...] = result

    @pl.when(pl.program_id(0) > 0)
    def _():
        out_ref[...] += result


def project_back(grads, weights):
    groups, tok_rows, _ = grads[0].shape
    width = weights.shape[0]
    head_width = width // groups

    def third(k):
        return pl.BlockSpec((width, head_width), lambda g: (0, k * groups + g))

    return pl.pallas_call(
        partial(project_back_kernel, len(grads)),
        grid=(groups,),
        in_specs=[pl.BlockSpec((1, tok_rows, 3 * PAIR), lambda g: (g, 0, 0))] * len(grads)
        + [third(0), third(1), third(2)],
        out_specs=pl.BlockSpec((tok_rows, width), lambda g: (0, 0)),
        out_shape=jax.ShapeDtypeStruct((tok_rows, width), float32),
        compiler_params=pltpu.CompilerParams(vmem_limit_bytes=VMEM_LIMIT),
        cost_estimate=pl.CostEstimate(
            flops=6 * tok_rows * width**2, bytes_accessed=6 * width**2 + 10 * tok_rows * width,
            transcendentals=0,
        ),
    )(*grads, weights, weights, weights)


def exact(left, right, dims=(((1,), (0,)), ((), ()))):
    return lax.dot_general(left, right, dims, precision=highest, preferred_element_type=float32)


def soap_kernel(
    factor_ref, g_ref, first_ref, second_ref, ls_ref, rs_ref, lb_ref, rb_ref,
    back_ref, first_out, second_out, ls_out, rs_out, gram_ref, turn_ref,
):
    gradient = factor_ref[0, 0] * g_ref[0].astype(float32)
    left_base, right_base = lb_ref[0], rb_ref[0]
    left_new = decay_rate * ls_ref[0] + (1.0 - decay_rate) * exact(gradient, gradient, NT)
    right_new = decay_rate * rs_ref[0] + (1.0 - decay_rate) * exact(gradient, gradient, TN)
    ls_out[0] = left_new
    rs_out[0] = right_new
    turned = exact(left_base, exact(gradient, right_base), TN)
    first_new = decay_rate * first_ref[0] + (1.0 - decay_rate) * turned
    second_new = decay_rate * second_ref[0] + (1.0 - decay_rate) * turned * turned
    first_out[0] = first_new
    second_out[0] = second_new
    correct = 1.0 - decay_rate**STEP
    direction = first_new / correct / (jnp.sqrt(second_new / correct) + eps_adam)
    back_ref[0] = exact(left_base, exact(direction, right_base, NT)).astype(back_ref.dtype)
    for side, stat, base in ((0, left_new, left_base), (1, right_new, right_base)):
        turn = exact(stat, base).T
        turn_ref[0, side] = turn
        gram_ref[0, side] = exact(turn, turn, NT)


def soap_update(factor, gradient, first_old, second_old, left_old, right_old, left_base, right_base):
    slots, order, _ = gradient.shape
    one = pl.BlockSpec((1, order, order), lambda s: (s, 0, 0))
    two = pl.BlockSpec((1, 2, order, order), lambda s: (s, 0, 0, 0))
    single = jax.ShapeDtypeStruct((slots, order, order), float32)
    double = jax.ShapeDtypeStruct((slots, 2, order, order), float32)
    return pl.pallas_call(
        soap_kernel,
        grid=(slots,),
        in_specs=[pl.BlockSpec(memory_space=pltpu.SMEM)] + [one] * 7,
        out_specs=[one] * 5 + [two] * 2,
        out_shape=[jax.ShapeDtypeStruct((slots, order, order), bfloat16)] + [single] * 4 + [double] * 2,
        compiler_params=pltpu.CompilerParams(vmem_limit_bytes=VMEM_LIMIT),
        cost_estimate=pl.CostEstimate(
            flops=slots * 120 * order**3, bytes_accessed=slots * 60 * order**2, transcendentals=0
        ),
    )(factor.reshape(1, 1), gradient, first_old, second_old, left_old, right_old, left_base, right_base)


def renew_kernel(rows, gram_ref, turn_ref, q_ref, x_ref, u_ref):
    count, order = gram_ref.shape[0], gram_ref.shape[1]
    eye = (
        lax.broadcasted_iota(jnp.int32, (rows, rows), 0)
        == lax.broadcasted_iota(jnp.int32, (rows, rows), 1)
    ).astype(float32)
    sublane = lax.broadcasted_iota(jnp.int32, (1, 8, 1), 1)
    for low in range(0, order, rows):
        part = slice(low, low + rows)

        def panel(at, carry, low=low, part=part):
            row = jnp.concatenate([gram_ref[at, part, :], turn_ref[at, part, :]], 1)
            if low:
                row = row - exact(u_ref[at, :low, part], u_ref[at, :low, :], TN)
            u_ref[at, part, :] = row
            x_ref[at] = jnp.concatenate([row[:, part], eye], 1)
            return carry

        lax.fori_loop(0, count, panel, 0, unroll=2)
        for j in range(rows):
            tile = j // 8 * 8
            row = x_ref[:, j : j + 1, :]
            row = row * (1.0 / row[:, :, j : j + 1])
            top = x_ref[:, tile : tile + 8, :]
            below = jnp.where(sublane > j - tile, top[:, :, j : j + 1], 0.0)
            x_ref[:, tile : tile + 8, :] = top - below * row
            if tile + 8 < rows:
                rest = x_ref[:, tile + 8 :, :]
                x_ref[:, tile + 8 :, :] = rest - rest[:, :, j : j + 1] * row

        def solve(at, carry, part=part):
            both = x_ref[at]
            diagonal = jnp.sum(both[:, :rows] * eye, 1, keepdims=True)
            u_ref[at, part, :] = exact(both[:, rows:] * lax.rsqrt(diagonal), u_ref[at, part, :])
            return carry

        lax.fori_loop(0, count, solve, 0, unroll=2)

    def turn_back(at, carry):
        q_ref[at] = u_ref[at, :, order:].T
        return carry

    lax.fori_loop(0, count, turn_back, 0)


def renew_bases(gram, turn, rows=64):
    count, order, _ = gram.shape
    return pl.pallas_call(
        partial(renew_kernel, rows),
        out_shape=jax.ShapeDtypeStruct(gram.shape, float32),
        in_specs=[pl.BlockSpec(memory_space=pltpu.VMEM)] * 2,
        out_specs=pl.BlockSpec(memory_space=pltpu.VMEM),
        scratch_shapes=[
            pltpu.VMEM((count, rows, 2 * rows), float32),
            pltpu.VMEM((count, order, 2 * order), float32),
        ],
        compiler_params=pltpu.CompilerParams(vmem_limit_bytes=VMEM_LIMIT),
        cost_estimate=pl.CostEstimate(
            flops=count * 200 * order**3, bytes_accessed=count * 12 * order**2, transcendentals=0
        ),
    )(gram, turn)


def partner(bit, narrow_bits):
    axis, step = ("narrow", 1 << bit) if bit < narrow_bits else ("wide", 1 << (bit - narrow_bits))
    place = lax.axis_index(axis)
    mine = lax.rem(place // step, 2)
    return {axis: place + step - 2 * step * mine}, mine


def greet(peers):
    barrier = pltpu.get_barrier_semaphore()
    for device, _ in peers:
        pl.semaphore_signal(barrier, inc=1, device_id=device, device_id_type=MESH)
    pl.semaphore_wait(barrier, len(peers))


def mesh_bits():
    narrow_bits = lax.axis_size("narrow").bit_length() - 1
    return narrow_bits + lax.axis_size("wide").bit_length() - 1, narrow_bits


def reduce_steps(bits, narrow_bits, plans, chunks, sources, outs, scratch):
    count = len(sources)
    held = scratch[:count]
    arrived = [scratch[count * (1 + s) : count * (2 + s)] for s in range(bits)]
    load_sem, send_sem, recv_sem = scratch[count * (1 + bits) :]
    peers = [partner(b, narrow_bits) for b in range(bits)]
    first = plans[0][0]
    order_of_dims = list(reversed(range(bits)))
    whole = slice(None)

    def within(order, stage, current):
        return tuple(
            peers[b][1] if b in order[:stage] else current if b == order[stage] else whole
            for b in order_of_dims
            if b != first
        )

    def of_source(value):
        return tuple(value if b == first else whole for b in order_of_dims)

    def rows_of(chunk):
        at, row, rows, colour = chunks[chunk]
        return at, plans[colour], (pl.ds(row, rows), whole)

    def send(chunk, stage):
        at, order, part = rows_of(chunk)
        device, mine = peers[order[stage]]
        if stage == 0:
            source = sources[at].at[of_source(1 - mine) + part]
        else:
            source = held[at].at[within(order, stage, 1 - mine) + part]
        return pltpu.make_async_remote_copy(
            src_ref=source,
            dst_ref=arrived[stage][at].at[(whole,) * (bits - 1 - stage) + part],
            send_sem=send_sem.at[chunk, stage],
            recv_sem=recv_sem.at[chunk, stage],
            device_id=device,
            device_id_type=MESH,
        )

    def load(chunk):
        at, order, part = rows_of(chunk)
        return pltpu.make_async_copy(
            sources[at].at[of_source(peers[first][1]) + part],
            held[at].at[(whole,) * (bits - 1) + part],
            load_sem.at[chunk],
        )

    def begin(chunk):
        send(chunk, 0).start()
        load(chunk).start()

    def finish(chunk, stage):
        at, order, part = rows_of(chunk)
        if stage == 0:
            load(chunk).wait()
        send(chunk, stage).wait_recv()
        left = bits - 1 - stage
        keep = within(order, stage, peers[order[stage]][1])
        if left == 0:
            own = held[at][keep + part].astype(float32)
            outs[at][part] = own + arrived[stage][at][part].astype(float32)
            return
        free = [i for i, k in enumerate(keep) if isinstance(k, slice)]

        def add(m, carry):
            which = tuple(m // (1 << (left - 1 - i)) % 2 for i in range(left))
            spot = list(keep)
            for i, f in enumerate(free):
                spot[f] = which[i]
            spot = tuple(spot) + part
            held[at][spot] = held[at][spot] + arrived[stage][at][which + part]
            return carry

        lax.fori_loop(0, 1 << left, add, 0)
        send(chunk, stage + 1).start()

    def drain():
        for chunk in range(len(chunks)):
            for stage in range(bits):
                send(chunk, stage).wait_send()

    return peers, begin, finish, drain


def reduce_kernel(bits, narrow_bits, plans, chunks, count, *refs):
    peers, begin, finish, drain = reduce_steps(
        bits, narrow_bits, plans, chunks, refs[:count], refs[count : 2 * count], refs[2 * count :]
    )
    greet(peers)
    total = len(chunks)
    for chunk in range(min(AHEAD, total)):
        begin(chunk)
    for step in range(total + 2 * bits):
        for stage in reversed(range(bits)):
            chunk = step - 2 * stage
            if 0 <= chunk < total:
                finish(chunk, stage)
                if stage == 0 and chunk + AHEAD < total:
                    begin(chunk + AHEAD)
    drain()


def slot_table(chunks, bits, slots, pace, delay):
    table = [[] for _ in range(slots + 1)]
    done = sorted(
        (chunk * pace + (stage + 1) * delay, -stage, chunk, stage)
        for chunk in range(chunks)
        for stage in range(bits)
    )
    for when, _, chunk, stage in done:
        table[min(int(when), slots)].append((chunk, stage))
    return table


def reduce_plan(parts, pieces):
    bits, narrow_bits = mesh_bits()
    shapes = [part.shape[1:] for part in parts]
    kinds = [part.dtype for part in parts]
    chunks = []
    for at, (shape, cut) in enumerate(zip(shapes, pieces)):
        rows = shape[0] // cut
        for row in range(0, shape[0], rows):
            chunks.append((at, row, rows, len(chunks) % len(ORDERS)))
    later = tuple(range(3, bits))
    plans = tuple(tuple(b for part in order for b in (later if part is None else (part,))) for order in ORDERS)
    sizes = [bits - 1] + [bits - 1 - stage for stage in range(bits)]
    scratch = [
        pltpu.VMEM((2,) * size + shape, kind)
        for size in sizes
        for shape, kind in zip(shapes, kinds)
    ]
    total = len(chunks)
    scratch += [
        pltpu.SemaphoreType.DMA((total,)),
        pltpu.SemaphoreType.DMA((total, bits)),
        pltpu.SemaphoreType.DMA((total, bits)),
    ]
    outs = [jax.ShapeDtypeStruct(shape, float32) for shape in shapes]
    halved = [part.reshape((2,) * bits + shape) for part, shape in zip(parts, shapes)]
    return bits, narrow_bits, plans, tuple(chunks), halved, outs, scratch


def reduce_to_shards(parts, pieces, collective_id):
    bits, narrow_bits, plans, chunks, halved, outs, scratch = reduce_plan(parts, pieces)
    return pl.pallas_call(
        partial(reduce_kernel, bits, narrow_bits, plans, chunks, len(parts)),
        out_shape=outs,
        in_specs=[pl.BlockSpec(memory_space=pl.ANY)] * len(parts),
        out_specs=[pl.BlockSpec(memory_space=pltpu.VMEM)] * len(parts),
        scratch_shapes=scratch,
        compiler_params=pltpu.CompilerParams(
            collective_id=collective_id, has_side_effects=True, vmem_limit_bytes=58 * 2**20
        ),
        cost_estimate=pl.CostEstimate(flops=10**8, bytes_accessed=4 * 10**8, transcendentals=0),
    )(*halved)


def gather_steps(bits, narrow_bits, plans, chunks, sources, outs, scratch):
    own_sem, send_sem, recv_sem = scratch
    peers = [partner(b, narrow_bits) for b in range(bits)]
    dims = list(reversed(range(bits)))

    def place(chunk, stage):
        at, band, bands, col, cols, colour = chunks[chunk]
        done = plans[colour][:stage]
        index = tuple(slice(None) if b in done else peers[b][1] for b in dims)
        return outs[at].at[(pl.ds(band, bands),) + index + (slice(None), pl.ds(col, cols))]

    def own(chunk):
        at, band, bands, col, cols, colour = chunks[chunk]
        return sources[at].at[pl.ds(band, bands), :, pl.ds(col, cols)]

    def send(chunk, stage):
        colour = chunks[chunk][-1]
        target = place(chunk, stage)
        return pltpu.make_async_remote_copy(
            src_ref=target if stage else own(chunk),
            dst_ref=target,
            send_sem=send_sem.at[chunk, stage],
            recv_sem=recv_sem.at[chunk, stage],
            device_id=peers[plans[colour][stage]][0],
            device_id_type=MESH,
        )

    def keep(chunk):
        return pltpu.make_async_copy(own(chunk), place(chunk, 0), own_sem.at[chunk])

    def begin(chunk):
        send(chunk, 0).start()
        keep(chunk).start()

    def finish(chunk, stage):
        if stage == 0:
            keep(chunk).wait()
        send(chunk, stage).wait_recv()
        if stage + 1 < bits:
            send(chunk, stage + 1).start()

    def drain():
        for chunk in range(len(chunks)):
            for stage in range(bits):
                send(chunk, stage).wait_send()

    return peers, begin, finish, drain


def gather_kernel(bits, narrow_bits, plans, chunks, count, *refs):
    peers, begin, finish, drain = gather_steps(
        bits, narrow_bits, plans, chunks, refs[:count], refs[count : 2 * count], refs[2 * count :]
    )
    greet(peers)
    total = len(chunks)
    for chunk in range(total):
        begin(chunk)
    for step in range(total + SKEW * bits):
        for stage in reversed(range(bits)):
            chunk = step - SKEW * stage
            if 0 <= chunk < total:
                finish(chunk, stage)
    drain()


def gather_plan(parts, pieces):
    bits, narrow_bits = mesh_bits()
    chunks = []
    for at, (part, (cut, cut_cols)) in enumerate(zip(parts, pieces)):
        bands, cols = part.shape[0] // cut, part.shape[2] // cut_cols
        for band in range(0, part.shape[0], bands):
            for col in range(0, part.shape[2], cols):
                chunks.append((at, band, bands, col, cols, len(chunks) % 2))
    later = tuple(reversed(range(3, bits)))
    plans = (later + (1, 2, 0), later + (2, 1, 0))
    total = len(chunks)
    outs = [
        jax.ShapeDtypeStruct(part.shape[:1] + (2,) * bits + part.shape[1:], part.dtype)
        for part in parts
    ]
    scratch = [
        pltpu.SemaphoreType.DMA((total,)),
        pltpu.SemaphoreType.DMA((total, bits)),
        pltpu.SemaphoreType.DMA((total, bits)),
    ]
    return bits, narrow_bits, plans, tuple(chunks), outs, scratch


def gather_bands(parts, pieces, collective_id):
    bits, narrow_bits, plans, chunks, outs, scratch = gather_plan(parts, pieces)
    results = pl.pallas_call(
        partial(gather_kernel, bits, narrow_bits, plans, chunks, len(parts)),
        out_shape=outs,
        in_specs=[pl.BlockSpec(memory_space=pl.ANY)] * len(parts),
        out_specs=[pl.BlockSpec(memory_space=pl.ANY)] * len(parts),
        scratch_shapes=scratch,
        compiler_params=pltpu.CompilerParams(collective_id=collective_id, has_side_effects=True),
        cost_estimate=pl.CostEstimate(flops=0, bytes_accessed=10**8, transcendentals=0),
    )(*parts)
    return [
        result.reshape(part.shape[:1] + (1 << bits,) + part.shape[1:])
        for result, part in zip(results, parts)
    ]


def group_peers():
    count = lax.axis_size("narrow")
    me = lax.axis_index("narrow")
    return me, [({"narrow": lax.rem(me + d, count)}, lax.rem(me + d, count)) for d in range(count)]


def rows_at(place, rows):
    return pl.ds(pl.multiple_of(place * rows, rows), rows)


def attend_kernel(safe, chunk, halves, plan, slots, length_ref, *refs):
    count = plan[4]
    packed, sources = refs[:halves], refs[halves : halves + count]
    refs = refs[halves + count :]
    scenes_out, merged, mixed_out, log_ref = refs[:4]
    scene_ref, o_ref, vt_ref, s_ref, near_sem, in_sem, back_sem, out_sem = refs[4 + count : 12 + count]
    others, begin, finish, drain = gather_steps(
        *plan[:4], sources, refs[4 : 4 + count], refs[12 + count :]
    )
    seq_len = scene_ref.shape[1]
    me, peers = group_peers()
    devices = len(peers)
    tok_rows = seq_len // devices
    length = length_ref[0]
    half, step = pl.program_id(0), pl.program_id(1)
    last = pl.num_programs(1) - 1
    own = rows_at(me, tok_rows)

    def bring(h, d):
        device, place = peers[d]
        if d == 0:
            return pltpu.make_async_copy(packed[h].at[me], scene_ref.at[h, own], in_sem.at[h, 0])
        return pltpu.make_async_remote_copy(
            src_ref=packed[h].at[place],
            dst_ref=scene_ref.at[h, own],
            send_sem=near_sem.at[h, d],
            recv_sem=in_sem.at[h, d],
            device_id=device,
            device_id_type=MESH,
        )

    def give(h, d, at, to, sender):
        column = pl.ds(pl.multiple_of((sender * halves + h) * PAIR, PAIR), PAIR)
        target = merged.at[:, column]
        source = o_ref.at[h, rows_at(to, tok_rows)]
        if d == 0:
            return pltpu.make_async_copy(source, target, out_sem.at[h, 0])
        return pltpu.make_async_remote_copy(
            src_ref=source,
            dst_ref=target,
            send_sem=back_sem.at[h, d],
            recv_sem=out_sem.at[h, d],
            device_id={"narrow": to},
            device_id_type=MESH,
        )

    def save_scene(h):
        return pltpu.make_async_copy(scene_ref.at[h], scenes_out.at[h], near_sem.at[h, 0])

    def save_mixed(h):
        return pltpu.make_async_copy(o_ref.at[h], mixed_out.at[h], back_sem.at[h, 0])

    @pl.when((half == 0) & (step == 0))
    def _():
        greet(peers[1:] + others[plan[1] :])
        for d in range(devices):
            bring(0, d).start()
        for which in range(len(plan[3])):
            begin(which)

    for h in range(halves):

        @pl.when((half == h) & (step == 0))
        def _(h=h):
            for d in range(devices):
                if d:
                    bring(h, d).wait_recv()
                else:
                    bring(h, d).wait()
            if h + 1 < halves:
                for d in range(devices):
                    bring(h + 1, d).start()
            save_scene(h).start()
            vt_ref[...] = scene_ref[h, :, 2 * PAIR :].T

    points = 2 * seq_len // chunk

    def move_at(point):
        for h in range(halves):
            for s in range(devices):
                todo = slots[(h * devices + s) * 2 * points + point]
                if todo:

                    @pl.when((half == h) & (step == s))
                    def _(todo=todo):
                        for which, stage in todo:
                            finish(which, stage)

    to = lax.rem(me + 1 + step, devices)
    here = rows_at(to, tok_rows)
    outs = []
    for head in range(2):
        queries = one_head(scene_ref[half, here, :PAIR], head) * bfloat16(HEAD**-0.5)
        topmost = None
        for at in range(0, seq_len, chunk):
            move_at(head * points + at // chunk)
            scores = lax.dot_general(
                scene_ref[half, at : at + chunk, PAIR : 2 * PAIR],
                queries,
                NT,
                preferred_element_type=float32,
            )
            scores = hide(scores, at, safe, length)
            s_ref[head, at : at + chunk, :] = scores
            top = jnp.max(scores, 0, keepdims=True)
            topmost = top if topmost is None else jnp.maximum(topmost, top)
        totals = jnp.zeros_like(topmost)
        mixed = jnp.zeros((HEAD, tok_rows), float32)
        for at in range(0, seq_len, chunk):
            move_at(head * points + points // 2 + at // chunk)
            expo = jnp.exp(s_ref[head, at : at + chunk, :] - topmost)
            totals += jnp.sum(expo, 0, keepdims=True)
            mixed += jnp.dot(
                vt_ref[head * HEAD : (head + 1) * HEAD, at : at + chunk],
                expo.astype(bfloat16),
                preferred_element_type=float32,
            )
        outs.append(mixed * (1.0 / totals))
        log_ref[half, head : head + 1, here] = topmost + jnp.log(totals)
    o_ref[half, here, :] = jnp.concatenate(outs, 0).T.astype(bfloat16)

    for h in range(halves):
        for s in range(devices):

            @pl.when((half == h) & (step == s))
            def _(h=h, s=s):
                d = (s + 1) % devices
                give(h, d, s, lax.rem(me + d, devices), me).start()
                if s == devices - 1:
                    save_mixed(h).start()

    @pl.when((half == halves - 1) & (step == last))
    def _():
        for which, stage in slots[-1]:
            finish(which, stage)
        drain()
        for h in range(halves):
            for d in range(devices):
                if d:
                    bring(h, d).wait_send()
                    sender = lax.rem(me + devices - d, devices)
                    arriving = give(h, d, d, lax.rem(me + d, devices), sender)
                    arriving.wait_recv()
                    arriving.wait_send()
                else:
                    give(h, 0, 0, me, me).wait()
            save_scene(h).wait()
            save_mixed(h).wait()


def attend(lengths, packed, safe, parts, pieces, collective_id, chunk=512):
    devices, tok_rows, _ = packed[0].shape
    halves, seq_len = len(packed), devices * tok_rows
    width = devices * halves * PAIR
    anywhere = pl.BlockSpec(memory_space=pl.ANY)
    bits, narrow_bits, plans, chunks, outs, scratch = gather_plan(parts, pieces)
    slots = slot_table(
        len(chunks), bits, halves * devices * 4 * (seq_len // chunk), GATHER_PACE, GATHER_DELAY
    )
    plan = (bits, narrow_bits, plans, chunks, len(parts))
    results = pl.pallas_call(
        partial(attend_kernel, safe, chunk, halves, plan, slots),
        grid=(halves, devices),
        in_specs=[pl.BlockSpec(memory_space=pltpu.SMEM)] + [anywhere] * (halves + len(parts)),
        out_specs=[anywhere] * 3
        + [pl.BlockSpec((halves, 2, seq_len), lambda p, i: (0, 0, 0))]
        + [anywhere] * len(parts),
        out_shape=[
            jax.ShapeDtypeStruct((halves, seq_len, 3 * PAIR), bfloat16),
            jax.ShapeDtypeStruct((tok_rows, width), bfloat16),
            jax.ShapeDtypeStruct((halves, seq_len, PAIR), bfloat16),
            jax.ShapeDtypeStruct((halves, 2, seq_len), float32),
        ]
        + outs,
        scratch_shapes=[
            pltpu.VMEM((halves, seq_len, 3 * PAIR), bfloat16),
            pltpu.VMEM((halves, seq_len, PAIR), bfloat16),
            pltpu.VMEM((PAIR, seq_len), bfloat16),
            pltpu.VMEM((2, seq_len, tok_rows), float32),
        ]
        + [pltpu.SemaphoreType.DMA((halves, devices))] * 4
        + scratch,
        compiler_params=pltpu.CompilerParams(
            collective_id=collective_id, has_side_effects=True, vmem_limit_bytes=VMEM_LIMIT
        ),
        cost_estimate=pl.CostEstimate(
            flops=4 * halves * 2 * 4 * seq_len * seq_len * HEAD,
            bytes_accessed=16 * seq_len * PAIR * halves,
            transcendentals=0,
        ),
    )(lengths, *packed, *parts)
    gathered = [
        result.reshape(part.shape[0], 1 << bits, *part.shape[1:])
        for result, part in zip(results[4:], parts)
    ]
    return list(results[:4]) + gathered


def attend_backward_kernel(
    safe, chunk, halves, plan, slots, length_ref, scene_ref, o_ref, log_ref, d_merged, *refs
):
    count = plan[4]
    sources, packed_out, outs = refs[:count], refs[count], refs[count + 1 : 2 * count + 1]
    do_ref, stage_ref, kt_ref, dk_sum, dv_sum = refs[2 * count + 1 : 2 * count + 6]
    near_sem, in_sem, q_send, q_recv, kv_send, kv_recv = refs[2 * count + 6 : 2 * count + 12]
    others, begin, finish, drain = reduce_steps(*plan[:4], sources, outs, refs[2 * count + 12 :])
    total = len(plan[3])
    me, peers = group_peers()
    devices = len(peers)
    seq_len = scene_ref.shape[1]
    tok_rows = seq_len // devices
    length = length_ref[0]
    half, step = pl.program_id(0), pl.program_id(1)
    own = rows_at(me, tok_rows)
    chunks = seq_len // chunk

    def move(which, stage):
        finish(which, stage)
        if stage == 0 and which + AHEAD < total:
            begin(which + AHEAD)

    def move_at(head, part):
        for h in range(halves):
            for s in range(devices):
                todo = slots[((h * devices + s) * 2 + head) * chunks + part]
                if todo:

                    @pl.when((half == h) & (step == s))
                    def _(todo=todo):
                        for which, stage in todo:
                            move(which, stage)

    def bring(h, d):
        device, place = peers[d]
        column = pl.ds(pl.multiple_of((place * halves + h) * PAIR, PAIR), PAIR)
        source, target = d_merged.at[:, column], do_ref.at[h, own]
        if d == 0:
            return pltpu.make_async_copy(source, target, in_sem.at[h, 0])
        return pltpu.make_async_remote_copy(
            src_ref=source,
            dst_ref=target,
            send_sem=near_sem.at[h, d],
            recv_sem=in_sem.at[h, d],
            device_id=device,
            device_id_type=MESH,
        )

    def give(h, d, columns, send_sem, recv_sem, sender):
        device, place = peers[d]
        source = stage_ref.at[h, rows_at(place, tok_rows), columns]
        target = packed_out.at[h, sender, :, columns]
        if d == 0:
            return pltpu.make_async_copy(source, target, recv_sem.at[h, 0])
        return pltpu.make_async_remote_copy(
            src_ref=source,
            dst_ref=target,
            send_sem=send_sem.at[h, d],
            recv_sem=recv_sem.at[h, d],
            device_id=device,
            device_id_type=MESH,
        )

    q_columns, kv_columns = pl.ds(0, PAIR), pl.ds(PAIR, 2 * PAIR)

    @pl.when((half == 0) & (step == 0))
    def _():
        narrow_bits = plan[1]
        greet(peers[1:] + others[narrow_bits:])
        for h in range(halves):
            for d in range(devices):
                bring(h, d).start()
        for which in range(min(AHEAD, total)):
            begin(which)

    for h in range(halves):

        @pl.when((half == h) & (step == 0))
        def _(h=h):
            kt_ref[...] = scene_ref[0, :, PAIR : 2 * PAIR].T
            dk_sum[...] = jnp.zeros_like(dk_sum)
            dv_sum[...] = jnp.zeros_like(dv_sum)
            for d in range(devices):
                if d:
                    bring(h, d).wait_recv()
                else:
                    bring(h, d).wait()

    here = rows_at(lax.rem(me + 1 + step, devices), tok_rows)
    products = (o_ref[0, here, :].astype(float32) * do_ref[half, here, :].astype(float32)).T
    turned = []
    for head in range(2):
        lanes = slice(head * HEAD, (head + 1) * HEAD)
        queries = one_head(scene_ref[0, here, :PAIR], head) * bfloat16(HEAD**-0.5)
        d_mixed = one_head(do_ref[half, here, :], head)
        inner = jnp.sum(products[lanes, :], 0, keepdims=True)
        log_total = log_ref[0, head : head + 1, here]
        d_queries = jnp.zeros((HEAD, tok_rows), float32)
        for index in range(chunks):
            move_at(head, index)
            at = index * chunk
            part = slice(at, at + chunk)
            scores = lax.dot_general(
                scene_ref[0, part, PAIR : 2 * PAIR], queries, NT, preferred_element_type=float32
            )
            probs = jnp.exp(hide(scores, at, safe, length) - log_total)
            d_probs = lax.dot_general(
                scene_ref[0, part, 2 * PAIR :], d_mixed, NT, preferred_element_type=float32
            )
            dv_sum[part, :] += jnp.dot(
                probs.astype(bfloat16), d_mixed, preferred_element_type=float32
            )
            d_scores = (probs * (d_probs - inner)).astype(bfloat16)
            dk_sum[part, :] += jnp.dot(d_scores, queries, preferred_element_type=float32)
            d_queries += jnp.dot(kt_ref[lanes, part], d_scores, preferred_element_type=float32)
        turned.append(d_queries * HEAD**-0.5)
    stage_ref[half, here, :PAIR] = jnp.concatenate(turned, 0).T.astype(bfloat16)

    for h in range(halves):
        for s in range(devices):

            @pl.when((half == h) & (step == s))
            def _(h=h, s=s):
                give(h, (s + 1) % devices, q_columns, q_send, q_recv, me).start()
                if s == devices - 1:
                    stage_ref[h, :, PAIR : 2 * PAIR] = dk_sum[...].astype(bfloat16)
                    stage_ref[h, :, 2 * PAIR :] = dv_sum[...].astype(bfloat16)
                    for d in range(devices):
                        give(h, d, kv_columns, kv_send, kv_recv, me).start()

    @pl.when((half == halves - 1) & (step == devices - 1))
    def _():
        for which, stage in slots[-1]:
            move(which, stage)
        drain()
        for h in range(halves):
            for d in range(devices):
                for columns, send_sem, recv_sem in (
                    (q_columns, q_send, q_recv),
                    (kv_columns, kv_send, kv_recv),
                ):
                    sender = lax.rem(me + devices - d, devices)
                    copy = give(h, d, columns, send_sem, recv_sem, sender)
                    if d:
                        copy.wait_recv()
                        copy.wait_send()
                    else:
                        copy.wait()
                if d:
                    bring(h, d).wait_send()


def attend_backward(
    lengths, scenes, mixed, d_merged, log_totals, safe, parts, pieces, collective_id, chunk=512
):
    halves, seq_len, _ = scenes.shape
    devices = lax.axis_size("narrow")
    tok_rows = seq_len // devices
    bits, narrow_bits, plans, chunks, halved, outs, scratch = reduce_plan(parts, pieces)
    slots = slot_table(
        len(chunks), bits, halves * devices * 2 * (seq_len // chunk), PACE, DELAY
    )
    anywhere = pl.BlockSpec(memory_space=pl.ANY)

    def of_half(array):
        return pl.BlockSpec((1,) + array.shape[1:], lambda p, i: (p, 0, 0))

    return pl.pallas_call(
        partial(
            attend_backward_kernel,
            safe,
            chunk,
            halves,
            (bits, narrow_bits, plans, chunks, len(parts)),
            slots,
        ),
        grid=(halves, devices),
        in_specs=[
            pl.BlockSpec(memory_space=pltpu.SMEM),
            of_half(scenes),
            of_half(mixed),
            of_half(log_totals),
            anywhere,
        ]
        + [anywhere] * len(parts),
        out_specs=[anywhere] + [pl.BlockSpec(out.shape, lambda p, i: (0, 0)) for out in outs],
        out_shape=[jax.ShapeDtypeStruct((halves, devices, tok_rows, 3 * PAIR), bfloat16)] + outs,
        scratch_shapes=[
            pltpu.VMEM((halves, seq_len, PAIR), bfloat16),
            pltpu.VMEM((halves, seq_len, 3 * PAIR), bfloat16),
            pltpu.VMEM((PAIR, seq_len), bfloat16),
            pltpu.VMEM((seq_len, PAIR), float32),
            pltpu.VMEM((seq_len, PAIR), float32),
        ]
        + [pltpu.SemaphoreType.DMA((halves, devices))] * 6
        + scratch,
        compiler_params=pltpu.CompilerParams(
            collective_id=collective_id, has_side_effects=True, vmem_limit_bytes=60 * 2**20
        ),
        cost_estimate=pl.CostEstimate(
            flops=4 * halves * 2 * 10 * seq_len * seq_len * HEAD,
            bytes_accessed=32 * seq_len * PAIR,
            transcendentals=0,
        ),
    )(lengths, scenes, mixed, log_totals, d_merged, *halved)


def total_kernel(bits, narrow_bits, own_ref, sum_ref, arrived, send_sem, recv_sem):
    peers = [partner(b, narrow_bits) for b in range(bits)]
    greet(peers)
    sum_ref[...] = own_ref[...]
    for stage in range(bits):
        copy = pltpu.make_async_remote_copy(
            src_ref=sum_ref,
            dst_ref=arrived.at[stage],
            send_sem=send_sem.at[stage],
            recv_sem=recv_sem.at[stage],
            device_id=peers[stage][0],
            device_id_type=MESH,
        )
        copy.start()
        copy.wait()
        sum_ref[...] = sum_ref[...] + arrived[stage]


def total_of(value, collective_id):
    bits, narrow_bits = mesh_bits()
    tile = (8, 128)
    return pl.pallas_call(
        partial(total_kernel, bits, narrow_bits),
        out_shape=jax.ShapeDtypeStruct(tile, float32),
        in_specs=[pl.BlockSpec(memory_space=pltpu.VMEM)],
        out_specs=pl.BlockSpec(memory_space=pltpu.VMEM),
        scratch_shapes=[
            pltpu.VMEM((bits,) + tile, float32),
            pltpu.SemaphoreType.DMA((bits,)),
            pltpu.SemaphoreType.DMA((bits,)),
        ],
        compiler_params=pltpu.CompilerParams(collective_id=collective_id, has_side_effects=True),
    )(jnp.broadcast_to(value, tile))[0, 0]


def weight_grad_kernel(columns, band_rows, left_ref, *refs):
    right_refs, out_ref = refs[:-1], refs[-1]
    left = left_ref[...].T
    for at in range(0, len(columns), 2):
        blocks = []
        for spots in columns[at : at + 2]:
            right = [right_refs[i][g, :, start : start + size] for i, g, start, size in spots]
            right = right[0] if len(right) == 1 else jnp.concatenate(right, 1)
            block = jnp.dot(left, right, preferred_element_type=float32)
            blocks.append(block.astype(bfloat16).reshape(-1, band_rows, BLOCK))
        out_ref[:, at * band_rows : (at + 2) * band_rows, :] = jnp.concatenate(blocks, 1)


def weight_grad(left, rights, columns, device_count):
    tok_rows, height = left.shape
    band_rows = BLOCK // device_count
    bands, wide = height // BLOCK, len(columns)
    if band_rows % 8:
        right = [rights[i][g, :, start : start + n] for spots in columns for i, g, start, n in spots]
        right = jnp.concatenate(right, 1)
        product = jnp.einsum("td,te->de", left, right, preferred_element_type=float32)
        product = product.astype(bfloat16).reshape(bands, device_count, band_rows, wide, BLOCK)
        return product.transpose(1, 0, 3, 2, 4).reshape(device_count, -1, BLOCK)
    return pl.pallas_call(
        partial(weight_grad_kernel, columns, band_rows),
        grid=(bands,),
        in_specs=[
            pl.BlockSpec((tok_rows, BLOCK), lambda i: (0, i)),
        ]
        + [pl.BlockSpec(right.shape, lambda i: (0, 0, 0)) for right in rights],
        out_specs=pl.BlockSpec((device_count, wide * band_rows, BLOCK), lambda i: (0, i, 0)),
        out_shape=jax.ShapeDtypeStruct((device_count, bands * wide * band_rows, BLOCK), bfloat16),
        compiler_params=pltpu.CompilerParams(vmem_limit_bytes=VMEM_LIMIT),
        cost_estimate=pl.CostEstimate(
            flops=2 * tok_rows * bands * wide * BLOCK**2,
            bytes_accessed=2 * (tok_rows * (height + wide * BLOCK) + bands * wide * BLOCK**2),
            transcendentals=0,
        ),
    )(left, *rights)


def body(
    tokens,
    cotangent,
    lengths,
    owners,
    w_qkv,
    w_out,
    w_up,
    w_down,
    norm_gains,
    gain_first,
    gain_second,
    moment_first,
    moment_second,
    left_stat,
    right_stat,
    left_basis,
    right_basis,
):
    tok_rows, width = tokens.shape
    narrow_count = lax.axis_size("narrow")
    device_count = lax.axis_size("wide") * narrow_count
    seq_len = tok_rows * narrow_count
    cap_slots = moment_first.shape[0]
    masters = (w_qkv, w_out, w_up, w_down)
    lowered = tuple((layout.astype(jnp.bfloat16) for layout in masters)) + (
        norm_gains.astype(jnp.bfloat16),
    )
    share = norm_gains.shape[1]
    gains_low = jnp.pad(lowered[4], ((0, 6), (0, 128 - share)))[None]
    w_attn, gain_pair = gather_bands((lowered[0], gains_low), ((4, 2), (1, 1)), 3)
    w_attn = w_attn.reshape(width, 3 * width)
    gain_pair = gain_pair[0, :, :2, :share].transpose(1, 0, 2).reshape(2, width)
    gain_pair = gain_pair.astype(jnp.float32)
    w_proj, w_back = (
        gathered.reshape(-1, width)
        for gathered in lax.all_gather(lowered[1:4:2], ("wide", "narrow"), axis=1, tiled=True)
    )
    inputs = tokens.astype(jnp.float32)
    normed_one, inverse_one = normalize(inputs)
    act_one = (normed_one * gain_pair[0]).astype(jnp.bfloat16)
    head_width = width // narrow_count
    safe = seq_len - tok_rows
    packed = project(act_one, w_attn, narrow_count)
    halves = len(packed)
    scenes, merged, mixed, log_totals, w_hidden = attend(
        lengths, packed, safe, (lowered[2],), ((4, 2),), 4
    )
    w_hidden = w_hidden.reshape(width, FF)
    middle = inputs + jnp.dot(merged, w_proj, preferred_element_type=jnp.float32)
    normed_two, inverse_two = normalize(middle)
    act_two = (normed_two * gain_pair[1]).astype(jnp.bfloat16)
    hidden = jnp.dot(act_two, w_hidden, preferred_element_type=jnp.float32)
    active = jax.nn.gelu(hidden, approximate=True).astype(jnp.bfloat16)
    block_out = (middle + jnp.dot(active, w_back, preferred_element_type=jnp.float32)).astype(
        jnp.bfloat16
    )
    plain = lambda size: tuple(((0, 0, start, BLOCK),) for start in range(0, size, BLOCK))
    d_back = weight_grad(active, [cotangent[None]], plain(width), device_count)
    d_active = jnp.einsum("td,fd->tf", cotangent, w_back, preferred_element_type=jnp.float32)
    _, gelu_pull = jax.vjp(partial(jax.nn.gelu, approximate=True), hidden)
    d_hidden = gelu_pull(d_active)[0].astype(jnp.bfloat16)
    d_w_hidden = weight_grad(act_two, [d_hidden[None]], plain(FF), device_count)
    d_act_two = jnp.einsum("tf,df->td", d_hidden, w_hidden, preferred_element_type=jnp.float32)
    d_norm_two, d_gain_two = norm_backward(d_act_two, normed_two, inverse_two, gain_pair[1])
    d_middle = cotangent.astype(jnp.float32) + d_norm_two
    d_branch = d_middle.astype(jnp.bfloat16)
    d_proj = weight_grad(merged, [d_branch[None]], plain(width), device_count)
    d_merged = jnp.einsum("te,de->td", d_branch, w_proj, preferred_element_type=jnp.float32).astype(
        jnp.bfloat16
    )
    ready = (d_w_hidden, d_back, d_proj)
    d_packed, hidden_sum, back_sum, proj_sum = attend_backward(
        lengths, scenes, mixed, d_merged, log_totals, safe, ready, (8, 8, 2), 5
    )
    d_packed = [d_packed[half] for half in range(halves)]
    grouped = tuple(
        tuple((half, group, third * PAIR, PAIR) for half in range(halves))
        for third in range(3)
        for group in range(narrow_count)
    )
    d_attn = weight_grad(act_one, d_packed, grouped, device_count)
    d_act_one = project_back(d_packed, w_attn)
    d_norm_one, d_gain_one = norm_backward(d_act_one, normed_one, inverse_one, gain_pair[0])
    grad_tokens = (d_middle + d_norm_one).astype(jnp.bfloat16)
    gain_parts = jnp.stack([d_gain_one, d_gain_two]).reshape(2, device_count, share)
    gain_parts = jnp.pad(gain_parts.transpose(1, 0, 2), ((0, 0), (0, 6), (0, 128 - share)))
    attn_sum, gain_grad = reduce_to_shards((d_attn, gain_parts), (6, 1), 1)
    grad_shards = (attn_sum, proj_sum, hidden_sum, back_sum)
    gain_grad = gain_grad[:2, :share]
    band_rows = BLOCK // device_count
    local_squares = jnp.sum(gain_grad * gain_grad) + sum(
        (jnp.sum(shard * shard) for shard in grad_shards)
    )
    pieces = jnp.concatenate(grad_shards, 0).reshape(-1, band_rows, BLOCK)
    block_count = pieces.shape[0]
    order = lax.iota(jnp.int32, block_count)
    earlier = (owners[None, :] == owners[:, None]) & (order[None, :] < order[:, None])
    slots = owners * cap_slots + jnp.sum(earlier.astype(jnp.int32), 1)
    routing = (slots[None, :] == lax.iota(jnp.int32, device_count * cap_slots)[:, None]).astype(
        jnp.float32
    )
    routing = routing.reshape(device_count, cap_slots, block_count)
    grad_norm = jnp.sqrt(total_of(local_squares, 2))
    factor = jnp.minimum(1.0, clip_bound / grad_norm)
    arrived = lax.all_to_all(
        jnp.einsum("okb,bxy->koxy", routing, pieces, precision=highest).astype(jnp.bfloat16),
        ("wide", "narrow"),
        split_axis=1,
        concat_axis=1,
        tiled=True,
    )
    slot_grads = arrived.reshape(cap_slots, BLOCK, BLOCK)
    restored, first_new, second_new, left_new, right_new, gram, turn = soap_update(
        factor, slot_grads, moment_first, moment_second, left_stat, right_stat, left_basis, right_basis
    )
    square = (-1, BLOCK, BLOCK)
    bases = renew_bases(gram.reshape(square), turn.reshape(square))
    bases = bases.reshape(cap_slots, 2, BLOCK, BLOCK)
    left_turn, right_turn = bases[:, 0], bases[:, 1]
    returned = lax.all_to_all(
        shortened(restored.reshape(cap_slots, device_count, -1, BLOCK)),
        ("wide", "narrow"),
        split_axis=1,
        concat_axis=1,
        tiled=True,
    )
    back_pieces = jnp.einsum("okb,koxy->bxy", routing, returned, precision=highest)
    fan_list = (2 * width, max(1, width * 16 // seq_len), width, FF)
    updated = []
    offset = 0
    for master, fan_in in zip(masters, fan_list):
        band_count, band_rows, col_count = master.shape
        piece_count = band_count * (col_count // BLOCK)
        direction = from_pieces(back_pieces[offset : offset + piece_count], band_count, col_count)
        updated.append(master - fan_in ** (-0.5) * (direction + weight_decay * master))
        offset += piece_count
    clipped = gain_grad * factor
    gain_one_new = decay_rate * gain_first + (1.0 - decay_rate) * clipped
    gain_two_new = decay_rate * gain_second + (1.0 - decay_rate) * clipped * clipped
    correct = 1.0 - decay_rate**STEP
    gain_values = norm_gains - gain_rate * (gain_one_new / correct) / (
        jnp.sqrt(gain_two_new / correct) + eps_adam
    )
    return (
        block_out,
        grad_tokens,
        grad_norm,
        updated[0],
        updated[1],
        updated[2],
        updated[3],
        gain_values,
        gain_one_new,
        gain_two_new,
        first_new,
        second_new,
        left_new,
        right_new,
        left_turn,
        right_turn,
    )


def solution(mesh):
    in_specs = (
        P(("wide", "narrow"), None),
        P(("wide", "narrow"), None),
        P("wide"),
        P(),
        P(None, ("wide", "narrow"), None),
        P(None, ("wide", "narrow"), None),
        P(None, ("wide", "narrow"), None),
        P(None, ("wide", "narrow"), None),
        P(None, ("wide", "narrow")),
        P(None, ("wide", "narrow")),
        P(None, ("wide", "narrow")),
        P(("wide", "narrow"), None, None),
        P(("wide", "narrow"), None, None),
        P(("wide", "narrow"), None, None),
        P(("wide", "narrow"), None, None),
        P(("wide", "narrow"), None, None),
        P(("wide", "narrow"), None, None),
    )
    out_specs = (
        P(("wide", "narrow"), None),
        P(("wide", "narrow"), None),
        P(),
        P(None, ("wide", "narrow"), None),
        P(None, ("wide", "narrow"), None),
        P(None, ("wide", "narrow"), None),
        P(None, ("wide", "narrow"), None),
        P(None, ("wide", "narrow")),
        P(None, ("wide", "narrow")),
        P(None, ("wide", "narrow")),
        P(("wide", "narrow"), None, None),
        P(("wide", "narrow"), None, None),
        P(("wide", "narrow"), None, None),
        P(("wide", "narrow"), None, None),
        P(("wide", "narrow"), None, None),
        P(("wide", "narrow"), None, None),
    )
    return jax.shard_map(body, mesh=mesh, in_specs=in_specs, out_specs=out_specs, check_vma=False)
```

```python
from functools import partial

import jax
import jax.numpy as jnp
from jax import lax
from jax.experimental import pallas as pl
from jax.experimental.pallas import tpu as pltpu
from jax.sharding import PartitionSpec as P

FF = 4096
HEADS = 16
HEAD = 64
BLOCK = 256
STEP = 10


eps_norm = 1e-05
eps_adam = 1e-08
decay_rate = 0.5
clip_bound = 1.0
weight_decay = 0.01
gain_rate = 1.0
neg_large = -1e30
highest = lax.Precision.HIGHEST
float32 = jnp.float32
bfloat16 = jnp.bfloat16
PAIR = 2 * HEAD
NT = (((1,), (1,)), ((), ()))
TN = (((0,), (0,)), ((), ()))
MESH = pl.DeviceIdType.MESH
VMEM_LIMIT = 48 * 2**20
AHEAD = 8
SKEW = 3
ORDERS = ((0, 2, 1, None), (0, 1, 2, None), (0, 2, None, 1))
PACE = 3.7
DELAY = 12.0
GATHER_PACE = 6.0
GATHER_DELAY = 30.0
GELU = 0.7978845608
CUBIC = 0.044715


def shortened(shard):
    return jax.tree.map(lambda a: a.astype(jnp.bfloat16) if a.dtype == jnp.float32 else a, shard)


def normalize(values):
    center = values - jnp.mean(values, -1, keepdims=True)
    inverse = lax.rsqrt(jnp.mean(center * center, -1, keepdims=True) + eps_norm)
    return (center * inverse, inverse)


def norm_backward(d_result, normed, inverse, gain):
    scaled = d_result * gain
    d_gain = jnp.sum(d_result * normed, 0)
    d_input = inverse * (
        scaled
        - jnp.mean(scaled, -1, keepdims=True)
        - normed * jnp.mean(scaled * normed, -1, keepdims=True)
    )
    return (d_input, d_gain)


def one_head(matrix, head):
    lane = lax.broadcasted_iota(jnp.int32, matrix.shape, 1)
    return jnp.where(lane // HEAD == head, matrix, jnp.zeros_like(matrix))


def hide(scores, start, safe, length):
    if start + scores.shape[0] <= safe:
        return scores
    position = start + lax.broadcasted_iota(jnp.int32, scores.shape, 0)
    return jnp.where(position < length, scores, neg_large)


def project_kernel(acts_ref, wq_ref, wk_ref, wv_ref, *out_refs):
    thirds = (wq_ref, wk_ref, wv_ref)
    halves = len(out_refs)
    weights = jnp.concatenate(
        [third[:, h * PAIR : (h + 1) * PAIR] for h in range(halves) for third in thirds], 1
    )
    result = jnp.dot(acts_ref[...], weights, preferred_element_type=float32).astype(bfloat16)
    for h, out_ref in enumerate(out_refs):
        out_ref[0] = result[:, h * 3 * PAIR : (h + 1) * 3 * PAIR]


def project(acts, weights, groups):
    tok_rows, width = acts.shape
    head_width = width // groups
    halves = head_width // PAIR

    def third(k):
        return pl.BlockSpec((width, head_width), lambda g: (0, k * groups + g))

    return pl.pallas_call(
        project_kernel,
        grid=(groups,),
        in_specs=[pl.BlockSpec((tok_rows, width), lambda g: (0, 0)), third(0), third(1), third(2)],
        out_specs=[pl.BlockSpec((1, tok_rows, 3 * PAIR), lambda g: (g, 0, 0))] * halves,
        out_shape=[jax.ShapeDtypeStruct((groups, tok_rows, 3 * PAIR), bfloat16)] * halves,
        compiler_params=pltpu.CompilerParams(vmem_limit_bytes=VMEM_LIMIT),
        cost_estimate=pl.CostEstimate(
            flops=6 * tok_rows * width**2, bytes_accessed=6 * width**2 + 8 * tok_rows * width,
            transcendentals=0,
        ),
    )(acts, weights, weights, weights)


def project_back_kernel(halves, *refs):
    grads, (wq_ref, wk_ref, wv_ref, out_ref) = refs[:halves], refs[halves:]
    thirds = (wq_ref, wk_ref, wv_ref)
    weights = jnp.concatenate(
        [third[:, h * PAIR : (h + 1) * PAIR] for h in range(halves) for third in thirds], 1
    )
    rows = jnp.concatenate([grad[0] for grad in grads], 1)
    result = lax.dot_general(rows, weights, NT, preferred_element_type=float32)

    @pl.when(pl.program_id(0) == 0)
    def _():
        out_ref[...] = result

    @pl.when(pl.program_id(0) > 0)
    def _():
        out_ref[...] += result


def project_back(grads, weights):
    groups, tok_rows, _ = grads[0].shape
    width = weights.shape[0]
    head_width = width // groups

    def third(k):
        return pl.BlockSpec((width, head_width), lambda g: (0, k * groups + g))

    return pl.pallas_call(
        partial(project_back_kernel, len(grads)),
        grid=(groups,),
        in_specs=[pl.BlockSpec((1, tok_rows, 3 * PAIR), lambda g: (g, 0, 0))] * len(grads)
        + [third(0), third(1), third(2)],
        out_specs=pl.BlockSpec((tok_rows, width), lambda g: (0, 0)),
        out_shape=jax.ShapeDtypeStruct((tok_rows, width), float32),
        compiler_params=pltpu.CompilerParams(vmem_limit_bytes=VMEM_LIMIT),
        cost_estimate=pl.CostEstimate(
            flops=6 * tok_rows * width**2, bytes_accessed=6 * width**2 + 10 * tok_rows * width,
            transcendentals=0,
        ),
    )(*grads, weights, weights, weights)


def exact(left, right, dims=(((1,), (0,)), ((), ()))):
    return lax.dot_general(left, right, dims, precision=highest, preferred_element_type=float32)


def soap_kernel(
    factor_ref, g_ref, first_ref, second_ref, ls_ref, rs_ref, lb_ref, rb_ref,
    back_ref, first_out, second_out, ls_out, rs_out, gram_ref, turn_ref,
):
    gradient = factor_ref[0, 0] * g_ref[0].astype(float32)
    left_base, right_base = lb_ref[0], rb_ref[0]
    left_new = decay_rate * ls_ref[0] + (1.0 - decay_rate) * exact(gradient, gradient, NT)
    right_new = decay_rate * rs_ref[0] + (1.0 - decay_rate) * exact(gradient, gradient, TN)
    ls_out[0] = left_new
    rs_out[0] = right_new
    turned = exact(left_base, exact(gradient, right_base), TN)
    first_new = decay_rate * first_ref[0] + (1.0 - decay_rate) * turned
    second_new = decay_rate * second_ref[0] + (1.0 - decay_rate) * turned * turned
    first_out[0] = first_new
    second_out[0] = second_new
    correct = 1.0 - decay_rate**STEP
    direction = first_new / correct / (jnp.sqrt(second_new / correct) + eps_adam)
    back_ref[0] = exact(left_base, exact(direction, right_base, NT)).astype(back_ref.dtype)
    for side, stat, base in ((0, left_new, left_base), (1, right_new, right_base)):
        turn = exact(stat, base).T
        turn_ref[0, side] = turn
        gram_ref[0, side] = exact(turn, turn, NT)


def soap_update(factor, gradient, first_old, second_old, left_old, right_old, left_base, right_base):
    slots, order, _ = gradient.shape
    one = pl.BlockSpec((1, order, order), lambda s: (s, 0, 0))
    two = pl.BlockSpec((1, 2, order, order), lambda s: (s, 0, 0, 0))
    single = jax.ShapeDtypeStruct((slots, order, order), float32)
    double = jax.ShapeDtypeStruct((slots, 2, order, order), float32)
    return pl.pallas_call(
        soap_kernel,
        grid=(slots,),
        in_specs=[pl.BlockSpec(memory_space=pltpu.SMEM)] + [one] * 7,
        out_specs=[one] * 5 + [two] * 2,
        out_shape=[jax.ShapeDtypeStruct((slots, order, order), bfloat16)] + [single] * 4 + [double] * 2,
        compiler_params=pltpu.CompilerParams(vmem_limit_bytes=VMEM_LIMIT),
        cost_estimate=pl.CostEstimate(
            flops=slots * 120 * order**3, bytes_accessed=slots * 60 * order**2, transcendentals=0
        ),
    )(factor.reshape(1, 1), gradient, first_old, second_old, left_old, right_old, left_base, right_base)


def renew_kernel(rows, gram_ref, turn_ref, q_ref, x_ref, u_ref):
    count, order = gram_ref.shape[0], gram_ref.shape[1]
    eye = (
        lax.broadcasted_iota(jnp.int32, (rows, rows), 0)
        == lax.broadcasted_iota(jnp.int32, (rows, rows), 1)
    ).astype(float32)
    sublane = lax.broadcasted_iota(jnp.int32, (1, 8, 1), 1)
    for low in range(0, order, rows):
        part = slice(low, low + rows)

        def panel(at, carry, low=low, part=part):
            row = jnp.concatenate([gram_ref[at, part, :], turn_ref[at, part, :]], 1)
            if low:
                row = row - exact(u_ref[at, :low, part], u_ref[at, :low, :], TN)
            u_ref[at, part, :] = row
            x_ref[at] = jnp.concatenate([row[:, part], eye], 1)
            return carry

        lax.fori_loop(0, count, panel, 0, unroll=2)
        for j in range(rows):
            tile = j // 8 * 8
            row = x_ref[:, j : j + 1, :]
            row = row * (1.0 / row[:, :, j : j + 1])
            top = x_ref[:, tile : tile + 8, :]
            below = jnp.where(sublane > j - tile, top[:, :, j : j + 1], 0.0)
            x_ref[:, tile : tile + 8, :] = top - below * row
            if tile + 8 < rows:
                rest = x_ref[:, tile + 8 :, :]
                x_ref[:, tile + 8 :, :] = rest - rest[:, :, j : j + 1] * row

        def solve(at, carry, part=part):
            both = x_ref[at]
            diagonal = jnp.sum(both[:, :rows] * eye, 1, keepdims=True)
            u_ref[at, part, :] = exact(both[:, rows:] * lax.rsqrt(diagonal), u_ref[at, part, :])
            return carry

        lax.fori_loop(0, count, solve, 0, unroll=2)

    def turn_back(at, carry):
        q_ref[at] = u_ref[at, :, order:].T
        return carry

    lax.fori_loop(0, count, turn_back, 0)


def renew_bases(gram, turn, rows=64):
    count, order, _ = gram.shape
    return pl.pallas_call(
        partial(renew_kernel, rows),
        out_shape=jax.ShapeDtypeStruct(gram.shape, float32),
        in_specs=[pl.BlockSpec(memory_space=pltpu.VMEM)] * 2,
        out_specs=pl.BlockSpec(memory_space=pltpu.VMEM),
        scratch_shapes=[
            pltpu.VMEM((count, rows, 2 * rows), float32),
            pltpu.VMEM((count, order, 2 * order), float32),
        ],
        compiler_params=pltpu.CompilerParams(vmem_limit_bytes=VMEM_LIMIT),
        cost_estimate=pl.CostEstimate(
            flops=count * 200 * order**3, bytes_accessed=count * 12 * order**2, transcendentals=0
        ),
    )(gram, turn)


def partner(bit, narrow_bits):
    axis, step = ("narrow", 1 << bit) if bit < narrow_bits else ("wide", 1 << (bit - narrow_bits))
    place = lax.axis_index(axis)
    mine = lax.rem(place // step, 2)
    return {axis: place + step - 2 * step * mine}, mine


def greet(peers):
    barrier = pltpu.get_barrier_semaphore()
    for device, _ in peers:
        pl.semaphore_signal(barrier, inc=1, device_id=device, device_id_type=MESH)
    pl.semaphore_wait(barrier, len(peers))


def mesh_bits():
    narrow_bits = lax.axis_size("narrow").bit_length() - 1
    return narrow_bits + lax.axis_size("wide").bit_length() - 1, narrow_bits


def reduce_steps(bits, narrow_bits, plans, chunks, sources, outs, scratch):
    count = len(sources)
    held = scratch[:count]
    arrived = [scratch[count * (1 + s) : count * (2 + s)] for s in range(bits)]
    load_sem, send_sem, recv_sem = scratch[count * (1 + bits) :]
    peers = [partner(b, narrow_bits) for b in range(bits)]
    first = plans[0][0]
    order_of_dims = list(reversed(range(bits)))
    whole = slice(None)

    def within(order, stage, current):
        return tuple(
            peers[b][1] if b in order[:stage] else current if b == order[stage] else whole
            for b in order_of_dims
            if b != first
        )

    def of_source(value):
        return tuple(value if b == first else whole for b in order_of_dims)

    def rows_of(chunk):
        at, row, rows, colour = chunks[chunk]
        return at, plans[colour], (pl.ds(row, rows), whole)

    def send(chunk, stage):
        at, order, part = rows_of(chunk)
        device, mine = peers[order[stage]]
        if stage == 0:
            source = sources[at].at[of_source(1 - mine) + part]
        else:
            source = held[at].at[within(order, stage, 1 - mine) + part]
        return pltpu.make_async_remote_copy(
            src_ref=source,
            dst_ref=arrived[stage][at].at[(whole,) * (bits - 1 - stage) + part],
            send_sem=send_sem.at[chunk, stage],
            recv_sem=recv_sem.at[chunk, stage],
            device_id=device,
            device_id_type=MESH,
        )

    def load(chunk):
        at, order, part = rows_of(chunk)
        return pltpu.make_async_copy(
            sources[at].at[of_source(peers[first][1]) + part],
            held[at].at[(whole,) * (bits - 1) + part],
            load_sem.at[chunk],
        )

    def begin(chunk):
        send(chunk, 0).start()
        load(chunk).start()

    def finish(chunk, stage):
        at, order, part = rows_of(chunk)
        if stage == 0:
            load(chunk).wait()
        send(chunk, stage).wait_recv()
        left = bits - 1 - stage
        keep = within(order, stage, peers[order[stage]][1])
        if left == 0:
            own = held[at][keep + part].astype(float32)
            outs[at][part] = own + arrived[stage][at][part].astype(float32)
            return
        free = [i for i, k in enumerate(keep) if isinstance(k, slice)]

        def add(m, carry):
            which = tuple(m // (1 << (left - 1 - i)) % 2 for i in range(left))
            spot = list(keep)
            for i, f in enumerate(free):
                spot[f] = which[i]
            spot = tuple(spot) + part
            held[at][spot] = held[at][spot] + arrived[stage][at][which + part]
            return carry

        lax.fori_loop(0, 1 << left, add, 0)
        send(chunk, stage + 1).start()

    def drain():
        for chunk in range(len(chunks)):
            for stage in range(bits):
                send(chunk, stage).wait_send()

    return peers, begin, finish, drain


def reduce_kernel(bits, narrow_bits, plans, chunks, count, *refs):
    peers, begin, finish, drain = reduce_steps(
        bits, narrow_bits, plans, chunks, refs[:count], refs[count : 2 * count], refs[2 * count :]
    )
    greet(peers)
    total = len(chunks)
    for chunk in range(min(AHEAD, total)):
        begin(chunk)
    for step in range(total + 2 * bits):
        for stage in reversed(range(bits)):
            chunk = step - 2 * stage
            if 0 <= chunk < total:
                finish(chunk, stage)
                if stage == 0 and chunk + AHEAD < total:
                    begin(chunk + AHEAD)
    drain()


def slot_table(chunks, bits, slots, pace, delay):
    table = [[] for _ in range(slots + 1)]
    done = sorted(
        (chunk * pace + (stage + 1) * delay, -stage, chunk, stage)
        for chunk in range(chunks)
        for stage in range(bits)
    )
    for when, _, chunk, stage in done:
        table[min(int(when), slots)].append((chunk, stage))
    return table


def reduce_plan(parts, pieces):
    bits, narrow_bits = mesh_bits()
    shapes = [part.shape[1:] for part in parts]
    kinds = [part.dtype for part in parts]
    chunks = []
    for at, (shape, cut) in enumerate(zip(shapes, pieces)):
        rows = shape[0] // cut
        for row in range(0, shape[0], rows):
            chunks.append((at, row, rows, len(chunks) % len(ORDERS)))
    later = tuple(range(3, bits))
    plans = tuple(tuple(b for part in order for b in (later if part is None else (part,))) for order in ORDERS)
    sizes = [bits - 1] + [bits - 1 - stage for stage in range(bits)]
    scratch = [
        pltpu.VMEM((2,) * size + shape, kind)
        for size in sizes
        for shape, kind in zip(shapes, kinds)
    ]
    total = len(chunks)
    scratch += [
        pltpu.SemaphoreType.DMA((total,)),
        pltpu.SemaphoreType.DMA((total, bits)),
        pltpu.SemaphoreType.DMA((total, bits)),
    ]
    outs = [jax.ShapeDtypeStruct(shape, float32) for shape in shapes]
    halved = [part.reshape((2,) * bits + shape) for part, shape in zip(parts, shapes)]
    return bits, narrow_bits, plans, tuple(chunks), halved, outs, scratch


def reduce_to_shards(parts, pieces, collective_id):
    bits, narrow_bits, plans, chunks, halved, outs, scratch = reduce_plan(parts, pieces)
    return pl.pallas_call(
        partial(reduce_kernel, bits, narrow_bits, plans, chunks, len(parts)),
        out_shape=outs,
        in_specs=[pl.BlockSpec(memory_space=pl.ANY)] * len(parts),
        out_specs=[pl.BlockSpec(memory_space=pltpu.VMEM)] * len(parts),
        scratch_shapes=scratch,
        compiler_params=pltpu.CompilerParams(
            collective_id=collective_id, has_side_effects=True, vmem_limit_bytes=58 * 2**20
        ),
        cost_estimate=pl.CostEstimate(flops=10**8, bytes_accessed=4 * 10**8, transcendentals=0),
    )(*halved)


def gather_steps(bits, narrow_bits, plans, chunks, sources, outs, scratch):
    own_sem, send_sem, recv_sem = scratch
    peers = [partner(b, narrow_bits) for b in range(bits)]
    dims = list(reversed(range(bits)))

    def place(chunk, stage):
        at, band, bands, col, cols, colour = chunks[chunk]
        done = plans[colour][:stage]
        index = tuple(slice(None) if b in done else peers[b][1] for b in dims)
        return outs[at].at[(pl.ds(band, bands),) + index + (slice(None), pl.ds(col, cols))]

    def own(chunk):
        at, band, bands, col, cols, colour = chunks[chunk]
        return sources[at].at[pl.ds(band, bands), :, pl.ds(col, cols)]

    def send(chunk, stage):
        colour = chunks[chunk][-1]
        target = place(chunk, stage)
        return pltpu.make_async_remote_copy(
            src_ref=target if stage else own(chunk),
            dst_ref=target,
            send_sem=send_sem.at[chunk, stage],
            recv_sem=recv_sem.at[chunk, stage],
            device_id=peers[plans[colour][stage]][0],
            device_id_type=MESH,
        )

    def keep(chunk):
        return pltpu.make_async_copy(own(chunk), place(chunk, 0), own_sem.at[chunk])

    def begin(chunk):
        send(chunk, 0).start()
        keep(chunk).start()

    def finish(chunk, stage):
        if stage == 0:
            keep(chunk).wait()
        send(chunk, stage).wait_recv()
        if stage + 1 < bits:
            send(chunk, stage + 1).start()

    def drain():
        for chunk in range(len(chunks)):
            for stage in range(bits):
                send(chunk, stage).wait_send()

    return peers, begin, finish, drain


def gather_kernel(bits, narrow_bits, plans, chunks, count, *refs):
    peers, begin, finish, drain = gather_steps(
        bits, narrow_bits, plans, chunks, refs[:count], refs[count : 2 * count], refs[2 * count :]
    )
    greet(peers)
    total = len(chunks)
    for chunk in range(total):
        begin(chunk)
    for step in range(total + SKEW * bits):
        for stage in reversed(range(bits)):
            chunk = step - SKEW * stage
            if 0 <= chunk < total:
                finish(chunk, stage)
    drain()


def gather_plan(parts, pieces):
    bits, narrow_bits = mesh_bits()
    chunks = []
    for at, (part, (cut, cut_cols)) in enumerate(zip(parts, pieces)):
        bands, cols = part.shape[0] // cut, part.shape[2] // cut_cols
        for band in range(0, part.shape[0], bands):
            for col in range(0, part.shape[2], cols):
                chunks.append((at, band, bands, col, cols, len(chunks) % 2))
    later = tuple(reversed(range(3, bits)))
    plans = (later + (1, 2, 0), later + (2, 1, 0))
    total = len(chunks)
    outs = [
        jax.ShapeDtypeStruct(part.shape[:1] + (2,) * bits + part.shape[1:], part.dtype)
        for part in parts
    ]
    scratch = [
        pltpu.SemaphoreType.DMA((total,)),
        pltpu.SemaphoreType.DMA((total, bits)),
        pltpu.SemaphoreType.DMA((total, bits)),
    ]
    return bits, narrow_bits, plans, tuple(chunks), outs, scratch


def gather_bands(parts, pieces, collective_id):
    bits, narrow_bits, plans, chunks, outs, scratch = gather_plan(parts, pieces)
    results = pl.pallas_call(
        partial(gather_kernel, bits, narrow_bits, plans, chunks, len(parts)),
        out_shape=outs,
        in_specs=[pl.BlockSpec(memory_space=pl.ANY)] * len(parts),
        out_specs=[pl.BlockSpec(memory_space=pl.ANY)] * len(parts),
        scratch_shapes=scratch,
        compiler_params=pltpu.CompilerParams(collective_id=collective_id, has_side_effects=True),
        cost_estimate=pl.CostEstimate(flops=0, bytes_accessed=10**8, transcendentals=0),
    )(*parts)
    return [
        result.reshape(part.shape[:1] + (1 << bits,) + part.shape[1:])
        for result, part in zip(results, parts)
    ]


def group_peers():
    count = lax.axis_size("narrow")
    me = lax.axis_index("narrow")
    return me, [({"narrow": lax.rem(me + d, count)}, lax.rem(me + d, count)) for d in range(count)]


def rows_at(place, rows):
    return pl.ds(pl.multiple_of(place * rows, rows), rows)


def attend_kernel(safe, chunk, halves, plan, slots, length_ref, *refs):
    count = plan[4]
    packed, sources = refs[:halves], refs[halves : halves + count]
    refs = refs[halves + count :]
    scenes_out, merged, mixed_out, log_ref = refs[:4]
    scene_ref, o_ref, vt_ref, s_ref, near_sem, in_sem, back_sem, out_sem = refs[4 + count : 12 + count]
    others, begin, finish, drain = gather_steps(
        *plan[:4], sources, refs[4 : 4 + count], refs[12 + count :]
    )
    seq_len = scene_ref.shape[1]
    me, peers = group_peers()
    devices = len(peers)
    tok_rows = seq_len // devices
    length = length_ref[0]
    half, step = pl.program_id(0), pl.program_id(1)
    last = pl.num_programs(1) - 1
    own = rows_at(me, tok_rows)

    def bring(h, d):
        device, place = peers[d]
        if d == 0:
            return pltpu.make_async_copy(packed[h].at[me], scene_ref.at[h, own], in_sem.at[h, 0])
        return pltpu.make_async_remote_copy(
            src_ref=packed[h].at[place],
            dst_ref=scene_ref.at[h, own],
            send_sem=near_sem.at[h, d],
            recv_sem=in_sem.at[h, d],
            device_id=device,
            device_id_type=MESH,
        )

    def give(h, d, at, to, sender):
        column = pl.ds(pl.multiple_of((sender * halves + h) * PAIR, PAIR), PAIR)
        target = merged.at[:, column]
        source = o_ref.at[h, rows_at(to, tok_rows)]
        if d == 0:
            return pltpu.make_async_copy(source, target, out_sem.at[h, 0])
        return pltpu.make_async_remote_copy(
            src_ref=source,
            dst_ref=target,
            send_sem=back_sem.at[h, d],
            recv_sem=out_sem.at[h, d],
            device_id={"narrow": to},
            device_id_type=MESH,
        )

    def save_scene(h):
        return pltpu.make_async_copy(scene_ref.at[h], scenes_out.at[h], near_sem.at[h, 0])

    def save_mixed(h):
        return pltpu.make_async_copy(o_ref.at[h], mixed_out.at[h], back_sem.at[h, 0])

    @pl.when((half == 0) & (step == 0))
    def _():
        greet(peers[1:] + others[plan[1] :])
        for d in range(devices):
            bring(0, d).start()
        for which in range(len(plan[3])):
            begin(which)

    for h in range(halves):

        @pl.when((half == h) & (step == 0))
        def _(h=h):
            for d in range(devices):
                if d:
                    bring(h, d).wait_recv()
                else:
                    bring(h, d).wait()
            if h + 1 < halves:
                for d in range(devices):
                    bring(h + 1, d).start()
            save_scene(h).start()
            vt_ref[...] = scene_ref[h, :, 2 * PAIR :].T

    points = 2 * seq_len // chunk

    def move_at(point):
        for h in range(halves):
            for s in range(devices):
                todo = slots[(h * devices + s) * 2 * points + point]
                if todo:

                    @pl.when((half == h) & (step == s))
                    def _(todo=todo):
                        for which, stage in todo:
                            finish(which, stage)

    to = lax.rem(me + 1 + step, devices)
    here = rows_at(to, tok_rows)
    outs = []
    for head in range(2):
        queries = one_head(scene_ref[half, here, :PAIR], head) * bfloat16(HEAD**-0.5)
        topmost = None
        for at in range(0, seq_len, chunk):
            move_at(head * points + at // chunk)
            scores = lax.dot_general(
                scene_ref[half, at : at + chunk, PAIR : 2 * PAIR],
                queries,
                NT,
                preferred_element_type=float32,
            )
            scores = hide(scores, at, safe, length)
            s_ref[head, at : at + chunk, :] = scores
            top = jnp.max(scores, 0, keepdims=True)
            topmost = top if topmost is None else jnp.maximum(topmost, top)
        totals = jnp.zeros_like(topmost)
        mixed = jnp.zeros((HEAD, tok_rows), float32)
        for at in range(0, seq_len, chunk):
            move_at(head * points + points // 2 + at // chunk)
            expo = jnp.exp(s_ref[head, at : at + chunk, :] - topmost)
            totals += jnp.sum(expo, 0, keepdims=True)
            mixed += jnp.dot(
                vt_ref[head * HEAD : (head + 1) * HEAD, at : at + chunk],
                expo.astype(bfloat16),
                preferred_element_type=float32,
            )
        outs.append(mixed * (1.0 / totals))
        log_ref[half, head : head + 1, here] = topmost + jnp.log(totals)
    o_ref[half, here, :] = jnp.concatenate(outs, 0).T.astype(bfloat16)

    for h in range(halves):
        for s in range(devices):

            @pl.when((half == h) & (step == s))
            def _(h=h, s=s):
                d = (s + 1) % devices
                give(h, d, s, lax.rem(me + d, devices), me).start()
                if s == devices - 1:
                    save_mixed(h).start()

    @pl.when((half == halves - 1) & (step == last))
    def _():
        for which, stage in slots[-1]:
            finish(which, stage)
        drain()
        for h in range(halves):
            for d in range(devices):
                if d:
                    bring(h, d).wait_send()
                    sender = lax.rem(me + devices - d, devices)
                    arriving = give(h, d, d, lax.rem(me + d, devices), sender)
                    arriving.wait_recv()
                    arriving.wait_send()
                else:
                    give(h, 0, 0, me, me).wait()
            save_scene(h).wait()
            save_mixed(h).wait()


def attend(lengths, packed, safe, parts, pieces, collective_id, chunk=512):
    devices, tok_rows, _ = packed[0].shape
    halves, seq_len = len(packed), devices * tok_rows
    width = devices * halves * PAIR
    anywhere = pl.BlockSpec(memory_space=pl.ANY)
    bits, narrow_bits, plans, chunks, outs, scratch = gather_plan(parts, pieces)
    slots = slot_table(
        len(chunks), bits, halves * devices * 4 * (seq_len // chunk), GATHER_PACE, GATHER_DELAY
    )
    plan = (bits, narrow_bits, plans, chunks, len(parts))
    results = pl.pallas_call(
        partial(attend_kernel, safe, chunk, halves, plan, slots),
        grid=(halves, devices),
        in_specs=[pl.BlockSpec(memory_space=pltpu.SMEM)] + [anywhere] * (halves + len(parts)),
        out_specs=[anywhere] * 3
        + [pl.BlockSpec((halves, 2, seq_len), lambda p, i: (0, 0, 0))]
        + [anywhere] * len(parts),
        out_shape=[
            jax.ShapeDtypeStruct((halves, seq_len, 3 * PAIR), bfloat16),
            jax.ShapeDtypeStruct((tok_rows, width), bfloat16),
            jax.ShapeDtypeStruct((halves, seq_len, PAIR), bfloat16),
            jax.ShapeDtypeStruct((halves, 2, seq_len), float32),
        ]
        + outs,
        scratch_shapes=[
            pltpu.VMEM((halves, seq_len, 3 * PAIR), bfloat16),
            pltpu.VMEM((halves, seq_len, PAIR), bfloat16),
            pltpu.VMEM((PAIR, seq_len), bfloat16),
            pltpu.VMEM((2, seq_len, tok_rows), float32),
        ]
        + [pltpu.SemaphoreType.DMA((halves, devices))] * 4
        + scratch,
        compiler_params=pltpu.CompilerParams(
            collective_id=collective_id, has_side_effects=True, vmem_limit_bytes=VMEM_LIMIT
        ),
        cost_estimate=pl.CostEstimate(
            flops=4 * halves * 2 * 4 * seq_len * seq_len * HEAD,
            bytes_accessed=16 * seq_len * PAIR * halves,
            transcendentals=0,
        ),
    )(lengths, *packed, *parts)
    gathered = [
        result.reshape(part.shape[0], 1 << bits, *part.shape[1:])
        for result, part in zip(results[4:], parts)
    ]
    return list(results[:4]) + gathered


def attend_backward_kernel(
    safe, chunk, halves, plan, slots, length_ref, scene_ref, o_ref, log_ref, d_merged, *refs
):
    count = plan[4]
    sources, packed_out, outs = refs[:count], refs[count], refs[count + 1 : 2 * count + 1]
    do_ref, stage_ref, kt_ref, dk_sum, dv_sum = refs[2 * count + 1 : 2 * count + 6]
    near_sem, in_sem, q_send, q_recv, kv_send, kv_recv = refs[2 * count + 6 : 2 * count + 12]
    others, begin, finish, drain = reduce_steps(*plan[:4], sources, outs, refs[2 * count + 12 :])
    total = len(plan[3])
    me, peers = group_peers()
    devices = len(peers)
    seq_len = scene_ref.shape[1]
    tok_rows = seq_len // devices
    length = length_ref[0]
    half, step = pl.program_id(0), pl.program_id(1)
    own = rows_at(me, tok_rows)
    chunks = seq_len // chunk

    def move(which, stage):
        finish(which, stage)
        if stage == 0 and which + AHEAD < total:
            begin(which + AHEAD)

    def move_at(head, part):
        for h in range(halves):
            for s in range(devices):
                todo = slots[((h * devices + s) * 2 + head) * chunks + part]
                if todo:

                    @pl.when((half == h) & (step == s))
                    def _(todo=todo):
                        for which, stage in todo:
                            move(which, stage)

    def bring(h, d):
        device, place = peers[d]
        column = pl.ds(pl.multiple_of((place * halves + h) * PAIR, PAIR), PAIR)
        source, target = d_merged.at[:, column], do_ref.at[h, own]
        if d == 0:
            return pltpu.make_async_copy(source, target, in_sem.at[h, 0])
        return pltpu.make_async_remote_copy(
            src_ref=source,
            dst_ref=target,
            send_sem=near_sem.at[h, d],
            recv_sem=in_sem.at[h, d],
            device_id=device,
            device_id_type=MESH,
        )

    def give(h, d, columns, send_sem, recv_sem, sender):
        device, place = peers[d]
        source = stage_ref.at[h, rows_at(place, tok_rows), columns]
        target = packed_out.at[h, sender, :, columns]
        if d == 0:
            return pltpu.make_async_copy(source, target, recv_sem.at[h, 0])
        return pltpu.make_async_remote_copy(
            src_ref=source,
            dst_ref=target,
            send_sem=send_sem.at[h, d],
            recv_sem=recv_sem.at[h, d],
            device_id=device,
            device_id_type=MESH,
        )

    q_columns, kv_columns = pl.ds(0, PAIR), pl.ds(PAIR, 2 * PAIR)

    @pl.when((half == 0) & (step == 0))
    def _():
        narrow_bits = plan[1]
        greet(peers[1:] + others[narrow_bits:])
        for h in range(halves):
            for d in range(devices):
                bring(h, d).start()
        for which in range(min(AHEAD, total)):
            begin(which)

    for h in range(halves):

        @pl.when((half == h) & (step == 0))
        def _(h=h):
            kt_ref[...] = scene_ref[0, :, PAIR : 2 * PAIR].T
            dk_sum[...] = jnp.zeros_like(dk_sum)
            dv_sum[...] = jnp.zeros_like(dv_sum)
            for d in range(devices):
                if d:
                    bring(h, d).wait_recv()
                else:
                    bring(h, d).wait()

    here = rows_at(lax.rem(me + 1 + step, devices), tok_rows)
    products = (o_ref[0, here, :].astype(float32) * do_ref[half, here, :].astype(float32)).T
    turned = []
    for head in range(2):
        lanes = slice(head * HEAD, (head + 1) * HEAD)
        queries = one_head(scene_ref[0, here, :PAIR], head) * bfloat16(HEAD**-0.5)
        d_mixed = one_head(do_ref[half, here, :], head)
        inner = jnp.sum(products[lanes, :], 0, keepdims=True)
        log_total = log_ref[0, head : head + 1, here]
        d_queries = jnp.zeros((HEAD, tok_rows), float32)
        for index in range(chunks):
            move_at(head, index)
            at = index * chunk
            part = slice(at, at + chunk)
            scores = lax.dot_general(
                scene_ref[0, part, PAIR : 2 * PAIR], queries, NT, preferred_element_type=float32
            )
            probs = jnp.exp(hide(scores, at, safe, length) - log_total)
            d_probs = lax.dot_general(
                scene_ref[0, part, 2 * PAIR :], d_mixed, NT, preferred_element_type=float32
            )
            dv_sum[part, :] += jnp.dot(
                probs.astype(bfloat16), d_mixed, preferred_element_type=float32
            )
            d_scores = (probs * (d_probs - inner)).astype(bfloat16)
            dk_sum[part, :] += jnp.dot(d_scores, queries, preferred_element_type=float32)
            d_queries += jnp.dot(kt_ref[lanes, part], d_scores, preferred_element_type=float32)
        turned.append(d_queries * HEAD**-0.5)
    stage_ref[half, here, :PAIR] = jnp.concatenate(turned, 0).T.astype(bfloat16)

    for h in range(halves):
        for s in range(devices):

            @pl.when((half == h) & (step == s))
            def _(h=h, s=s):
                give(h, (s + 1) % devices, q_columns, q_send, q_recv, me).start()
                if s == devices - 1:
                    stage_ref[h, :, PAIR : 2 * PAIR] = dk_sum[...].astype(bfloat16)
                    stage_ref[h, :, 2 * PAIR :] = dv_sum[...].astype(bfloat16)
                    for d in range(devices):
                        give(h, d, kv_columns, kv_send, kv_recv, me).start()

    @pl.when((half == halves - 1) & (step == devices - 1))
    def _():
        for which, stage in slots[-1]:
            move(which, stage)
        drain()
        for h in range(halves):
            for d in range(devices):
                for columns, send_sem, recv_sem in (
                    (q_columns, q_send, q_recv),
                    (kv_columns, kv_send, kv_recv),
                ):
                    sender = lax.rem(me + devices - d, devices)
                    copy = give(h, d, columns, send_sem, recv_sem, sender)
                    if d:
                        copy.wait_recv()
                        copy.wait_send()
                    else:
                        copy.wait()
                if d:
                    bring(h, d).wait_send()


def attend_backward(
    lengths, scenes, mixed, d_merged, log_totals, safe, parts, pieces, collective_id, chunk=512
):
    halves, seq_len, _ = scenes.shape
    devices = lax.axis_size("narrow")
    tok_rows = seq_len // devices
    bits, narrow_bits, plans, chunks, halved, outs, scratch = reduce_plan(parts, pieces)
    slots = slot_table(
        len(chunks), bits, halves * devices * 2 * (seq_len // chunk), PACE, DELAY
    )
    anywhere = pl.BlockSpec(memory_space=pl.ANY)

    def of_half(array):
        return pl.BlockSpec((1,) + array.shape[1:], lambda p, i: (p, 0, 0))

    return pl.pallas_call(
        partial(
            attend_backward_kernel,
            safe,
            chunk,
            halves,
            (bits, narrow_bits, plans, chunks, len(parts)),
            slots,
        ),
        grid=(halves, devices),
        in_specs=[
            pl.BlockSpec(memory_space=pltpu.SMEM),
            of_half(scenes),
            of_half(mixed),
            of_half(log_totals),
            anywhere,
        ]
        + [anywhere] * len(parts),
        out_specs=[anywhere] + [pl.BlockSpec(out.shape, lambda p, i: (0, 0)) for out in outs],
        out_shape=[jax.ShapeDtypeStruct((halves, devices, tok_rows, 3 * PAIR), bfloat16)] + outs,
        scratch_shapes=[
            pltpu.VMEM((halves, seq_len, PAIR), bfloat16),
            pltpu.VMEM((halves, seq_len, 3 * PAIR), bfloat16),
            pltpu.VMEM((PAIR, seq_len), bfloat16),
            pltpu.VMEM((seq_len, PAIR), float32),
            pltpu.VMEM((seq_len, PAIR), float32),
        ]
        + [pltpu.SemaphoreType.DMA((halves, devices))] * 6
        + scratch,
        compiler_params=pltpu.CompilerParams(
            collective_id=collective_id, has_side_effects=True, vmem_limit_bytes=60 * 2**20
        ),
        cost_estimate=pl.CostEstimate(
            flops=4 * halves * 2 * 10 * seq_len * seq_len * HEAD,
            bytes_accessed=32 * seq_len * PAIR,
            transcendentals=0,
        ),
    )(lengths, scenes, mixed, log_totals, d_merged, *halved)


def feed_kernel(deal, acts_ref, grad_ref, middle_ref, up_ref, down_ref, out_ref, back_ref, one_ref, two_ref, turned_ref, sum_ref):
    at, last = pl.program_id(0), pl.num_programs(0) - 1

    @pl.when(at == 0)
    def _():
        sum_ref[...] = middle_ref[...]
        back_ref[...] = jnp.zeros_like(back_ref)
        turned_ref[...] = acts_ref[...].T

    acts, grad = acts_ref[...], grad_ref[...]
    hidden = jnp.dot(acts, up_ref[...], preferred_element_type=float32)
    square = hidden * hidden
    bend = jnp.tanh(GELU * hidden * (1.0 + CUBIC * square))
    share = 0.5 + 0.5 * bend
    active = (hidden * share).astype(bfloat16)
    slope = share + hidden * (0.5 - 0.5 * bend * bend) * (GELU + 3.0 * GELU * CUBIC * square)
    d_active = lax.dot_general(grad, down_ref[...], NT, preferred_element_type=float32)
    d_hidden = (d_active * slope).astype(bfloat16)
    sum_ref[...] += jnp.dot(active, down_ref[...], preferred_element_type=float32)
    back_ref[...] += lax.dot_general(d_hidden, up_ref[...], NT, preferred_element_type=float32)
    if deal:
        rows = BLOCK // one_ref.shape[0]
        d_up = jnp.dot(turned_ref[...], d_hidden, preferred_element_type=float32)
        d_up = d_up.astype(bfloat16)
        d_down = jnp.dot(active.T, grad, preferred_element_type=float32).astype(bfloat16)
        for band in range(d_up.shape[0] // BLOCK):
            blocks = [
                d_up[band * BLOCK : (band + 1) * BLOCK, start : start + BLOCK].reshape(-1, rows, BLOCK)
                for start in range(0, d_up.shape[1], BLOCK)
            ]
            one_ref[:, band] = jnp.concatenate(blocks, 1)
        blocks = [
            d_down[low : low + BLOCK, start : start + BLOCK].reshape(-1, rows, BLOCK)
            for low in range(0, d_down.shape[0], BLOCK)
            for start in range(0, d_down.shape[1], BLOCK)
        ]
        two_ref[...] = jnp.concatenate(blocks, 1)
    else:
        one_ref[...] = active
        two_ref[...] = d_hidden

    @pl.when(at == last)
    def _():
        out_ref[...] = sum_ref[...].astype(bfloat16)


def feed_forward(acts, grad, middle, w_up, w_down, device_count, tile=2 * BLOCK):
    tok_rows, width = acts.shape
    hidden = w_up.shape[1]
    rows = BLOCK // device_count
    deal = rows % 8 == 0
    full = pl.BlockSpec((tok_rows, width), lambda j: (0, 0))
    if deal:
        bands, blocks = width // BLOCK, hidden // BLOCK
        kinds = [(device_count, bands, blocks * rows, BLOCK), (device_count, blocks * bands * rows, BLOCK)]
        part = tile // BLOCK * rows
        specs = [
            pl.BlockSpec((device_count, bands, part, BLOCK), lambda j: (0, 0, j, 0)),
            pl.BlockSpec((device_count, bands * part, BLOCK), lambda j: (0, j, 0)),
        ]
    else:
        kinds = [(tok_rows, hidden)] * 2
        specs = [pl.BlockSpec((tok_rows, tile), lambda j: (0, j))] * 2
    out, back, one, two = pl.pallas_call(
        partial(feed_kernel, deal),
        grid=(hidden // tile,),
        in_specs=[full, full, full]
        + [
            pl.BlockSpec((width, tile), lambda j: (0, j)),
            pl.BlockSpec((tile, width), lambda j: (j, 0)),
        ],
        out_specs=[full, full] + specs,
        out_shape=[
            jax.ShapeDtypeStruct((tok_rows, width), bfloat16),
            jax.ShapeDtypeStruct((tok_rows, width), float32),
        ]
        + [jax.ShapeDtypeStruct(kind, bfloat16) for kind in kinds],
        scratch_shapes=[pltpu.VMEM((width, tok_rows), bfloat16), pltpu.VMEM((tok_rows, width), float32)],
        compiler_params=pltpu.CompilerParams(vmem_limit_bytes=58 * 2**20),
        cost_estimate=pl.CostEstimate(
            flops=12 * tok_rows * width * hidden, bytes_accessed=8 * width * hidden, transcendentals=0
        ),
    )(acts, grad, middle, w_up, w_down)
    if deal:
        return out, back, one.reshape(device_count, -1, BLOCK), two
    columns = lambda size: tuple(((0, 0, start, BLOCK),) for start in range(0, size, BLOCK))
    return (
        out,
        back,
        weight_grad(acts, [two[None]], columns(hidden), device_count),
        weight_grad(one, [grad[None]], columns(width), device_count),
    )


def ship_kernel(narrow_count, held_ref, *refs):
    shards, gain_ref = refs[:4], refs[4]
    arrived, total_ref = refs[5:7]
    pieces, outgoing, squares, send_sem, recv_sem, tile_send, tile_recv = refs[7:]
    devices, slots = outgoing.shape[:2]
    me = lax.axis_index("wide") * narrow_count + lax.axis_index("narrow")

    def device(d):
        place = lax.rem(me + d, devices)
        return place, {"wide": place // narrow_count, "narrow": lax.rem(place, narrow_count)}

    barrier = pltpu.get_barrier_semaphore()

    def announce(d, carry):
        pl.semaphore_signal(barrier, inc=1, device_id=device(d)[1], device_id_type=MESH)
        return carry

    lax.fori_loop(1, devices, announce, 0)
    at, own = 0, jnp.sum(gain_ref[...] * gain_ref[...])
    for shard in shards:
        values = shard[...]
        own += jnp.sum(values * values)
        pieces[at : at + values.shape[0]] = values
        at += values.shape[0]
    squares[me] = jnp.full(squares.shape[1:], own, float32)

    def pack(place, carry):
        for slot in range(slots):
            block = held_ref[place * slots + slot]
            piece = pieces[jnp.maximum(block, 0)]
            outgoing[place, slot] = jnp.where(block >= 0, piece, 0.0).astype(bfloat16)
        return carry

    lax.fori_loop(0, devices, pack, 0)
    pl.semaphore_wait(barrier, devices - 1)

    def copies(d):
        place, target = device(d)
        return (
            pltpu.make_async_remote_copy(
                src_ref=outgoing.at[place],
                dst_ref=arrived.at[:, me],
                send_sem=send_sem.at[d],
                recv_sem=recv_sem.at[d],
                device_id=target,
                device_id_type=MESH,
            ),
            pltpu.make_async_remote_copy(
                src_ref=squares.at[me],
                dst_ref=squares.at[me],
                send_sem=tile_send.at[d],
                recv_sem=tile_recv.at[d],
                device_id=target,
                device_id_type=MESH,
            ),
        )

    def start(d, carry):
        for copy in copies(d):
            copy.start()
        return carry

    lax.fori_loop(1, devices, start, 0)
    arrived[:, me] = outgoing[me]

    def arrive(d, carry):
        sender = lax.rem(me + devices - d, devices)
        pltpu.make_async_remote_copy(
            src_ref=outgoing.at[sender],
            dst_ref=arrived.at[:, sender],
            send_sem=send_sem.at[d],
            recv_sem=recv_sem.at[d],
            device_id=device(d)[1],
            device_id_type=MESH,
        ).wait_recv()
        pltpu.make_async_remote_copy(
            src_ref=squares.at[sender],
            dst_ref=squares.at[sender],
            send_sem=tile_send.at[d],
            recv_sem=tile_recv.at[d],
            device_id=device(d)[1],
            device_id_type=MESH,
        ).wait_recv()
        for copy in copies(d):
            copy.wait_send()
        return carry

    lax.fori_loop(1, devices, arrive, 0)
    total_ref[...] = jnp.sum(squares[...], 0)


def ship(shards, gain_grad, held, cap_slots, collective_id):
    devices = held.shape[0] // cap_slots
    rows = shards[0].shape[1]
    blocks = sum(shard.shape[0] for shard in shards)
    tile = (8, 128)
    vmem = pl.BlockSpec(memory_space=pltpu.VMEM)
    return pl.pallas_call(
        partial(ship_kernel, lax.axis_size("narrow")),
        in_specs=[pl.BlockSpec(memory_space=pltpu.SMEM)] + [vmem] * (len(shards) + 1),
        out_specs=[vmem, vmem],
        out_shape=[
            jax.ShapeDtypeStruct((cap_slots, devices, rows, BLOCK), bfloat16),
            jax.ShapeDtypeStruct(tile, float32),
        ],
        scratch_shapes=[
            pltpu.VMEM((blocks, rows, BLOCK), float32),
            pltpu.VMEM((devices, cap_slots, rows, BLOCK), bfloat16),
            pltpu.VMEM((devices,) + tile, float32),
        ]
        + [pltpu.SemaphoreType.DMA((devices,))] * 4,
        compiler_params=pltpu.CompilerParams(
            collective_id=collective_id, has_side_effects=True, vmem_limit_bytes=VMEM_LIMIT
        ),
    )(held, *shards, gain_grad)


def update_kernel(rates, slot_ref, back_ref, *refs):
    masters, outs = refs[: len(rates)], refs[len(rates) :]
    block = 0
    for rate, master, out in zip(rates, masters, outs):
        bands, _, columns = master.shape
        for band in range(bands):
            for start in range(0, columns, BLOCK):
                here = slice(start, start + BLOCK)
                old = master[band, :, here]
                step = back_ref[slot_ref[block]].astype(float32)
                out[band, :, here] = old - rate * (step + weight_decay * old)
                block += 1


def update(masters, rates, places, back):
    vmem = pl.BlockSpec(memory_space=pltpu.VMEM)
    return pl.pallas_call(
        partial(update_kernel, rates),
        in_specs=[pl.BlockSpec(memory_space=pltpu.SMEM)] + [vmem] * (len(masters) + 1),
        out_specs=[vmem] * len(masters),
        out_shape=[jax.ShapeDtypeStruct(master.shape, float32) for master in masters],
        compiler_params=pltpu.CompilerParams(vmem_limit_bytes=VMEM_LIMIT),
    )(places, back, *masters)


def weight_grad_kernel(columns, band_rows, left_ref, *refs):
    right_refs, out_ref = refs[:-1], refs[-1]
    left = left_ref[...].T
    for at in range(0, len(columns), 2):
        blocks = []
        for spots in columns[at : at + 2]:
            right = [right_refs[i][g, :, start : start + size] for i, g, start, size in spots]
            right = right[0] if len(right) == 1 else jnp.concatenate(right, 1)
            block = jnp.dot(left, right, preferred_element_type=float32)
            blocks.append(block.astype(bfloat16).reshape(-1, band_rows, BLOCK))
        out_ref[:, at * band_rows : (at + 2) * band_rows, :] = jnp.concatenate(blocks, 1)


def weight_grad(left, rights, columns, device_count):
    tok_rows, height = left.shape
    band_rows = BLOCK // device_count
    bands, wide = height // BLOCK, len(columns)
    if band_rows % 8:
        right = [rights[i][g, :, start : start + n] for spots in columns for i, g, start, n in spots]
        right = jnp.concatenate(right, 1)
        product = jnp.einsum("td,te->de", left, right, preferred_element_type=float32)
        product = product.astype(bfloat16).reshape(bands, device_count, band_rows, wide, BLOCK)
        return product.transpose(1, 0, 3, 2, 4).reshape(device_count, -1, BLOCK)
    return pl.pallas_call(
        partial(weight_grad_kernel, columns, band_rows),
        grid=(bands,),
        in_specs=[
            pl.BlockSpec((tok_rows, BLOCK), lambda i: (0, i)),
        ]
        + [pl.BlockSpec(right.shape, lambda i: (0, 0, 0)) for right in rights],
        out_specs=pl.BlockSpec((device_count, wide * band_rows, BLOCK), lambda i: (0, i, 0)),
        out_shape=jax.ShapeDtypeStruct((device_count, bands * wide * band_rows, BLOCK), bfloat16),
        compiler_params=pltpu.CompilerParams(vmem_limit_bytes=VMEM_LIMIT),
        cost_estimate=pl.CostEstimate(
            flops=2 * tok_rows * bands * wide * BLOCK**2,
            bytes_accessed=2 * (tok_rows * (height + wide * BLOCK) + bands * wide * BLOCK**2),
            transcendentals=0,
        ),
    )(left, *rights)


def body(
    tokens,
    cotangent,
    lengths,
    owners,
    w_qkv,
    w_out,
    w_up,
    w_down,
    norm_gains,
    gain_first,
    gain_second,
    moment_first,
    moment_second,
    left_stat,
    right_stat,
    left_basis,
    right_basis,
):
    tok_rows, width = tokens.shape
    narrow_count = lax.axis_size("narrow")
    device_count = lax.axis_size("wide") * narrow_count
    seq_len = tok_rows * narrow_count
    cap_slots = moment_first.shape[0]
    masters = (w_qkv, w_out, w_up, w_down)
    lowered = tuple((layout.astype(jnp.bfloat16) for layout in masters)) + (
        norm_gains.astype(jnp.bfloat16),
    )
    share = norm_gains.shape[1]
    gains_low = jnp.pad(lowered[4], ((0, 6), (0, 128 - share)))[None]
    w_attn, gain_pair = gather_bands((lowered[0], gains_low), ((4, 2), (1, 1)), 3)
    w_attn = w_attn.reshape(width, 3 * width)
    gain_pair = gain_pair[0, :, :2, :share].transpose(1, 0, 2).reshape(2, width)
    gain_pair = gain_pair.astype(jnp.float32)
    w_proj, w_back = (
        gathered.reshape(-1, width)
        for gathered in lax.all_gather(lowered[1:4:2], ("wide", "narrow"), axis=1, tiled=True)
    )
    inputs = tokens.astype(jnp.float32)
    normed_one, inverse_one = normalize(inputs)
    act_one = (normed_one * gain_pair[0]).astype(jnp.bfloat16)
    head_width = width // narrow_count
    safe = seq_len - tok_rows
    packed = project(act_one, w_attn, narrow_count)
    halves = len(packed)
    scenes, merged, mixed, log_totals, w_hidden = attend(
        lengths, packed, safe, (lowered[2],), ((4, 2),), 4
    )
    w_hidden = w_hidden.reshape(width, FF)
    middle = inputs + jnp.dot(merged, w_proj, preferred_element_type=jnp.float32)
    normed_two, inverse_two = normalize(middle)
    act_two = (normed_two * gain_pair[1]).astype(jnp.bfloat16)
    block_out, d_act_two, d_w_hidden, d_back = feed_forward(
        act_two, cotangent, middle, w_hidden, w_back, device_count
    )
    d_norm_two, d_gain_two = norm_backward(d_act_two, normed_two, inverse_two, gain_pair[1])
    d_middle = cotangent.astype(jnp.float32) + d_norm_two
    d_branch = d_middle.astype(jnp.bfloat16)
    plain = lambda size: tuple(((0, 0, start, BLOCK),) for start in range(0, size, BLOCK))
    d_proj = weight_grad(merged, [d_branch[None]], plain(width), device_count)
    d_merged = jnp.einsum("te,de->td", d_branch, w_proj, preferred_element_type=jnp.float32).astype(
        jnp.bfloat16
    )
    ready = (d_w_hidden, d_back, d_proj)
    d_packed, hidden_sum, back_sum, proj_sum = attend_backward(
        lengths, scenes, mixed, d_merged, log_totals, safe, ready, (8, 8, 2), 5
    )
    d_packed = [d_packed[half] for half in range(halves)]
    grouped = tuple(
        tuple((half, group, third * PAIR, PAIR) for half in range(halves))
        for third in range(3)
        for group in range(narrow_count)
    )
    d_attn = weight_grad(act_one, d_packed, grouped, device_count)
    d_act_one = project_back(d_packed, w_attn)
    d_norm_one, d_gain_one = norm_backward(d_act_one, normed_one, inverse_one, gain_pair[0])
    grad_tokens = (d_middle + d_norm_one).astype(jnp.bfloat16)
    gain_parts = jnp.stack([d_gain_one, d_gain_two]).reshape(2, device_count, share)
    gain_parts = jnp.pad(gain_parts.transpose(1, 0, 2), ((0, 0), (0, 6), (0, 128 - share)))
    attn_sum, gain_grad = reduce_to_shards((d_attn, gain_parts), (6, 1), 1)
    band_rows = BLOCK // device_count
    block_count = owners.shape[0]
    order = lax.iota(jnp.int32, block_count)
    earlier = (owners[None, :] == owners[:, None]) & (order[None, :] < order[:, None])
    rank = jnp.sum(earlier.astype(jnp.int32), 1)
    slots = owners * cap_slots + rank
    every = lax.iota(jnp.int32, device_count * cap_slots)
    held = jnp.max(jnp.where(slots[None, :] == every[:, None], order[None, :], -1), 1)
    shards = [
        shard.reshape(-1, band_rows, BLOCK)
        for shard in (attn_sum, proj_sum, hidden_sum, back_sum)
    ]
    slot_grads, squares = ship(shards, gain_grad, held, cap_slots, 2)
    gain_grad = gain_grad[:2, :share]
    grad_norm = jnp.sqrt(squares[0, 0])
    factor = jnp.minimum(1.0, clip_bound / grad_norm)
    slot_grads = slot_grads.reshape(cap_slots, BLOCK, BLOCK)
    restored, first_new, second_new, left_new, right_new, gram, turn = soap_update(
        factor, slot_grads, moment_first, moment_second, left_stat, right_stat, left_basis, right_basis
    )
    square = (-1, BLOCK, BLOCK)
    bases = renew_bases(gram.reshape(square), turn.reshape(square))
    bases = bases.reshape(cap_slots, 2, BLOCK, BLOCK)
    left_turn, right_turn = bases[:, 0], bases[:, 1]
    returned = lax.all_to_all(
        shortened(restored.reshape(cap_slots, device_count, -1, BLOCK)),
        ("wide", "narrow"),
        split_axis=1,
        concat_axis=1,
        tiled=True,
    )
    fan_list = (2 * width, max(1, width * 16 // seq_len), width, FF)
    rates = tuple(fan_in ** (-0.5) for fan_in in fan_list)
    places = rank * device_count + owners
    updated = update(masters, rates, places, returned.reshape(-1, band_rows, BLOCK))
    clipped = gain_grad * factor
    gain_one_new = decay_rate * gain_first + (1.0 - decay_rate) * clipped
    gain_two_new = decay_rate * gain_second + (1.0 - decay_rate) * clipped * clipped
    correct = 1.0 - decay_rate**STEP
    gain_values = norm_gains - gain_rate * (gain_one_new / correct) / (
        jnp.sqrt(gain_two_new / correct) + eps_adam
    )
    return (
        block_out,
        grad_tokens,
        grad_norm,
        updated[0],
        updated[1],
        updated[2],
        updated[3],
        gain_values,
        gain_one_new,
        gain_two_new,
        first_new,
        second_new,
        left_new,
        right_new,
        left_turn,
        right_turn,
    )


def solution(mesh):
    in_specs = (
        P(("wide", "narrow"), None),
        P(("wide", "narrow"), None),
        P("wide"),
        P(),
        P(None, ("wide", "narrow"), None),
        P(None, ("wide", "narrow"), None),
        P(None, ("wide", "narrow"), None),
        P(None, ("wide", "narrow"), None),
        P(None, ("wide", "narrow")),
        P(None, ("wide", "narrow")),
        P(None, ("wide", "narrow")),
        P(("wide", "narrow"), None, None),
        P(("wide", "narrow"), None, None),
        P(("wide", "narrow"), None, None),
        P(("wide", "narrow"), None, None),
        P(("wide", "narrow"), None, None),
        P(("wide", "narrow"), None, None),
    )
    out_specs = (
        P(("wide", "narrow"), None),
        P(("wide", "narrow"), None),
        P(),
        P(None, ("wide", "narrow"), None),
        P(None, ("wide", "narrow"), None),
        P(None, ("wide", "narrow"), None),
        P(None, ("wide", "narrow"), None),
        P(None, ("wide", "narrow")),
        P(None, ("wide", "narrow")),
        P(None, ("wide", "narrow")),
        P(("wide", "narrow"), None, None),
        P(("wide", "narrow"), None, None),
        P(("wide", "narrow"), None, None),
        P(("wide", "narrow"), None, None),
        P(("wide", "narrow"), None, None),
        P(("wide", "narrow"), None, None),
    )
    return jax.shard_map(body, mesh=mesh, in_specs=in_specs, out_specs=out_specs, check_vma=False)
```

```python
from functools import partial

import jax
import jax.numpy as jnp
from jax import lax
from jax.experimental import pallas as pl
from jax.experimental.pallas import tpu as pltpu
from jax.sharding import PartitionSpec as P

FF = 4096
HEADS = 16
HEAD = 64
BLOCK = 256
STEP = 10


eps_norm = 1e-05
eps_adam = 1e-08
decay_rate = 0.5
clip_bound = 1.0
weight_decay = 0.01
gain_rate = 1.0
neg_large = -1e30
highest = lax.Precision.HIGHEST
float32 = jnp.float32
bfloat16 = jnp.bfloat16
PAIR = 2 * HEAD
NT = (((1,), (1,)), ((), ()))
TN = (((0,), (0,)), ((), ()))
MESH = pl.DeviceIdType.MESH
VMEM_LIMIT = 48 * 2**20
AHEAD = 8
SKEW = 3
ORDERS = ((0, 2, 1, None), (0, 1, 2, None), (0, 2, None, 1))
PACE = 3.7
DELAY = 12.0
GATHER_PACE = 6.0
GATHER_DELAY = 30.0
SETTLE_DELAY = 6.0
GELU = 0.7978845608
CUBIC = 0.044715


def shortened(shard):
    return jax.tree.map(lambda a: a.astype(jnp.bfloat16) if a.dtype == jnp.float32 else a, shard)


def normalize(values):
    center = values - jnp.mean(values, -1, keepdims=True)
    inverse = lax.rsqrt(jnp.mean(center * center, -1, keepdims=True) + eps_norm)
    return (center * inverse, inverse)


def norm_backward(d_result, normed, inverse, gain):
    scaled = d_result * gain
    d_gain = jnp.sum(d_result * normed, 0)
    d_input = inverse * (
        scaled
        - jnp.mean(scaled, -1, keepdims=True)
        - normed * jnp.mean(scaled * normed, -1, keepdims=True)
    )
    return (d_input, d_gain)


def one_head(matrix, head):
    lane = lax.broadcasted_iota(jnp.int32, matrix.shape, 1)
    return jnp.where(lane // HEAD == head, matrix, jnp.zeros_like(matrix))


def hide(scores, start, safe, length):
    if start + scores.shape[0] <= safe:
        return scores
    position = start + lax.broadcasted_iota(jnp.int32, scores.shape, 0)
    return jnp.where(position < length, scores, neg_large)


def project_kernel(acts_ref, wq_ref, wk_ref, wv_ref, *out_refs):
    thirds = (wq_ref, wk_ref, wv_ref)
    halves = len(out_refs)
    weights = jnp.concatenate(
        [third[:, h * PAIR : (h + 1) * PAIR] for h in range(halves) for third in thirds], 1
    )
    result = jnp.dot(acts_ref[...], weights, preferred_element_type=float32).astype(bfloat16)
    for h, out_ref in enumerate(out_refs):
        out_ref[0] = result[:, h * 3 * PAIR : (h + 1) * 3 * PAIR]


def project(acts, weights, groups):
    tok_rows, width = acts.shape
    head_width = width // groups
    halves = head_width // PAIR

    def third(k):
        return pl.BlockSpec((width, head_width), lambda g: (0, k * groups + g))

    return pl.pallas_call(
        project_kernel,
        grid=(groups,),
        in_specs=[pl.BlockSpec((tok_rows, width), lambda g: (0, 0)), third(0), third(1), third(2)],
        out_specs=[pl.BlockSpec((1, tok_rows, 3 * PAIR), lambda g: (g, 0, 0))] * halves,
        out_shape=[jax.ShapeDtypeStruct((groups, tok_rows, 3 * PAIR), bfloat16)] * halves,
        compiler_params=pltpu.CompilerParams(vmem_limit_bytes=VMEM_LIMIT),
        cost_estimate=pl.CostEstimate(
            flops=6 * tok_rows * width**2, bytes_accessed=6 * width**2 + 8 * tok_rows * width,
            transcendentals=0,
        ),
    )(acts, weights, weights, weights)


def project_back_kernel(halves, *refs):
    grads, (wq_ref, wk_ref, wv_ref, out_ref) = refs[:halves], refs[halves:]
    thirds = (wq_ref, wk_ref, wv_ref)
    weights = jnp.concatenate(
        [third[:, h * PAIR : (h + 1) * PAIR] for h in range(halves) for third in thirds], 1
    )
    rows = jnp.concatenate([grad[0] for grad in grads], 1)
    result = lax.dot_general(rows, weights, NT, preferred_element_type=float32)

    @pl.when(pl.program_id(0) == 0)
    def _():
        out_ref[...] = result

    @pl.when(pl.program_id(0) > 0)
    def _():
        out_ref[...] += result


def project_back(grads, weights):
    groups, tok_rows, _ = grads[0].shape
    width = weights.shape[0]
    head_width = width // groups

    def third(k):
        return pl.BlockSpec((width, head_width), lambda g: (0, k * groups + g))

    return pl.pallas_call(
        partial(project_back_kernel, len(grads)),
        grid=(groups,),
        in_specs=[pl.BlockSpec((1, tok_rows, 3 * PAIR), lambda g: (g, 0, 0))] * len(grads)
        + [third(0), third(1), third(2)],
        out_specs=pl.BlockSpec((tok_rows, width), lambda g: (0, 0)),
        out_shape=jax.ShapeDtypeStruct((tok_rows, width), float32),
        compiler_params=pltpu.CompilerParams(vmem_limit_bytes=VMEM_LIMIT),
        cost_estimate=pl.CostEstimate(
            flops=6 * tok_rows * width**2, bytes_accessed=6 * width**2 + 10 * tok_rows * width,
            transcendentals=0,
        ),
    )(*grads, weights, weights, weights)


def exact(left, right, dims=(((1,), (0,)), ((), ()))):
    return lax.dot_general(left, right, dims, precision=highest, preferred_element_type=float32)


def soap_kernel(
    factor_ref, g_ref, first_ref, second_ref, ls_ref, rs_ref, lb_ref, rb_ref,
    back_ref, first_out, second_out, ls_out, rs_out, gram_ref, turn_ref,
):
    factor = factor_ref[0, 0]
    rough = g_ref[0]
    gradient = factor * rough.astype(float32)
    half_square = (1.0 - decay_rate) * factor * factor
    left_base, right_base = lb_ref[0], rb_ref[0]
    left_square = lax.dot_general(rough, rough, NT, preferred_element_type=float32)
    right_square = jnp.dot(rough.T, rough, preferred_element_type=float32)
    left_new = decay_rate * ls_ref[0] + half_square * left_square
    right_new = decay_rate * rs_ref[0] + half_square * right_square
    ls_out[0] = left_new
    rs_out[0] = right_new
    turned = exact(left_base, exact(gradient, right_base), TN)
    first_new = decay_rate * first_ref[0] + (1.0 - decay_rate) * turned
    second_new = decay_rate * second_ref[0] + (1.0 - decay_rate) * turned * turned
    first_out[0] = first_new
    second_out[0] = second_new
    correct = 1.0 - decay_rate**STEP
    direction = first_new / correct / (jnp.sqrt(second_new / correct) + eps_adam)
    back_ref[0] = exact(left_base, exact(direction, right_base, NT)).astype(back_ref.dtype)
    for side, stat, base in ((0, left_new, left_base), (1, right_new, right_base)):
        turn = exact(stat, base).T
        turn_ref[0, side] = turn
        gram_ref[0, side] = exact(turn, turn, NT)


def soap_update(factor, gradient, first_old, second_old, left_old, right_old, left_base, right_base):
    slots, order, _ = gradient.shape
    one = pl.BlockSpec((1, order, order), lambda s: (s, 0, 0))
    two = pl.BlockSpec((1, 2, order, order), lambda s: (s, 0, 0, 0))
    single = jax.ShapeDtypeStruct((slots, order, order), float32)
    double = jax.ShapeDtypeStruct((slots, 2, order, order), float32)
    return pl.pallas_call(
        soap_kernel,
        grid=(slots,),
        in_specs=[pl.BlockSpec(memory_space=pltpu.SMEM)] + [one] * 7,
        out_specs=[one] * 5 + [two] * 2,
        out_shape=[jax.ShapeDtypeStruct((slots, order, order), bfloat16)] + [single] * 4 + [double] * 2,
        compiler_params=pltpu.CompilerParams(vmem_limit_bytes=VMEM_LIMIT),
        cost_estimate=pl.CostEstimate(
            flops=slots * 120 * order**3, bytes_accessed=slots * 60 * order**2, transcendentals=0
        ),
    )(factor.reshape(1, 1), gradient, first_old, second_old, left_old, right_old, left_base, right_base)


def renew_kernel(rows, gram_ref, turn_ref, left_ref, right_ref, x_ref, u_ref):
    count, order = gram_ref.shape[0], gram_ref.shape[1]
    eye = (
        lax.broadcasted_iota(jnp.int32, (rows, rows), 0)
        == lax.broadcasted_iota(jnp.int32, (rows, rows), 1)
    ).astype(float32)
    sublane = lax.broadcasted_iota(jnp.int32, (1, 8, 1), 1)
    for low in range(0, order, rows):
        part = slice(low, low + rows)

        def panel(at, carry, low=low, part=part):
            row = jnp.concatenate([gram_ref[at, part, :], turn_ref[at, part, :]], 1)
            if low:
                row = row - exact(u_ref[at, :low, part], u_ref[at, :low, :], TN)
            u_ref[at, part, :] = row
            x_ref[at] = jnp.concatenate([row[:, part], eye], 1)
            return carry

        lax.fori_loop(0, count, panel, 0, unroll=2)
        for j in range(rows):
            tile = j // 8 * 8
            row = x_ref[:, j : j + 1, :]
            row = row * (1.0 / row[:, :, j : j + 1])
            top = x_ref[:, tile : tile + 8, :]
            below = jnp.where(sublane > j - tile, top[:, :, j : j + 1], 0.0)
            x_ref[:, tile : tile + 8, :] = top - below * row
            if tile + 8 < rows:
                rest = x_ref[:, tile + 8 :, :]
                x_ref[:, tile + 8 :, :] = rest - rest[:, :, j : j + 1] * row

        def solve(at, carry, part=part):
            both = x_ref[at]
            diagonal = jnp.sum(both[:, :rows] * eye, 1, keepdims=True)
            u_ref[at, part, :] = exact(both[:, rows:] * lax.rsqrt(diagonal), u_ref[at, part, :])
            return carry

        lax.fori_loop(0, count, solve, 0, unroll=2)

    def turn_back(at, carry):
        left_ref[at] = u_ref[2 * at, :, order:].T
        right_ref[at] = u_ref[2 * at + 1, :, order:].T
        return carry

    lax.fori_loop(0, count // 2, turn_back, 0)


def renew_bases(gram, turn, rows=64):
    count, order, _ = gram.shape
    return pl.pallas_call(
        partial(renew_kernel, rows),
        out_shape=[jax.ShapeDtypeStruct((count // 2, order, order), float32)] * 2,
        in_specs=[pl.BlockSpec(memory_space=pltpu.VMEM)] * 2,
        out_specs=[pl.BlockSpec(memory_space=pltpu.VMEM)] * 2,
        scratch_shapes=[
            pltpu.VMEM((count, rows, 2 * rows), float32),
            pltpu.VMEM((count, order, 2 * order), float32),
        ],
        compiler_params=pltpu.CompilerParams(vmem_limit_bytes=VMEM_LIMIT),
        cost_estimate=pl.CostEstimate(
            flops=count * 200 * order**3, bytes_accessed=count * 12 * order**2, transcendentals=0
        ),
    )(gram, turn)


def partner(bit, narrow_bits):
    axis, step = ("narrow", 1 << bit) if bit < narrow_bits else ("wide", 1 << (bit - narrow_bits))
    place = lax.axis_index(axis)
    mine = lax.rem(place // step, 2)
    return {axis: place + step - 2 * step * mine}, mine


def greet(peers):
    barrier = pltpu.get_barrier_semaphore()
    for device, _ in peers:
        pl.semaphore_signal(barrier, inc=1, device_id=device, device_id_type=MESH)
    pl.semaphore_wait(barrier, len(peers))


def mesh_bits():
    narrow_bits = lax.axis_size("narrow").bit_length() - 1
    return narrow_bits + lax.axis_size("wide").bit_length() - 1, narrow_bits


def reduce_steps(bits, narrow_bits, plans, chunks, sources, outs, scratch):
    count = len(sources)
    held = scratch[:count]
    arrived = [scratch[count * (1 + s) : count * (2 + s)] for s in range(bits)]
    load_sem, send_sem, recv_sem = scratch[count * (1 + bits) :]
    peers = [partner(b, narrow_bits) for b in range(bits)]
    first = plans[0][0]
    order_of_dims = list(reversed(range(bits)))
    whole = slice(None)

    def within(order, stage, current):
        return tuple(
            peers[b][1] if b in order[:stage] else current if b == order[stage] else whole
            for b in order_of_dims
            if b != first
        )

    def of_source(value):
        return tuple(value if b == first else whole for b in order_of_dims)

    def rows_of(chunk):
        at, row, rows, colour = chunks[chunk]
        return at, plans[colour], (pl.ds(row, rows), whole)

    def send(chunk, stage):
        at, order, part = rows_of(chunk)
        device, mine = peers[order[stage]]
        if stage == 0:
            source = sources[at].at[of_source(1 - mine) + part]
        else:
            source = held[at].at[within(order, stage, 1 - mine) + part]
        return pltpu.make_async_remote_copy(
            src_ref=source,
            dst_ref=arrived[stage][at].at[(whole,) * (bits - 1 - stage) + part],
            send_sem=send_sem.at[chunk, stage],
            recv_sem=recv_sem.at[chunk, stage],
            device_id=device,
            device_id_type=MESH,
        )

    def load(chunk):
        at, order, part = rows_of(chunk)
        return pltpu.make_async_copy(
            sources[at].at[of_source(peers[first][1]) + part],
            held[at].at[(whole,) * (bits - 1) + part],
            load_sem.at[chunk],
        )

    def begin(chunk):
        send(chunk, 0).start()
        load(chunk).start()

    def finish(chunk, stage):
        at, order, part = rows_of(chunk)
        if stage == 0:
            load(chunk).wait()
        send(chunk, stage).wait_recv()
        left = bits - 1 - stage
        keep = within(order, stage, peers[order[stage]][1])
        if left == 0:
            own = held[at][keep + part].astype(float32)
            outs[at][part] = own + arrived[stage][at][part].astype(float32)
            return
        free = [i for i, k in enumerate(keep) if isinstance(k, slice)]

        def add(m, carry):
            which = tuple(m // (1 << (left - 1 - i)) % 2 for i in range(left))
            spot = list(keep)
            for i, f in enumerate(free):
                spot[f] = which[i]
            spot = tuple(spot) + part
            held[at][spot] = held[at][spot] + arrived[stage][at][which + part]
            return carry

        lax.fori_loop(0, 1 << left, add, 0)
        send(chunk, stage + 1).start()

    def drain():
        for chunk in range(len(chunks)):
            for stage in range(bits):
                send(chunk, stage).wait_send()

    return peers, begin, finish, drain


def reduce_kernel(bits, narrow_bits, plans, chunks, count, *refs):
    peers, begin, finish, drain = reduce_steps(
        bits, narrow_bits, plans, chunks, refs[:count], refs[count : 2 * count], refs[2 * count :]
    )
    greet(peers)
    total = len(chunks)
    for chunk in range(min(AHEAD, total)):
        begin(chunk)
    for step in range(total + 2 * bits):
        for stage in reversed(range(bits)):
            chunk = step - 2 * stage
            if 0 <= chunk < total:
                finish(chunk, stage)
                if stage == 0 and chunk + AHEAD < total:
                    begin(chunk + AHEAD)
    drain()


def slot_table(chunks, bits, slots, pace, delay):
    table = [[] for _ in range(slots + 1)]
    done = sorted(
        (chunk * pace + (stage + 1) * delay, -stage, chunk, stage)
        for chunk in range(chunks)
        for stage in range(bits)
    )
    for when, _, chunk, stage in done:
        table[min(int(when), slots)].append((chunk, stage))
    return table


def reduce_plan(parts, pieces, orders=None):
    orders = ORDERS if orders is None else orders
    bits, narrow_bits = mesh_bits()
    shapes = [part.shape[1:] for part in parts]
    kinds = [part.dtype for part in parts]
    chunks = []
    for at, (shape, cut) in enumerate(zip(shapes, pieces)):
        rows = shape[0] // cut
        for row in range(0, shape[0], rows):
            chunks.append((at, row, rows, len(chunks) % len(orders)))
    later = tuple(range(3, bits))
    plans = tuple(tuple(b for part in order for b in (later if part is None else (part,))) for order in orders)
    sizes = [bits - 1] + [bits - 1 - stage for stage in range(bits)]
    scratch = [
        pltpu.VMEM((2,) * size + shape, kind)
        for size in sizes
        for shape, kind in zip(shapes, kinds)
    ]
    total = len(chunks)
    scratch += [
        pltpu.SemaphoreType.DMA((total,)),
        pltpu.SemaphoreType.DMA((total, bits)),
        pltpu.SemaphoreType.DMA((total, bits)),
    ]
    outs = [jax.ShapeDtypeStruct(shape, float32) for shape in shapes]
    halved = [
        part.reshape((2,) * bits + shape) if hasattr(part, "reshape") else part
        for part, shape in zip(parts, shapes)
    ]
    return bits, narrow_bits, plans, tuple(chunks), halved, outs, scratch


def reduce_to_shards(parts, pieces, collective_id):
    bits, narrow_bits, plans, chunks, halved, outs, scratch = reduce_plan(parts, pieces)
    return pl.pallas_call(
        partial(reduce_kernel, bits, narrow_bits, plans, chunks, len(parts)),
        out_shape=outs,
        in_specs=[pl.BlockSpec(memory_space=pl.ANY)] * len(parts),
        out_specs=[pl.BlockSpec(memory_space=pltpu.VMEM)] * len(parts),
        scratch_shapes=scratch,
        compiler_params=pltpu.CompilerParams(
            collective_id=collective_id, has_side_effects=True, vmem_limit_bytes=58 * 2**20
        ),
        cost_estimate=pl.CostEstimate(flops=10**8, bytes_accessed=4 * 10**8, transcendentals=0),
    )(*halved)


def gather_steps(bits, narrow_bits, plans, chunks, sources, outs, scratch):
    own_sem, send_sem, recv_sem = scratch
    peers = [partner(b, narrow_bits) for b in range(bits)]
    dims = list(reversed(range(bits)))

    def place(chunk, stage):
        at, band, bands, col, cols, colour = chunks[chunk]
        done = plans[colour][:stage]
        index = tuple(slice(None) if b in done else peers[b][1] for b in dims)
        return outs[at].at[(pl.ds(band, bands),) + index + (slice(None), pl.ds(col, cols))]

    def own(chunk):
        at, band, bands, col, cols, colour = chunks[chunk]
        return sources[at].at[pl.ds(band, bands), :, pl.ds(col, cols)]

    def send(chunk, stage):
        colour = chunks[chunk][-1]
        target = place(chunk, stage)
        return pltpu.make_async_remote_copy(
            src_ref=target if stage else own(chunk),
            dst_ref=target,
            send_sem=send_sem.at[chunk, stage],
            recv_sem=recv_sem.at[chunk, stage],
            device_id=peers[plans[colour][stage]][0],
            device_id_type=MESH,
        )

    def keep(chunk):
        return pltpu.make_async_copy(own(chunk), place(chunk, 0), own_sem.at[chunk])

    def begin(chunk):
        send(chunk, 0).start()
        keep(chunk).start()

    def finish(chunk, stage):
        if stage == 0:
            keep(chunk).wait()
        send(chunk, stage).wait_recv()
        if stage + 1 < bits:
            send(chunk, stage + 1).start()

    def drain():
        for chunk in range(len(chunks)):
            for stage in range(bits):
                send(chunk, stage).wait_send()

    return peers, begin, finish, drain


def gather_kernel(bits, narrow_bits, plans, chunks, count, *refs):
    peers, begin, finish, drain = gather_steps(
        bits, narrow_bits, plans, chunks, refs[:count], refs[count : 2 * count], refs[2 * count :]
    )
    greet(peers)
    total = len(chunks)
    for chunk in range(total):
        begin(chunk)
    for step in range(total + SKEW * bits):
        for stage in reversed(range(bits)):
            chunk = step - SKEW * stage
            if 0 <= chunk < total:
                finish(chunk, stage)
    drain()


def gather_plan(parts, pieces):
    bits, narrow_bits = mesh_bits()
    chunks = []
    for at, (part, (cut, cut_cols)) in enumerate(zip(parts, pieces)):
        bands, cols = part.shape[0] // cut, part.shape[2] // cut_cols
        for band in range(0, part.shape[0], bands):
            for col in range(0, part.shape[2], cols):
                chunks.append((at, band, bands, col, cols, len(chunks) % 2))
    later = tuple(reversed(range(3, bits)))
    plans = (later + (1, 2, 0), later + (2, 1, 0))
    total = len(chunks)
    outs = [
        jax.ShapeDtypeStruct(part.shape[:1] + (2,) * bits + part.shape[1:], part.dtype)
        for part in parts
    ]
    scratch = [
        pltpu.SemaphoreType.DMA((total,)),
        pltpu.SemaphoreType.DMA((total, bits)),
        pltpu.SemaphoreType.DMA((total, bits)),
    ]
    return bits, narrow_bits, plans, tuple(chunks), outs, scratch


def gather_bands(parts, pieces, collective_id):
    bits, narrow_bits, plans, chunks, outs, scratch = gather_plan(parts, pieces)
    results = pl.pallas_call(
        partial(gather_kernel, bits, narrow_bits, plans, chunks, len(parts)),
        out_shape=outs,
        in_specs=[pl.BlockSpec(memory_space=pl.ANY)] * len(parts),
        out_specs=[pl.BlockSpec(memory_space=pl.ANY)] * len(parts),
        scratch_shapes=scratch,
        compiler_params=pltpu.CompilerParams(collective_id=collective_id, has_side_effects=True),
        cost_estimate=pl.CostEstimate(flops=0, bytes_accessed=10**8, transcendentals=0),
    )(*parts)
    return [
        result.reshape(part.shape[:1] + (1 << bits,) + part.shape[1:])
        for result, part in zip(results, parts)
    ]


def group_peers():
    count = lax.axis_size("narrow")
    me = lax.axis_index("narrow")
    return me, [({"narrow": lax.rem(me + d, count)}, lax.rem(me + d, count)) for d in range(count)]


def rows_at(place, rows):
    return pl.ds(pl.multiple_of(place * rows, rows), rows)


def attend_kernel(safe, chunk, halves, plan, slots, length_ref, *refs):
    count = plan[4]
    packed, sources = refs[:halves], refs[halves : halves + count]
    refs = refs[halves + count :]
    scenes_out, merged, mixed_out, log_ref = refs[:4]
    scene_ref, o_ref, vt_ref, s_ref, near_sem, in_sem, back_sem, out_sem = refs[4 + count : 12 + count]
    others, begin, finish, drain = gather_steps(
        *plan[:4], sources, refs[4 : 4 + count], refs[12 + count :]
    )
    seq_len = scene_ref.shape[1]
    me, peers = group_peers()
    devices = len(peers)
    tok_rows = seq_len // devices
    length = length_ref[0]
    half, step = pl.program_id(0), pl.program_id(1)
    last = pl.num_programs(1) - 1
    own = rows_at(me, tok_rows)

    def bring(h, d):
        device, place = peers[d]
        if d == 0:
            return pltpu.make_async_copy(packed[h].at[me], scene_ref.at[h, own], in_sem.at[h, 0])
        return pltpu.make_async_remote_copy(
            src_ref=packed[h].at[place],
            dst_ref=scene_ref.at[h, own],
            send_sem=near_sem.at[h, d],
            recv_sem=in_sem.at[h, d],
            device_id=device,
            device_id_type=MESH,
        )

    def give(h, d, at, to, sender):
        column = pl.ds(pl.multiple_of((sender * halves + h) * PAIR, PAIR), PAIR)
        target = merged.at[:, column]
        source = o_ref.at[h, rows_at(to, tok_rows)]
        if d == 0:
            return pltpu.make_async_copy(source, target, out_sem.at[h, 0])
        return pltpu.make_async_remote_copy(
            src_ref=source,
            dst_ref=target,
            send_sem=back_sem.at[h, d],
            recv_sem=out_sem.at[h, d],
            device_id={"narrow": to},
            device_id_type=MESH,
        )

    def save_scene(h):
        return pltpu.make_async_copy(scene_ref.at[h], scenes_out.at[h], near_sem.at[h, 0])

    def save_mixed(h):
        return pltpu.make_async_copy(o_ref.at[h], mixed_out.at[h], back_sem.at[h, 0])

    @pl.when((half == 0) & (step == 0))
    def _():
        greet(peers[1:] + others[plan[1] :])
        for d in range(devices):
            bring(0, d).start()
        for which in range(len(plan[3])):
            begin(which)

    for h in range(halves):

        @pl.when((half == h) & (step == 0))
        def _(h=h):
            for d in range(devices):
                if d:
                    bring(h, d).wait_recv()
                else:
                    bring(h, d).wait()
            if h + 1 < halves:
                for d in range(devices):
                    bring(h + 1, d).start()
            save_scene(h).start()
            vt_ref[...] = scene_ref[h, :, 2 * PAIR :].T

    points = 2 * seq_len // chunk

    def move_at(point):
        for h in range(halves):
            for s in range(devices):
                todo = slots[(h * devices + s) * 2 * points + point]
                if todo:

                    @pl.when((half == h) & (step == s))
                    def _(todo=todo):
                        for which, stage in todo:
                            finish(which, stage)

    to = lax.rem(me + 1 + step, devices)
    here = rows_at(to, tok_rows)
    outs = []
    for head in range(2):
        queries = one_head(scene_ref[half, here, :PAIR], head) * bfloat16(HEAD**-0.5)
        topmost = None
        for at in range(0, seq_len, chunk):
            move_at(head * points + at // chunk)
            scores = lax.dot_general(
                scene_ref[half, at : at + chunk, PAIR : 2 * PAIR],
                queries,
                NT,
                preferred_element_type=float32,
            )
            scores = hide(scores, at, safe, length)
            s_ref[head, at : at + chunk, :] = scores
            top = jnp.max(scores, 0, keepdims=True)
            topmost = top if topmost is None else jnp.maximum(topmost, top)
        totals = jnp.zeros_like(topmost)
        mixed = jnp.zeros((HEAD, tok_rows), float32)
        for at in range(0, seq_len, chunk):
            move_at(head * points + points // 2 + at // chunk)
            expo = jnp.exp(s_ref[head, at : at + chunk, :] - topmost)
            totals += jnp.sum(expo, 0, keepdims=True)
            mixed += jnp.dot(
                vt_ref[head * HEAD : (head + 1) * HEAD, at : at + chunk],
                expo.astype(bfloat16),
                preferred_element_type=float32,
            )
        outs.append(mixed * (1.0 / totals))
        log_ref[half, head : head + 1, here] = topmost + jnp.log(totals)
    o_ref[half, here, :] = jnp.concatenate(outs, 0).T.astype(bfloat16)

    for h in range(halves):
        for s in range(devices):

            @pl.when((half == h) & (step == s))
            def _(h=h, s=s):
                d = (s + 1) % devices
                give(h, d, s, lax.rem(me + d, devices), me).start()
                if s == devices - 1:
                    save_mixed(h).start()

    @pl.when((half == halves - 1) & (step == last))
    def _():
        for which, stage in slots[-1]:
            finish(which, stage)
        drain()
        for h in range(halves):
            for d in range(devices):
                if d:
                    bring(h, d).wait_send()
                    sender = lax.rem(me + devices - d, devices)
                    arriving = give(h, d, d, lax.rem(me + d, devices), sender)
                    arriving.wait_recv()
                    arriving.wait_send()
                else:
                    give(h, 0, 0, me, me).wait()
            save_scene(h).wait()
            save_mixed(h).wait()


def attend(lengths, packed, safe, parts, pieces, collective_id, chunk=512):
    devices, tok_rows, _ = packed[0].shape
    halves, seq_len = len(packed), devices * tok_rows
    width = devices * halves * PAIR
    anywhere = pl.BlockSpec(memory_space=pl.ANY)
    bits, narrow_bits, plans, chunks, outs, scratch = gather_plan(parts, pieces)
    slots = slot_table(
        len(chunks), bits, halves * devices * 4 * (seq_len // chunk), GATHER_PACE, GATHER_DELAY
    )
    plan = (bits, narrow_bits, plans, chunks, len(parts))
    results = pl.pallas_call(
        partial(attend_kernel, safe, chunk, halves, plan, slots),
        grid=(halves, devices),
        in_specs=[pl.BlockSpec(memory_space=pltpu.SMEM)] + [anywhere] * (halves + len(parts)),
        out_specs=[anywhere] * 3
        + [pl.BlockSpec((halves, 2, seq_len), lambda p, i: (0, 0, 0))]
        + [anywhere] * len(parts),
        out_shape=[
            jax.ShapeDtypeStruct((halves, seq_len, 3 * PAIR), bfloat16),
            jax.ShapeDtypeStruct((tok_rows, width), bfloat16),
            jax.ShapeDtypeStruct((halves, seq_len, PAIR), bfloat16),
            jax.ShapeDtypeStruct((halves, 2, seq_len), float32),
        ]
        + outs,
        scratch_shapes=[
            pltpu.VMEM((halves, seq_len, 3 * PAIR), bfloat16),
            pltpu.VMEM((halves, seq_len, PAIR), bfloat16),
            pltpu.VMEM((PAIR, seq_len), bfloat16),
            pltpu.VMEM((2, seq_len, tok_rows), float32),
        ]
        + [pltpu.SemaphoreType.DMA((halves, devices))] * 4
        + scratch,
        compiler_params=pltpu.CompilerParams(
            collective_id=collective_id, has_side_effects=True, vmem_limit_bytes=VMEM_LIMIT
        ),
        cost_estimate=pl.CostEstimate(
            flops=4 * halves * 2 * 4 * seq_len * seq_len * HEAD,
            bytes_accessed=16 * seq_len * PAIR * halves,
            transcendentals=0,
        ),
    )(lengths, *packed, *parts)
    gathered = [
        result.reshape(part.shape[0], 1 << bits, *part.shape[1:])
        for result, part in zip(results[4:], parts)
    ]
    return list(results[:4]) + gathered


def attend_backward_kernel(
    safe, chunk, halves, plan, slots, length_ref, scene_ref, o_ref, log_ref, d_merged, *refs
):
    count = plan[4]
    sources, packed_out, outs = refs[:count], refs[count], refs[count + 1 : 2 * count + 1]
    do_ref, stage_ref, kt_ref, dk_sum, dv_sum = refs[2 * count + 1 : 2 * count + 6]
    near_sem, in_sem, q_send, q_recv, kv_send, kv_recv = refs[2 * count + 6 : 2 * count + 12]
    others, begin, finish, drain = reduce_steps(*plan[:4], sources, outs, refs[2 * count + 12 :])
    total = len(plan[3])
    me, peers = group_peers()
    devices = len(peers)
    seq_len = scene_ref.shape[1]
    tok_rows = seq_len // devices
    length = length_ref[0]
    half, step = pl.program_id(0), pl.program_id(1)
    own = rows_at(me, tok_rows)
    chunks = seq_len // chunk

    def move(which, stage):
        finish(which, stage)
        if stage == 0 and which + AHEAD < total:
            begin(which + AHEAD)

    def move_at(head, part):
        for h in range(halves):
            for s in range(devices):
                todo = slots[((h * devices + s) * 2 + head) * chunks + part]
                if todo:

                    @pl.when((half == h) & (step == s))
                    def _(todo=todo):
                        for which, stage in todo:
                            move(which, stage)

    def bring(h, d):
        device, place = peers[d]
        column = pl.ds(pl.multiple_of((place * halves + h) * PAIR, PAIR), PAIR)
        source, target = d_merged.at[:, column], do_ref.at[h, own]
        if d == 0:
            return pltpu.make_async_copy(source, target, in_sem.at[h, 0])
        return pltpu.make_async_remote_copy(
            src_ref=source,
            dst_ref=target,
            send_sem=near_sem.at[h, d],
            recv_sem=in_sem.at[h, d],
            device_id=device,
            device_id_type=MESH,
        )

    def give(h, d, columns, send_sem, recv_sem, sender):
        device, place = peers[d]
        source = stage_ref.at[h, rows_at(place, tok_rows), columns]
        target = packed_out.at[h, sender, :, columns]
        if d == 0:
            return pltpu.make_async_copy(source, target, recv_sem.at[h, 0])
        return pltpu.make_async_remote_copy(
            src_ref=source,
            dst_ref=target,
            send_sem=send_sem.at[h, d],
            recv_sem=recv_sem.at[h, d],
            device_id=device,
            device_id_type=MESH,
        )

    q_columns, kv_columns = pl.ds(0, PAIR), pl.ds(PAIR, 2 * PAIR)

    @pl.when((half == 0) & (step == 0))
    def _():
        narrow_bits = plan[1]
        greet(peers[1:] + others[narrow_bits:])
        for h in range(halves):
            for d in range(devices):
                bring(h, d).start()
        for which in range(min(AHEAD, total)):
            begin(which)

    for h in range(halves):

        @pl.when((half == h) & (step == 0))
        def _(h=h):
            kt_ref[...] = scene_ref[0, :, PAIR : 2 * PAIR].T
            dk_sum[...] = jnp.zeros_like(dk_sum)
            dv_sum[...] = jnp.zeros_like(dv_sum)
            for d in range(devices):
                if d:
                    bring(h, d).wait_recv()
                else:
                    bring(h, d).wait()

    here = rows_at(lax.rem(me + 1 + step, devices), tok_rows)
    products = (o_ref[0, here, :].astype(float32) * do_ref[half, here, :].astype(float32)).T
    turned = []
    for head in range(2):
        lanes = slice(head * HEAD, (head + 1) * HEAD)
        queries = one_head(scene_ref[0, here, :PAIR], head) * bfloat16(HEAD**-0.5)
        d_mixed = one_head(do_ref[half, here, :], head)
        inner = jnp.sum(products[lanes, :], 0, keepdims=True)
        log_total = log_ref[0, head : head + 1, here]
        d_queries = jnp.zeros((HEAD, tok_rows), float32)
        for index in range(chunks):
            move_at(head, index)
            at = index * chunk
            part = slice(at, at + chunk)
            scores = lax.dot_general(
                scene_ref[0, part, PAIR : 2 * PAIR], queries, NT, preferred_element_type=float32
            )
            probs = jnp.exp(hide(scores, at, safe, length) - log_total)
            d_probs = lax.dot_general(
                scene_ref[0, part, 2 * PAIR :], d_mixed, NT, preferred_element_type=float32
            )
            dv_sum[part, :] += jnp.dot(
                probs.astype(bfloat16), d_mixed, preferred_element_type=float32
            )
            d_scores = (probs * (d_probs - inner)).astype(bfloat16)
            dk_sum[part, :] += jnp.dot(d_scores, queries, preferred_element_type=float32)
            d_queries += jnp.dot(kt_ref[lanes, part], d_scores, preferred_element_type=float32)
        turned.append(d_queries * HEAD**-0.5)
    stage_ref[half, here, :PAIR] = jnp.concatenate(turned, 0).T.astype(bfloat16)

    for h in range(halves):
        for s in range(devices):

            @pl.when((half == h) & (step == s))
            def _(h=h, s=s):
                give(h, (s + 1) % devices, q_columns, q_send, q_recv, me).start()
                if s == devices - 1:
                    stage_ref[h, :, PAIR : 2 * PAIR] = dk_sum[...].astype(bfloat16)
                    stage_ref[h, :, 2 * PAIR :] = dv_sum[...].astype(bfloat16)
                    for d in range(devices):
                        give(h, d, kv_columns, kv_send, kv_recv, me).start()

    @pl.when((half == halves - 1) & (step == devices - 1))
    def _():
        for which, stage in slots[-1]:
            move(which, stage)
        drain()
        for h in range(halves):
            for d in range(devices):
                for columns, send_sem, recv_sem in (
                    (q_columns, q_send, q_recv),
                    (kv_columns, kv_send, kv_recv),
                ):
                    sender = lax.rem(me + devices - d, devices)
                    copy = give(h, d, columns, send_sem, recv_sem, sender)
                    if d:
                        copy.wait_recv()
                        copy.wait_send()
                    else:
                        copy.wait()
                if d:
                    bring(h, d).wait_send()


def attend_backward(
    lengths, scenes, mixed, d_merged, log_totals, safe, parts, pieces, collective_id, chunk=512
):
    halves, seq_len, _ = scenes.shape
    devices = lax.axis_size("narrow")
    tok_rows = seq_len // devices
    bits, narrow_bits, plans, chunks, halved, outs, scratch = reduce_plan(parts, pieces)
    slots = slot_table(
        len(chunks), bits, halves * devices * 2 * (seq_len // chunk), PACE, DELAY
    )
    anywhere = pl.BlockSpec(memory_space=pl.ANY)

    def of_half(array):
        return pl.BlockSpec((1,) + array.shape[1:], lambda p, i: (p, 0, 0))

    return pl.pallas_call(
        partial(
            attend_backward_kernel,
            safe,
            chunk,
            halves,
            (bits, narrow_bits, plans, chunks, len(parts)),
            slots,
        ),
        grid=(halves, devices),
        in_specs=[
            pl.BlockSpec(memory_space=pltpu.SMEM),
            of_half(scenes),
            of_half(mixed),
            of_half(log_totals),
            anywhere,
        ]
        + [anywhere] * len(parts),
        out_specs=[anywhere] + [pl.BlockSpec(out.shape, lambda p, i: (0, 0)) for out in outs],
        out_shape=[jax.ShapeDtypeStruct((halves, devices, tok_rows, 3 * PAIR), bfloat16)] + outs,
        scratch_shapes=[
            pltpu.VMEM((halves, seq_len, PAIR), bfloat16),
            pltpu.VMEM((halves, seq_len, 3 * PAIR), bfloat16),
            pltpu.VMEM((PAIR, seq_len), bfloat16),
            pltpu.VMEM((seq_len, PAIR), float32),
            pltpu.VMEM((seq_len, PAIR), float32),
        ]
        + [pltpu.SemaphoreType.DMA((halves, devices))] * 6
        + scratch,
        compiler_params=pltpu.CompilerParams(
            collective_id=collective_id, has_side_effects=True, vmem_limit_bytes=60 * 2**20
        ),
        cost_estimate=pl.CostEstimate(
            flops=4 * halves * 2 * 10 * seq_len * seq_len * HEAD,
            bytes_accessed=32 * seq_len * PAIR,
            transcendentals=0,
        ),
    )(lengths, scenes, mixed, log_totals, d_merged, *halved)


def settle_kernel(plan, acts_ref, grads_ref, weights_ref, sum_ref, back_ref, right_ref, left_ref, dealt, *scratch):
    bits = plan[0]
    halves, groups, tok_rows, _ = grads_ref.shape
    width = acts_ref.shape[1]
    bands = width // BLOCK
    chunks = plan[3]
    peers, begin, finish, drain = reduce_steps(*plan[:4], [dealt], [sum_ref], scratch)
    left_ref[...] = acts_ref[...].T
    blocks = 3 * width // BLOCK
    for half in range(halves):
        for group in range(groups):
            for third in range(3):
                start = third * width + (group * halves + half) * PAIR
                right_ref[:, start : start + PAIR] = grads_ref[
                    half, group, :, third * PAIR : (third + 1) * PAIR
                ]
    rows = BLOCK >> bits

    def band_product(band):
        left = left_ref[band * BLOCK : (band + 1) * BLOCK, :]
        for at in range(0, blocks, 2):
            pair = jnp.dot(
                left, right_ref[:, at * BLOCK : (at + 2) * BLOCK], preferred_element_type=float32
            ).astype(bfloat16)
            pair = [pair[:, h * BLOCK : (h + 1) * BLOCK].reshape(-1, rows, BLOCK) for h in range(2)]
            low = (band * blocks + at) * rows
            both = jnp.concatenate(pair, 1)
            dealt[(slice(None),) * bits + (slice(low, low + 2 * rows),)] = both.reshape(
                (2,) * bits + both.shape[1:]
            )

    def back_product(band):
        here = slice(band * BLOCK, (band + 1) * BLOCK)
        back_ref[:, here] = lax.dot_general(
            right_ref[...], weights_ref[here, :], NT, preferred_element_type=float32
        )

    each = len(chunks) // bands
    work = [(2.5 * band, -1, band, -1) for band in range(2 * bands)]
    for chunk in range(len(chunks)):
        for stage in range(bits):
            ready = max(2.5 * (chunk // each + 1), 3.5 * chunk)
            work.append((ready + SETTLE_DELAY * (stage + 1), -stage, chunk, stage))
    for _, _, which, stage in sorted(work):
        if stage >= 0:
            finish(which, stage)
        elif which < bands:
            band_product(which)
            if which == 0:
                greet(peers)
            for chunk in range(which * each, (which + 1) * each):
                begin(chunk)
        else:
            back_product(which - bands)
    drain()


def settle(acts, grads, weights, device_count, collective_id):
    tok_rows, width = acts.shape
    rows = 3 * width * width // BLOCK // device_count
    dealt = jax.ShapeDtypeStruct((device_count, rows, BLOCK), bfloat16)
    bits, narrow_bits, plans, chunks, _, outs, scratch = reduce_plan(
        [dealt], (2 * width // BLOCK,), ORDERS[:2]
    )
    vmem = pl.BlockSpec(memory_space=pltpu.VMEM)
    return pl.pallas_call(
        partial(settle_kernel, (bits, narrow_bits, plans, chunks)),
        in_specs=[vmem] * 3,
        out_specs=[vmem] * 2,
        out_shape=outs + [jax.ShapeDtypeStruct((tok_rows, width), float32)],
        scratch_shapes=[
            pltpu.VMEM((tok_rows, 3 * width), bfloat16),
            pltpu.VMEM((width, tok_rows), bfloat16),
            pltpu.VMEM((2,) * bits + (rows, BLOCK), bfloat16),
        ]
        + scratch,
        compiler_params=pltpu.CompilerParams(
            collective_id=collective_id, has_side_effects=True, vmem_limit_bytes=60 * 2**20
        ),
        cost_estimate=pl.CostEstimate(
            flops=12 * tok_rows * width**2, bytes_accessed=10**8, transcendentals=0
        ),
    )(acts, grads, weights)


def feed_kernel(deal, acts_ref, grad_ref, middle_ref, up_ref, down_ref, out_ref, back_ref, one_ref, two_ref, turned_ref, sum_ref):
    at, last = pl.program_id(0), pl.num_programs(0) - 1

    @pl.when(at == 0)
    def _():
        sum_ref[...] = middle_ref[...]
        back_ref[...] = jnp.zeros_like(back_ref)
        turned_ref[...] = acts_ref[...].T

    acts, grad = acts_ref[...], grad_ref[...]
    hidden = jnp.dot(acts, up_ref[...], preferred_element_type=float32)
    square = hidden * hidden
    bend = jnp.tanh(GELU * hidden * (1.0 + CUBIC * square))
    share = 0.5 + 0.5 * bend
    active = (hidden * share).astype(bfloat16)
    slope = share + hidden * (0.5 - 0.5 * bend * bend) * (GELU + 3.0 * GELU * CUBIC * square)
    d_active = lax.dot_general(grad, down_ref[...], NT, preferred_element_type=float32)
    d_hidden = (d_active * slope).astype(bfloat16)
    sum_ref[...] += jnp.dot(active, down_ref[...], preferred_element_type=float32)
    back_ref[...] += lax.dot_general(d_hidden, up_ref[...], NT, preferred_element_type=float32)
    if deal:
        rows = BLOCK // one_ref.shape[0]
        d_up = jnp.dot(turned_ref[...], d_hidden, preferred_element_type=float32)
        d_up = d_up.astype(bfloat16)
        d_down = jnp.dot(active.T, grad, preferred_element_type=float32).astype(bfloat16)
        for band in range(d_up.shape[0] // BLOCK):
            blocks = [
                d_up[band * BLOCK : (band + 1) * BLOCK, start : start + BLOCK].reshape(-1, rows, BLOCK)
                for start in range(0, d_up.shape[1], BLOCK)
            ]
            one_ref[:, band] = jnp.concatenate(blocks, 1)
        blocks = [
            d_down[low : low + BLOCK, start : start + BLOCK].reshape(-1, rows, BLOCK)
            for low in range(0, d_down.shape[0], BLOCK)
            for start in range(0, d_down.shape[1], BLOCK)
        ]
        two_ref[...] = jnp.concatenate(blocks, 1)
    else:
        one_ref[...] = active
        two_ref[...] = d_hidden

    @pl.when(at == last)
    def _():
        out_ref[...] = sum_ref[...].astype(bfloat16)


def feed_forward(acts, grad, middle, w_up, w_down, device_count, tile=2 * BLOCK):
    tok_rows, width = acts.shape
    hidden = w_up.shape[1]
    rows = BLOCK // device_count
    deal = rows % 8 == 0
    full = pl.BlockSpec((tok_rows, width), lambda j: (0, 0))
    if deal:
        bands, blocks = width // BLOCK, hidden // BLOCK
        kinds = [(device_count, bands, blocks * rows, BLOCK), (device_count, blocks * bands * rows, BLOCK)]
        part = tile // BLOCK * rows
        specs = [
            pl.BlockSpec((device_count, bands, part, BLOCK), lambda j: (0, 0, j, 0)),
            pl.BlockSpec((device_count, bands * part, BLOCK), lambda j: (0, j, 0)),
        ]
    else:
        kinds = [(tok_rows, hidden)] * 2
        specs = [pl.BlockSpec((tok_rows, tile), lambda j: (0, j))] * 2
    out, back, one, two = pl.pallas_call(
        partial(feed_kernel, deal),
        grid=(hidden // tile,),
        in_specs=[full, full, full]
        + [
            pl.BlockSpec((width, tile), lambda j: (0, j)),
            pl.BlockSpec((tile, width), lambda j: (j, 0)),
        ],
        out_specs=[full, full] + specs,
        out_shape=[
            jax.ShapeDtypeStruct((tok_rows, width), bfloat16),
            jax.ShapeDtypeStruct((tok_rows, width), float32),
        ]
        + [jax.ShapeDtypeStruct(kind, bfloat16) for kind in kinds],
        scratch_shapes=[pltpu.VMEM((width, tok_rows), bfloat16), pltpu.VMEM((tok_rows, width), float32)],
        compiler_params=pltpu.CompilerParams(vmem_limit_bytes=58 * 2**20),
        cost_estimate=pl.CostEstimate(
            flops=12 * tok_rows * width * hidden, bytes_accessed=8 * width * hidden, transcendentals=0
        ),
    )(acts, grad, middle, w_up, w_down)
    if deal:
        return out, back, one.reshape(device_count, -1, BLOCK), two
    columns = lambda size: tuple(((0, 0, start, BLOCK),) for start in range(0, size, BLOCK))
    return (
        out,
        back,
        weight_grad(acts, [two[None]], columns(hidden), device_count),
        weight_grad(one, [grad[None]], columns(width), device_count),
    )


def ship_kernel(narrow_count, held_ref, *refs):
    shards, gain_ref = refs[:4], refs[4]
    arrived, total_ref = refs[5:7]
    pieces, outgoing, squares, send_sem, recv_sem, tile_send, tile_recv = refs[7:]
    devices, slots = outgoing.shape[:2]
    me = lax.axis_index("wide") * narrow_count + lax.axis_index("narrow")

    def device(d):
        place = lax.rem(me + d, devices)
        return place, {"wide": place // narrow_count, "narrow": lax.rem(place, narrow_count)}

    barrier = pltpu.get_barrier_semaphore()

    def announce(d, carry):
        pl.semaphore_signal(barrier, inc=1, device_id=device(d)[1], device_id_type=MESH)
        return carry

    lax.fori_loop(1, devices, announce, 0)
    at, own = 0, jnp.zeros((), float32)
    for shard in shards:
        values = shard[...]
        own += jnp.sum(values * values)
        pieces[at : at + values.shape[0]] = values
        at += values.shape[0]
    squares[me, : gain_ref.shape[0]] = gain_ref[...]
    squares[me, gain_ref.shape[0] :] = jnp.full((8, 128), own, float32)

    def pack(place, carry):
        for slot in range(slots):
            block = held_ref[place * slots + slot]
            piece = pieces[jnp.maximum(block, 0)]
            outgoing[place, slot] = jnp.where(block >= 0, piece, 0.0).astype(bfloat16)
        return carry

    lax.fori_loop(0, devices, pack, 0)
    pl.semaphore_wait(barrier, devices - 1)

    def copies(d):
        place, target = device(d)
        return (
            pltpu.make_async_remote_copy(
                src_ref=outgoing.at[place],
                dst_ref=arrived.at[:, me],
                send_sem=send_sem.at[d],
                recv_sem=recv_sem.at[d],
                device_id=target,
                device_id_type=MESH,
            ),
            pltpu.make_async_remote_copy(
                src_ref=squares.at[me],
                dst_ref=squares.at[me],
                send_sem=tile_send.at[d],
                recv_sem=tile_recv.at[d],
                device_id=target,
                device_id_type=MESH,
            ),
        )

    def start(d, carry):
        for copy in copies(d):
            copy.start()
        return carry

    lax.fori_loop(1, devices, start, 0)
    arrived[:, me] = outgoing[me]

    def arrive(d, carry):
        sender = lax.rem(me + devices - d, devices)
        pltpu.make_async_remote_copy(
            src_ref=outgoing.at[sender],
            dst_ref=arrived.at[:, sender],
            send_sem=send_sem.at[d],
            recv_sem=recv_sem.at[d],
            device_id=device(d)[1],
            device_id_type=MESH,
        ).wait_recv()
        pltpu.make_async_remote_copy(
            src_ref=squares.at[sender],
            dst_ref=squares.at[sender],
            send_sem=tile_send.at[d],
            recv_sem=tile_recv.at[d],
            device_id=device(d)[1],
            device_id_type=MESH,
        ).wait_recv()
        for copy in copies(d):
            copy.wait_send()
        return carry

    lax.fori_loop(1, devices, arrive, 0)
    total_ref[...] = jnp.sum(squares[...], 0)


def ship(shards, gain_grad, held, cap_slots, collective_id):
    devices = held.shape[0] // cap_slots
    rows = shards[0].shape[1]
    blocks = sum(shard.shape[0] for shard in shards)
    tile = (gain_grad.shape[0] + 8, 128)
    vmem = pl.BlockSpec(memory_space=pltpu.VMEM)
    return pl.pallas_call(
        partial(ship_kernel, lax.axis_size("narrow")),
        in_specs=[pl.BlockSpec(memory_space=pltpu.SMEM)] + [vmem] * (len(shards) + 1),
        out_specs=[vmem, vmem],
        out_shape=[
            jax.ShapeDtypeStruct((cap_slots, devices, rows, BLOCK), bfloat16),
            jax.ShapeDtypeStruct(tile, float32),
        ],
        scratch_shapes=[
            pltpu.VMEM((blocks, rows, BLOCK), float32),
            pltpu.VMEM((devices, cap_slots, rows, BLOCK), bfloat16),
            pltpu.VMEM((devices,) + tile, float32),
        ]
        + [pltpu.SemaphoreType.DMA((devices,))] * 4,
        compiler_params=pltpu.CompilerParams(
            collective_id=collective_id, has_side_effects=True, vmem_limit_bytes=VMEM_LIMIT
        ),
    )(held, *shards, gain_grad)


def update_kernel(rates, slot_ref, back_ref, *refs):
    masters, outs = refs[: len(rates)], refs[len(rates) :]
    block = 0
    for rate, master, out in zip(rates, masters, outs):
        bands, _, columns = master.shape
        for band in range(bands):
            for start in range(0, columns, BLOCK):
                here = slice(start, start + BLOCK)
                old = master[band, :, here]
                step = back_ref[slot_ref[block]].astype(float32)
                out[band, :, here] = old - rate * (step + weight_decay * old)
                block += 1


def update(masters, rates, places, back):
    vmem = pl.BlockSpec(memory_space=pltpu.VMEM)
    return pl.pallas_call(
        partial(update_kernel, rates),
        in_specs=[pl.BlockSpec(memory_space=pltpu.SMEM)] + [vmem] * (len(masters) + 1),
        out_specs=[vmem] * len(masters),
        out_shape=[jax.ShapeDtypeStruct(master.shape, float32) for master in masters],
        compiler_params=pltpu.CompilerParams(vmem_limit_bytes=VMEM_LIMIT),
    )(places, back, *masters)


def weight_grad_kernel(columns, band_rows, left_ref, *refs):
    right_refs, out_ref = refs[:-1], refs[-1]
    left = left_ref[...].T
    for at in range(0, len(columns), 2):
        blocks = []
        for spots in columns[at : at + 2]:
            right = [right_refs[i][g, :, start : start + size] for i, g, start, size in spots]
            right = right[0] if len(right) == 1 else jnp.concatenate(right, 1)
            block = jnp.dot(left, right, preferred_element_type=float32)
            blocks.append(block.astype(bfloat16).reshape(-1, band_rows, BLOCK))
        out_ref[:, at * band_rows : (at + 2) * band_rows, :] = jnp.concatenate(blocks, 1)


def weight_grad(left, rights, columns, device_count):
    tok_rows, height = left.shape
    band_rows = BLOCK // device_count
    bands, wide = height // BLOCK, len(columns)
    if band_rows % 8:
        right = [rights[i][g, :, start : start + n] for spots in columns for i, g, start, n in spots]
        right = jnp.concatenate(right, 1)
        product = jnp.einsum("td,te->de", left, right, preferred_element_type=float32)
        product = product.astype(bfloat16).reshape(bands, device_count, band_rows, wide, BLOCK)
        return product.transpose(1, 0, 3, 2, 4).reshape(device_count, -1, BLOCK)
    return pl.pallas_call(
        partial(weight_grad_kernel, columns, band_rows),
        grid=(bands,),
        in_specs=[
            pl.BlockSpec((tok_rows, BLOCK), lambda i: (0, i)),
        ]
        + [pl.BlockSpec(right.shape, lambda i: (0, 0, 0)) for right in rights],
        out_specs=pl.BlockSpec((device_count, wide * band_rows, BLOCK), lambda i: (0, i, 0)),
        out_shape=jax.ShapeDtypeStruct((device_count, bands * wide * band_rows, BLOCK), bfloat16),
        compiler_params=pltpu.CompilerParams(vmem_limit_bytes=VMEM_LIMIT),
        cost_estimate=pl.CostEstimate(
            flops=2 * tok_rows * bands * wide * BLOCK**2,
            bytes_accessed=2 * (tok_rows * (height + wide * BLOCK) + bands * wide * BLOCK**2),
            transcendentals=0,
        ),
    )(left, *rights)


def body(
    tokens,
    cotangent,
    lengths,
    owners,
    w_qkv,
    w_out,
    w_up,
    w_down,
    norm_gains,
    gain_first,
    gain_second,
    moment_first,
    moment_second,
    left_stat,
    right_stat,
    left_basis,
    right_basis,
):
    tok_rows, width = tokens.shape
    narrow_count = lax.axis_size("narrow")
    device_count = lax.axis_size("wide") * narrow_count
    seq_len = tok_rows * narrow_count
    cap_slots = moment_first.shape[0]
    masters = (w_qkv, w_out, w_up, w_down)
    lowered = tuple((layout.astype(jnp.bfloat16) for layout in masters)) + (
        norm_gains.astype(jnp.bfloat16),
    )
    share = norm_gains.shape[1]
    gains_low = jnp.pad(lowered[4], ((0, 6), (0, 128 - share)))[None]
    w_attn, gain_pair = gather_bands((lowered[0], gains_low), ((4, 2), (1, 1)), 3)
    w_attn = w_attn.reshape(width, 3 * width)
    gain_pair = gain_pair[0, :, :2, :share].transpose(1, 0, 2).reshape(2, width)
    gain_pair = gain_pair.astype(jnp.float32)
    w_proj, w_back = (
        gathered.reshape(-1, width)
        for gathered in lax.all_gather(lowered[1:4:2], ("wide", "narrow"), axis=1, tiled=True)
    )
    inputs = tokens.astype(jnp.float32)
    normed_one, inverse_one = normalize(inputs)
    act_one = (normed_one * gain_pair[0]).astype(jnp.bfloat16)
    head_width = width // narrow_count
    safe = seq_len - tok_rows
    packed = project(act_one, w_attn, narrow_count)
    halves = len(packed)
    scenes, merged, mixed, log_totals, w_hidden = attend(
        lengths, packed, safe, (lowered[2],), ((4, 2),), 4
    )
    w_hidden = w_hidden.reshape(width, FF)
    middle = inputs + jnp.dot(merged, w_proj, preferred_element_type=jnp.float32)
    normed_two, inverse_two = normalize(middle)
    act_two = (normed_two * gain_pair[1]).astype(jnp.bfloat16)
    block_out, d_act_two, d_w_hidden, d_back = feed_forward(
        act_two, cotangent, middle, w_hidden, w_back, device_count
    )
    d_norm_two, d_gain_two = norm_backward(d_act_two, normed_two, inverse_two, gain_pair[1])
    d_middle = cotangent.astype(jnp.float32) + d_norm_two
    d_branch = d_middle.astype(jnp.bfloat16)
    plain = lambda size: tuple(((0, 0, start, BLOCK),) for start in range(0, size, BLOCK))
    d_proj = weight_grad(merged, [d_branch[None]], plain(width), device_count)
    d_merged = jnp.einsum("te,de->td", d_branch, w_proj, preferred_element_type=jnp.float32).astype(
        jnp.bfloat16
    )
    ready = (d_w_hidden, d_back, d_proj)
    d_packed, hidden_sum, back_sum, proj_sum = attend_backward(
        lengths, scenes, mixed, d_merged, log_totals, safe, ready, (8, 8, 2), 5
    )
    if BLOCK // device_count % 8:
        d_packed = [d_packed[half] for half in range(halves)]
        grouped = tuple(
            tuple((half, group, third * PAIR, PAIR) for half in range(halves))
            for third in range(3)
            for group in range(narrow_count)
        )
        d_attn = weight_grad(act_one, d_packed, grouped, device_count)
        (attn_sum,) = reduce_to_shards((d_attn,), (6,), 1)
        d_act_one = project_back(d_packed, w_attn)
    else:
        attn_sum, d_act_one = settle(act_one, d_packed, w_attn, device_count, 1)
    d_norm_one, d_gain_one = norm_backward(d_act_one, normed_one, inverse_one, gain_pair[0])
    grad_tokens = (d_middle + d_norm_one).astype(jnp.bfloat16)
    gain_parts = jnp.stack([d_gain_one, d_gain_two]).reshape(-1, 128)
    band_rows = BLOCK // device_count
    block_count = owners.shape[0]
    order = lax.iota(jnp.int32, block_count)
    earlier = (owners[None, :] == owners[:, None]) & (order[None, :] < order[:, None])
    rank = jnp.sum(earlier.astype(jnp.int32), 1)
    slots = owners * cap_slots + rank
    every = lax.iota(jnp.int32, device_count * cap_slots)
    held = jnp.max(jnp.where(slots[None, :] == every[:, None], order[None, :], -1), 1)
    shards = [
        shard.reshape(-1, band_rows, BLOCK)
        for shard in (attn_sum, proj_sum, hidden_sum, back_sum)
    ]
    slot_grads, totals = ship(shards, gain_parts, held, cap_slots, 2)
    place = lax.axis_index(("wide", "narrow"))
    gain_grad = totals[:-8].reshape(2, width)
    grad_norm = jnp.sqrt(totals[-1, 0] + jnp.sum(gain_grad * gain_grad))
    gain_grad = lax.dynamic_slice_in_dim(gain_grad, place * share, share, 1)
    factor = jnp.minimum(1.0, clip_bound / grad_norm)
    slot_grads = slot_grads.reshape(cap_slots, BLOCK, BLOCK)
    restored, first_new, second_new, left_new, right_new, gram, turn = soap_update(
        factor, slot_grads, moment_first, moment_second, left_stat, right_stat, left_basis, right_basis
    )
    square = (-1, BLOCK, BLOCK)
    left_turn, right_turn = renew_bases(gram.reshape(square), turn.reshape(square))
    returned = lax.all_to_all(
        shortened(restored.reshape(cap_slots, device_count, -1, BLOCK)),
        ("wide", "narrow"),
        split_axis=1,
        concat_axis=1,
        tiled=True,
    )
    fan_list = (2 * width, max(1, width * 16 // seq_len), width, FF)
    rates = tuple(fan_in ** (-0.5) for fan_in in fan_list)
    places = rank * device_count + owners
    updated = update(masters, rates, places, returned.reshape(-1, band_rows, BLOCK))
    clipped = gain_grad * factor
    gain_one_new = decay_rate * gain_first + (1.0 - decay_rate) * clipped
    gain_two_new = decay_rate * gain_second + (1.0 - decay_rate) * clipped * clipped
    correct = 1.0 - decay_rate**STEP
    gain_values = norm_gains - gain_rate * (gain_one_new / correct) / (
        jnp.sqrt(gain_two_new / correct) + eps_adam
    )
    return (
        block_out,
        grad_tokens,
        grad_norm,
        updated[0],
        updated[1],
        updated[2],
        updated[3],
        gain_values,
        gain_one_new,
        gain_two_new,
        first_new,
        second_new,
        left_new,
        right_new,
        left_turn,
        right_turn,
    )


def solution(mesh):
    in_specs = (
        P(("wide", "narrow"), None),
        P(("wide", "narrow"), None),
        P("wide"),
        P(),
        P(None, ("wide", "narrow"), None),
        P(None, ("wide", "narrow"), None),
        P(None, ("wide", "narrow"), None),
        P(None, ("wide", "narrow"), None),
        P(None, ("wide", "narrow")),
        P(None, ("wide", "narrow")),
        P(None, ("wide", "narrow")),
        P(("wide", "narrow"), None, None),
        P(("wide", "narrow"), None, None),
        P(("wide", "narrow"), None, None),
        P(("wide", "narrow"), None, None),
        P(("wide", "narrow"), None, None),
        P(("wide", "narrow"), None, None),
    )
    out_specs = (
        P(("wide", "narrow"), None),
        P(("wide", "narrow"), None),
        P(),
        P(None, ("wide", "narrow"), None),
        P(None, ("wide", "narrow"), None),
        P(None, ("wide", "narrow"), None),
        P(None, ("wide", "narrow"), None),
        P(None, ("wide", "narrow")),
        P(None, ("wide", "narrow")),
        P(None, ("wide", "narrow")),
        P(("wide", "narrow"), None, None),
        P(("wide", "narrow"), None, None),
        P(("wide", "narrow"), None, None),
        P(("wide", "narrow"), None, None),
        P(("wide", "narrow"), None, None),
        P(("wide", "narrow"), None, None),
    )
    return jax.shard_map(body, mesh=mesh, in_specs=in_specs, out_specs=out_specs, check_vma=False)
```

```python
from functools import partial

import jax
import jax.numpy as jnp
from jax import lax
from jax.experimental import pallas as pl
from jax.experimental.pallas import tpu as pltpu
from jax.sharding import PartitionSpec as P

FF = 4096
HEADS = 16
HEAD = 64
BLOCK = 256
STEP = 10


eps_norm = 1e-05
eps_adam = 1e-08
decay_rate = 0.5
clip_bound = 1.0
weight_decay = 0.01
gain_rate = 1.0
neg_large = -1e30
highest = lax.Precision.HIGHEST
float32 = jnp.float32
bfloat16 = jnp.bfloat16
PAIR = 2 * HEAD
NT = (((1,), (1,)), ((), ()))
TN = (((0,), (0,)), ((), ()))
MESH = pl.DeviceIdType.MESH
VMEM_LIMIT = 48 * 2**20
AHEAD = 8
SKEW = 3
ORDERS = ((0, 2, 1, None), (0, 1, 2, None), (0, 2, None, 1))
PACE = 3.7
DELAY = 12.0
GATHER_PACE = 6.0
GATHER_DELAY = 30.0
SETTLE_DELAY = 6.0
TOGETHER = 2
GELU = 0.7978845608
CUBIC = 0.044715


def shortened(shard):
    return jax.tree.map(lambda a: a.astype(jnp.bfloat16) if a.dtype == jnp.float32 else a, shard)


def normalize(values):
    center = values - jnp.mean(values, -1, keepdims=True)
    inverse = lax.rsqrt(jnp.mean(center * center, -1, keepdims=True) + eps_norm)
    return (center * inverse, inverse)


def norm_backward(d_result, normed, inverse, gain):
    scaled = d_result * gain
    d_gain = jnp.sum(d_result * normed, 0)
    d_input = inverse * (
        scaled
        - jnp.mean(scaled, -1, keepdims=True)
        - normed * jnp.mean(scaled * normed, -1, keepdims=True)
    )
    return (d_input, d_gain)


def one_head(matrix, head):
    lane = lax.broadcasted_iota(jnp.int32, matrix.shape, 1)
    return jnp.where(lane // HEAD == head, matrix, jnp.zeros_like(matrix))


def hide(scores, start, safe, length):
    if start + scores.shape[0] <= safe:
        return scores
    position = start + lax.broadcasted_iota(jnp.int32, scores.shape, 0)
    return jnp.where(position < length, scores, neg_large)


def project_kernel(acts_ref, wq_ref, wk_ref, wv_ref, *out_refs):
    thirds = (wq_ref, wk_ref, wv_ref)
    halves = len(out_refs)
    weights = jnp.concatenate(
        [third[:, h * PAIR : (h + 1) * PAIR] for h in range(halves) for third in thirds], 1
    )
    result = jnp.dot(acts_ref[...], weights, preferred_element_type=float32).astype(bfloat16)
    for h, out_ref in enumerate(out_refs):
        out_ref[0] = result[:, h * 3 * PAIR : (h + 1) * 3 * PAIR]


def project(acts, weights, groups):
    tok_rows, width = acts.shape
    head_width = width // groups
    halves = head_width // PAIR

    def third(k):
        return pl.BlockSpec((width, head_width), lambda g: (0, k * groups + g))

    return pl.pallas_call(
        project_kernel,
        grid=(groups,),
        in_specs=[pl.BlockSpec((tok_rows, width), lambda g: (0, 0)), third(0), third(1), third(2)],
        out_specs=[pl.BlockSpec((1, tok_rows, 3 * PAIR), lambda g: (g, 0, 0))] * halves,
        out_shape=[jax.ShapeDtypeStruct((groups, tok_rows, 3 * PAIR), bfloat16)] * halves,
        compiler_params=pltpu.CompilerParams(vmem_limit_bytes=VMEM_LIMIT),
        cost_estimate=pl.CostEstimate(
            flops=6 * tok_rows * width**2, bytes_accessed=6 * width**2 + 8 * tok_rows * width,
            transcendentals=0,
        ),
    )(acts, weights, weights, weights)


def project_back_kernel(halves, *refs):
    grads, (wq_ref, wk_ref, wv_ref, out_ref) = refs[:halves], refs[halves:]
    thirds = (wq_ref, wk_ref, wv_ref)
    weights = jnp.concatenate(
        [third[:, h * PAIR : (h + 1) * PAIR] for h in range(halves) for third in thirds], 1
    )
    rows = jnp.concatenate([grad[0] for grad in grads], 1)
    result = lax.dot_general(rows, weights, NT, preferred_element_type=float32)

    @pl.when(pl.program_id(0) == 0)
    def _():
        out_ref[...] = result

    @pl.when(pl.program_id(0) > 0)
    def _():
        out_ref[...] += result


def project_back(grads, weights):
    groups, tok_rows, _ = grads[0].shape
    width = weights.shape[0]
    head_width = width // groups

    def third(k):
        return pl.BlockSpec((width, head_width), lambda g: (0, k * groups + g))

    return pl.pallas_call(
        partial(project_back_kernel, len(grads)),
        grid=(groups,),
        in_specs=[pl.BlockSpec((1, tok_rows, 3 * PAIR), lambda g: (g, 0, 0))] * len(grads)
        + [third(0), third(1), third(2)],
        out_specs=pl.BlockSpec((tok_rows, width), lambda g: (0, 0)),
        out_shape=jax.ShapeDtypeStruct((tok_rows, width), float32),
        compiler_params=pltpu.CompilerParams(vmem_limit_bytes=VMEM_LIMIT),
        cost_estimate=pl.CostEstimate(
            flops=6 * tok_rows * width**2, bytes_accessed=6 * width**2 + 10 * tok_rows * width,
            transcendentals=0,
        ),
    )(*grads, weights, weights, weights)


def exact(left, right, dims=(((1,), (0,)), ((), ()))):
    return lax.dot_general(left, right, dims, precision=highest, preferred_element_type=float32)


def soap_kernel(
    factor_ref, g_ref, first_ref, second_ref, ls_ref, rs_ref, lb_ref, rb_ref,
    back_ref, first_out, second_out, ls_out, rs_out, gram_ref, turn_ref,
):
    factor = factor_ref[0, 0]
    rough = g_ref[0]
    gradient = factor * rough.astype(float32)
    half_square = (1.0 - decay_rate) * factor * factor
    left_base, right_base = lb_ref[0], rb_ref[0]
    left_square = lax.dot_general(rough, rough, NT, preferred_element_type=float32)
    right_square = jnp.dot(rough.T, rough, preferred_element_type=float32)
    left_new = decay_rate * ls_ref[0] + half_square * left_square
    right_new = decay_rate * rs_ref[0] + half_square * right_square
    ls_out[0] = left_new
    rs_out[0] = right_new
    turned = exact(left_base, exact(gradient, right_base), TN)
    first_new = decay_rate * first_ref[0] + (1.0 - decay_rate) * turned
    second_new = decay_rate * second_ref[0] + (1.0 - decay_rate) * turned * turned
    first_out[0] = first_new
    second_out[0] = second_new
    correct = 1.0 - decay_rate**STEP
    direction = first_new / correct / (jnp.sqrt(second_new / correct) + eps_adam)
    back_ref[0] = exact(left_base, exact(direction, right_base, NT)).astype(back_ref.dtype)
    for side, stat, base in ((0, left_new, left_base), (1, right_new, right_base)):
        turn = exact(stat, base).T
        turn_ref[0, side] = turn
        gram_ref[0, side] = exact(turn, turn, NT)


def soap_update(factor, gradient, first_old, second_old, left_old, right_old, left_base, right_base):
    slots, order, _ = gradient.shape
    one = pl.BlockSpec((1, order, order), lambda s: (s, 0, 0))
    two = pl.BlockSpec((1, 2, order, order), lambda s: (s, 0, 0, 0))
    single = jax.ShapeDtypeStruct((slots, order, order), float32)
    double = jax.ShapeDtypeStruct((slots, 2, order, order), float32)
    return pl.pallas_call(
        soap_kernel,
        grid=(slots,),
        in_specs=[pl.BlockSpec(memory_space=pltpu.SMEM)] + [one] * 7,
        out_specs=[one] * 5 + [two] * 2,
        out_shape=[jax.ShapeDtypeStruct((slots, order, order), bfloat16)] + [single] * 4 + [double] * 2,
        compiler_params=pltpu.CompilerParams(vmem_limit_bytes=VMEM_LIMIT),
        cost_estimate=pl.CostEstimate(
            flops=slots * 120 * order**3, bytes_accessed=slots * 60 * order**2, transcendentals=0
        ),
    )(factor.reshape(1, 1), gradient, first_old, second_old, left_old, right_old, left_base, right_base)


def eliminate(x_ref, j):
    count, rows, lanes = x_ref.shape
    tile = j // 8 * 8
    sublane = lax.broadcasted_iota(jnp.int32, (1, 8, 1), 1)
    spread = lambda column: jnp.broadcast_to(column, (count, 1, lanes))
    pivots = [x_ref[:, j + k : j + k + 1, :] for k in range(TOGETHER)]
    corner = [
        [spread(pivots[k][:, :, j + q : j + q + 1]) for q in range(TOGETHER)]
        for k in range(TOGETHER)
    ]
    scaled, factors = [], []
    for k in range(TOGETHER):
        inverse = 1.0 / corner[k][k]
        scaled.append(pivots[k] * inverse)
        factors.append({})
        for q in range(k + 1, TOGETHER):
            factor = corner[k][q] * inverse
            factors[k][q] = factor
            pivots[q] = pivots[q] - factor * pivots[k]
            for t in range(q, TOGETHER):
                corner[q][t] = corner[q][t] - factor * corner[k][t]

    def below(old, masked):
        parts = [old[:, :, j + k : j + k + 1] for k in range(TOGETHER)]
        new = old
        for k in range(TOGETHER):
            part = jnp.broadcast_to(parts[k], old.shape)
            for q in range(k):
                part = part - parts[q] * factors[q][k]
            parts[k] = part
            kept = jnp.where(sublane > j + k - tile, part, 0.0) if masked else part
            new = new - kept * scaled[k]
        return new

    x_ref[:, tile : tile + 8, :] = below(x_ref[:, tile : tile + 8, :], True)
    for start in range(tile + 8, rows, 8):
        x_ref[:, start : start + 8, :] = below(x_ref[:, start : start + 8, :], False)


def renew_kernel(rows, gram_ref, turn_ref, left_ref, right_ref, x_ref, u_ref):
    count, order = gram_ref.shape[0], gram_ref.shape[1]
    eye = (
        lax.broadcasted_iota(jnp.int32, (rows, rows), 0)
        == lax.broadcasted_iota(jnp.int32, (rows, rows), 1)
    ).astype(float32)
    sublane = lax.broadcasted_iota(jnp.int32, (1, 8, 1), 1)
    for low in range(0, order, rows):
        part = slice(low, low + rows)
        edge = low // 128 * 128

        def panel(at, carry, low=low, part=part, edge=edge):
            row = jnp.concatenate([gram_ref[at, part, edge:], turn_ref[at, part, :]], 1)
            if low:
                row = row - exact(u_ref[at, :low, part], u_ref[at, :low, edge:], TN)
            u_ref[at, part, edge:] = row
            x_ref[at] = jnp.concatenate([row[:, low - edge : low - edge + rows], eye], 1)
            return carry

        lax.fori_loop(0, count, panel, 0, unroll=2)
        for j in range(0, rows, TOGETHER):
            eliminate(x_ref, j)

        def solve(at, carry, part=part, edge=edge):
            both = x_ref[at]
            diagonal = jnp.sum(both[:, :rows] * eye, 1, keepdims=True)
            inverse = both[:, rows:] * lax.rsqrt(diagonal)
            u_ref[at, part, edge:] = exact(inverse, u_ref[at, part, edge:])
            return carry

        lax.fori_loop(0, count, solve, 0, unroll=2)

    def turn_back(at, carry):
        left_ref[at] = u_ref[2 * at, :, order:].T
        right_ref[at] = u_ref[2 * at + 1, :, order:].T
        return carry

    lax.fori_loop(0, count // 2, turn_back, 0)


def renew_bases(gram, turn, rows=64):
    count, order, _ = gram.shape
    return pl.pallas_call(
        partial(renew_kernel, rows),
        out_shape=[jax.ShapeDtypeStruct((count // 2, order, order), float32)] * 2,
        in_specs=[pl.BlockSpec(memory_space=pltpu.VMEM)] * 2,
        out_specs=[pl.BlockSpec(memory_space=pltpu.VMEM)] * 2,
        scratch_shapes=[
            pltpu.VMEM((count, rows, 2 * rows), float32),
            pltpu.VMEM((count, order, 2 * order), float32),
        ],
        compiler_params=pltpu.CompilerParams(vmem_limit_bytes=VMEM_LIMIT),
        cost_estimate=pl.CostEstimate(
            flops=count * 200 * order**3, bytes_accessed=count * 12 * order**2, transcendentals=0
        ),
    )(gram, turn)


def partner(bit, narrow_bits):
    axis, step = ("narrow", 1 << bit) if bit < narrow_bits else ("wide", 1 << (bit - narrow_bits))
    place = lax.axis_index(axis)
    mine = lax.rem(place // step, 2)
    return {axis: place + step - 2 * step * mine}, mine


def greet(peers):
    barrier = pltpu.get_barrier_semaphore()
    for device, _ in peers:
        pl.semaphore_signal(barrier, inc=1, device_id=device, device_id_type=MESH)
    pl.semaphore_wait(barrier, len(peers))


def mesh_bits():
    narrow_bits = lax.axis_size("narrow").bit_length() - 1
    return narrow_bits + lax.axis_size("wide").bit_length() - 1, narrow_bits


def reduce_steps(bits, narrow_bits, plans, chunks, sources, outs, scratch):
    count = len(sources)
    held = scratch[:count]
    arrived = [scratch[count * (1 + s) : count * (2 + s)] for s in range(bits)]
    load_sem, send_sem, recv_sem = scratch[count * (1 + bits) :]
    peers = [partner(b, narrow_bits) for b in range(bits)]
    first = plans[0][0]
    order_of_dims = list(reversed(range(bits)))
    whole = slice(None)

    def within(order, stage, current):
        return tuple(
            peers[b][1] if b in order[:stage] else current if b == order[stage] else whole
            for b in order_of_dims
            if b != first
        )

    def of_source(value):
        return tuple(value if b == first else whole for b in order_of_dims)

    def rows_of(chunk):
        at, row, rows, colour = chunks[chunk]
        return at, plans[colour], (pl.ds(row, rows), whole)

    def send(chunk, stage):
        at, order, part = rows_of(chunk)
        device, mine = peers[order[stage]]
        if stage == 0:
            source = sources[at].at[of_source(1 - mine) + part]
        else:
            source = held[at].at[within(order, stage, 1 - mine) + part]
        return pltpu.make_async_remote_copy(
            src_ref=source,
            dst_ref=arrived[stage][at].at[(whole,) * (bits - 1 - stage) + part],
            send_sem=send_sem.at[chunk, stage],
            recv_sem=recv_sem.at[chunk, stage],
            device_id=device,
            device_id_type=MESH,
        )

    def load(chunk):
        at, order, part = rows_of(chunk)
        return pltpu.make_async_copy(
            sources[at].at[of_source(peers[first][1]) + part],
            held[at].at[(whole,) * (bits - 1) + part],
            load_sem.at[chunk],
        )

    def begin(chunk):
        send(chunk, 0).start()
        load(chunk).start()

    def finish(chunk, stage):
        at, order, part = rows_of(chunk)
        if stage == 0:
            load(chunk).wait()
        send(chunk, stage).wait_recv()
        left = bits - 1 - stage
        keep = within(order, stage, peers[order[stage]][1])
        if left == 0:
            own = held[at][keep + part].astype(float32)
            outs[at][part] = own + arrived[stage][at][part].astype(float32)
            return
        free = [i for i, k in enumerate(keep) if isinstance(k, slice)]

        def add(m, carry):
            which = tuple(m // (1 << (left - 1 - i)) % 2 for i in range(left))
            spot = list(keep)
            for i, f in enumerate(free):
                spot[f] = which[i]
            spot = tuple(spot) + part
            held[at][spot] = held[at][spot] + arrived[stage][at][which + part]
            return carry

        lax.fori_loop(0, 1 << left, add, 0)
        send(chunk, stage + 1).start()

    def drain():
        for chunk in range(len(chunks)):
            for stage in range(bits):
                send(chunk, stage).wait_send()

    return peers, begin, finish, drain


def reduce_kernel(bits, narrow_bits, plans, chunks, count, *refs):
    peers, begin, finish, drain = reduce_steps(
        bits, narrow_bits, plans, chunks, refs[:count], refs[count : 2 * count], refs[2 * count :]
    )
    greet(peers)
    total = len(chunks)
    for chunk in range(min(AHEAD, total)):
        begin(chunk)
    for step in range(total + 2 * bits):
        for stage in reversed(range(bits)):
            chunk = step - 2 * stage
            if 0 <= chunk < total:
                finish(chunk, stage)
                if stage == 0 and chunk + AHEAD < total:
                    begin(chunk + AHEAD)
    drain()


def slot_table(chunks, bits, slots, pace, delay):
    table = [[] for _ in range(slots + 1)]
    done = sorted(
        (chunk * pace + (stage + 1) * delay, -stage, chunk, stage)
        for chunk in range(chunks)
        for stage in range(bits)
    )
    for when, _, chunk, stage in done:
        table[min(int(when), slots)].append((chunk, stage))
    return table


def reduce_plan(parts, pieces, orders=None):
    orders = ORDERS if orders is None else orders
    bits, narrow_bits = mesh_bits()
    shapes = [part.shape[1:] for part in parts]
    kinds = [part.dtype for part in parts]
    chunks = []
    for at, (shape, cut) in enumerate(zip(shapes, pieces)):
        rows = shape[0] // cut
        for row in range(0, shape[0], rows):
            chunks.append((at, row, rows, len(chunks) % len(orders)))
    later = tuple(range(3, bits))
    plans = tuple(tuple(b for part in order for b in (later if part is None else (part,))) for order in orders)
    sizes = [bits - 1] + [bits - 1 - stage for stage in range(bits)]
    scratch = [
        pltpu.VMEM((2,) * size + shape, kind)
        for size in sizes
        for shape, kind in zip(shapes, kinds)
    ]
    total = len(chunks)
    scratch += [
        pltpu.SemaphoreType.DMA((total,)),
        pltpu.SemaphoreType.DMA((total, bits)),
        pltpu.SemaphoreType.DMA((total, bits)),
    ]
    outs = [jax.ShapeDtypeStruct(shape, float32) for shape in shapes]
    halved = [
        part.reshape((2,) * bits + shape) if hasattr(part, "reshape") else part
        for part, shape in zip(parts, shapes)
    ]
    return bits, narrow_bits, plans, tuple(chunks), halved, outs, scratch


def reduce_to_shards(parts, pieces, collective_id):
    bits, narrow_bits, plans, chunks, halved, outs, scratch = reduce_plan(parts, pieces)
    return pl.pallas_call(
        partial(reduce_kernel, bits, narrow_bits, plans, chunks, len(parts)),
        out_shape=outs,
        in_specs=[pl.BlockSpec(memory_space=pl.ANY)] * len(parts),
        out_specs=[pl.BlockSpec(memory_space=pltpu.VMEM)] * len(parts),
        scratch_shapes=scratch,
        compiler_params=pltpu.CompilerParams(
            collective_id=collective_id, has_side_effects=True, vmem_limit_bytes=58 * 2**20
        ),
        cost_estimate=pl.CostEstimate(flops=10**8, bytes_accessed=4 * 10**8, transcendentals=0),
    )(*halved)


def gather_steps(bits, narrow_bits, plans, chunks, sources, outs, scratch):
    own_sem, send_sem, recv_sem = scratch
    peers = [partner(b, narrow_bits) for b in range(bits)]
    dims = list(reversed(range(bits)))

    def place(chunk, stage):
        at, band, bands, col, cols, colour = chunks[chunk]
        done = plans[colour][:stage]
        index = tuple(slice(None) if b in done else peers[b][1] for b in dims)
        return outs[at].at[(pl.ds(band, bands),) + index + (slice(None), pl.ds(col, cols))]

    def own(chunk):
        at, band, bands, col, cols, colour = chunks[chunk]
        return sources[at].at[pl.ds(band, bands), :, pl.ds(col, cols)]

    def send(chunk, stage):
        colour = chunks[chunk][-1]
        target = place(chunk, stage)
        return pltpu.make_async_remote_copy(
            src_ref=target if stage else own(chunk),
            dst_ref=target,
            send_sem=send_sem.at[chunk, stage],
            recv_sem=recv_sem.at[chunk, stage],
            device_id=peers[plans[colour][stage]][0],
            device_id_type=MESH,
        )

    def keep(chunk):
        return pltpu.make_async_copy(own(chunk), place(chunk, 0), own_sem.at[chunk])

    def begin(chunk):
        send(chunk, 0).start()
        keep(chunk).start()

    def finish(chunk, stage):
        if stage == 0:
            keep(chunk).wait()
        send(chunk, stage).wait_recv()
        if stage + 1 < bits:
            send(chunk, stage + 1).start()

    def drain():
        for chunk in range(len(chunks)):
            for stage in range(bits):
                send(chunk, stage).wait_send()

    return peers, begin, finish, drain


def gather_kernel(bits, narrow_bits, plans, chunks, count, *refs):
    peers, begin, finish, drain = gather_steps(
        bits, narrow_bits, plans, chunks, refs[:count], refs[count : 2 * count], refs[2 * count :]
    )
    greet(peers)
    total = len(chunks)
    for chunk in range(total):
        begin(chunk)
    for step in range(total + SKEW * bits):
        for stage in reversed(range(bits)):
            chunk = step - SKEW * stage
            if 0 <= chunk < total:
                finish(chunk, stage)
    drain()


def gather_plan(parts, pieces):
    bits, narrow_bits = mesh_bits()
    chunks = []
    for at, (part, (cut, cut_cols)) in enumerate(zip(parts, pieces)):
        bands, cols = part.shape[0] // cut, part.shape[2] // cut_cols
        for band in range(0, part.shape[0], bands):
            for col in range(0, part.shape[2], cols):
                chunks.append((at, band, bands, col, cols, len(chunks) % 2))
    later = tuple(reversed(range(3, bits)))
    plans = (later + (1, 2, 0), later + (2, 1, 0))
    total = len(chunks)
    outs = [
        jax.ShapeDtypeStruct(part.shape[:1] + (2,) * bits + part.shape[1:], part.dtype)
        for part in parts
    ]
    scratch = [
        pltpu.SemaphoreType.DMA((total,)),
        pltpu.SemaphoreType.DMA((total, bits)),
        pltpu.SemaphoreType.DMA((total, bits)),
    ]
    return bits, narrow_bits, plans, tuple(chunks), outs, scratch


def gather_bands(parts, pieces, collective_id):
    bits, narrow_bits, plans, chunks, outs, scratch = gather_plan(parts, pieces)
    results = pl.pallas_call(
        partial(gather_kernel, bits, narrow_bits, plans, chunks, len(parts)),
        out_shape=outs,
        in_specs=[pl.BlockSpec(memory_space=pl.ANY)] * len(parts),
        out_specs=[pl.BlockSpec(memory_space=pl.ANY)] * len(parts),
        scratch_shapes=scratch,
        compiler_params=pltpu.CompilerParams(collective_id=collective_id, has_side_effects=True),
        cost_estimate=pl.CostEstimate(flops=0, bytes_accessed=10**8, transcendentals=0),
    )(*parts)
    return [
        result.reshape(part.shape[:1] + (1 << bits,) + part.shape[1:])
        for result, part in zip(results, parts)
    ]


def group_peers():
    count = lax.axis_size("narrow")
    me = lax.axis_index("narrow")
    return me, [({"narrow": lax.rem(me + d, count)}, lax.rem(me + d, count)) for d in range(count)]


def rows_at(place, rows):
    return pl.ds(pl.multiple_of(place * rows, rows), rows)


def attend_kernel(safe, chunk, halves, plan, slots, length_ref, *refs):
    count = plan[4]
    packed, sources = refs[:halves], refs[halves : halves + count]
    refs = refs[halves + count :]
    scenes_out, merged, mixed_out, log_ref = refs[:4]
    scene_ref, o_ref, vt_ref, s_ref, near_sem, in_sem, back_sem, out_sem = refs[4 + count : 12 + count]
    others, begin, finish, drain = gather_steps(
        *plan[:4], sources, refs[4 : 4 + count], refs[12 + count :]
    )
    seq_len = scene_ref.shape[1]
    me, peers = group_peers()
    devices = len(peers)
    tok_rows = seq_len // devices
    length = length_ref[0]
    half, step = pl.program_id(0), pl.program_id(1)
    last = pl.num_programs(1) - 1
    own = rows_at(me, tok_rows)

    def bring(h, d):
        device, place = peers[d]
        if d == 0:
            return pltpu.make_async_copy(packed[h].at[me], scene_ref.at[h, own], in_sem.at[h, 0])
        return pltpu.make_async_remote_copy(
            src_ref=packed[h].at[place],
            dst_ref=scene_ref.at[h, own],
            send_sem=near_sem.at[h, d],
            recv_sem=in_sem.at[h, d],
            device_id=device,
            device_id_type=MESH,
        )

    def give(h, d, at, to, sender):
        column = pl.ds(pl.multiple_of((sender * halves + h) * PAIR, PAIR), PAIR)
        target = merged.at[:, column]
        source = o_ref.at[h, rows_at(to, tok_rows)]
        if d == 0:
            return pltpu.make_async_copy(source, target, out_sem.at[h, 0])
        return pltpu.make_async_remote_copy(
            src_ref=source,
            dst_ref=target,
            send_sem=back_sem.at[h, d],
            recv_sem=out_sem.at[h, d],
            device_id={"narrow": to},
            device_id_type=MESH,
        )

    def save_scene(h):
        return pltpu.make_async_copy(scene_ref.at[h], scenes_out.at[h], near_sem.at[h, 0])

    def save_mixed(h):
        return pltpu.make_async_copy(o_ref.at[h], mixed_out.at[h], back_sem.at[h, 0])

    @pl.when((half == 0) & (step == 0))
    def _():
        greet(peers[1:] + others[plan[1] :])
        for d in range(devices):
            bring(0, d).start()
        for which in range(len(plan[3])):
            begin(which)

    for h in range(halves):

        @pl.when((half == h) & (step == 0))
        def _(h=h):
            for d in range(devices):
                if d:
                    bring(h, d).wait_recv()
                else:
                    bring(h, d).wait()
            if h + 1 < halves:
                for d in range(devices):
                    bring(h + 1, d).start()
            save_scene(h).start()
            vt_ref[...] = scene_ref[h, :, 2 * PAIR :].T

    points = 2 * seq_len // chunk

    def move_at(point):
        for h in range(halves):
            for s in range(devices):
                todo = slots[(h * devices + s) * 2 * points + point]
                if todo:

                    @pl.when((half == h) & (step == s))
                    def _(todo=todo):
                        for which, stage in todo:
                            finish(which, stage)

    to = lax.rem(me + 1 + step, devices)
    here = rows_at(to, tok_rows)
    outs = []
    for head in range(2):
        queries = one_head(scene_ref[half, here, :PAIR], head) * bfloat16(HEAD**-0.5)
        topmost = None
        for at in range(0, seq_len, chunk):
            move_at(head * points + at // chunk)
            scores = lax.dot_general(
                scene_ref[half, at : at + chunk, PAIR : 2 * PAIR],
                queries,
                NT,
                preferred_element_type=float32,
            )
            scores = hide(scores, at, safe, length)
            s_ref[head, at : at + chunk, :] = scores
            top = jnp.max(scores, 0, keepdims=True)
            topmost = top if topmost is None else jnp.maximum(topmost, top)
        totals = jnp.zeros_like(topmost)
        mixed = jnp.zeros((HEAD, tok_rows), float32)
        for at in range(0, seq_len, chunk):
            move_at(head * points + points // 2 + at // chunk)
            expo = jnp.exp(s_ref[head, at : at + chunk, :] - topmost)
            totals += jnp.sum(expo, 0, keepdims=True)
            mixed += jnp.dot(
                vt_ref[head * HEAD : (head + 1) * HEAD, at : at + chunk],
                expo.astype(bfloat16),
                preferred_element_type=float32,
            )
        outs.append(mixed * (1.0 / totals))
        log_ref[half, head : head + 1, here] = topmost + jnp.log(totals)
    o_ref[half, here, :] = jnp.concatenate(outs, 0).T.astype(bfloat16)

    for h in range(halves):
        for s in range(devices):

            @pl.when((half == h) & (step == s))
            def _(h=h, s=s):
                d = (s + 1) % devices
                give(h, d, s, lax.rem(me + d, devices), me).start()
                if s == devices - 1:
                    save_mixed(h).start()

    @pl.when((half == halves - 1) & (step == last))
    def _():
        for which, stage in slots[-1]:
            finish(which, stage)
        drain()
        for h in range(halves):
            for d in range(devices):
                if d:
                    bring(h, d).wait_send()
                    sender = lax.rem(me + devices - d, devices)
                    arriving = give(h, d, d, lax.rem(me + d, devices), sender)
                    arriving.wait_recv()
                    arriving.wait_send()
                else:
                    give(h, 0, 0, me, me).wait()
            save_scene(h).wait()
            save_mixed(h).wait()


def attend(lengths, packed, safe, parts, pieces, collective_id, chunk=512):
    devices, tok_rows, _ = packed[0].shape
    halves, seq_len = len(packed), devices * tok_rows
    width = devices * halves * PAIR
    anywhere = pl.BlockSpec(memory_space=pl.ANY)
    bits, narrow_bits, plans, chunks, outs, scratch = gather_plan(parts, pieces)
    slots = slot_table(
        len(chunks), bits, halves * devices * 4 * (seq_len // chunk), GATHER_PACE, GATHER_DELAY
    )
    plan = (bits, narrow_bits, plans, chunks, len(parts))
    results = pl.pallas_call(
        partial(attend_kernel, safe, chunk, halves, plan, slots),
        grid=(halves, devices),
        in_specs=[pl.BlockSpec(memory_space=pltpu.SMEM)] + [anywhere] * (halves + len(parts)),
        out_specs=[anywhere] * 3
        + [pl.BlockSpec((halves, 2, seq_len), lambda p, i: (0, 0, 0))]
        + [anywhere] * len(parts),
        out_shape=[
            jax.ShapeDtypeStruct((halves, seq_len, 3 * PAIR), bfloat16),
            jax.ShapeDtypeStruct((tok_rows, width), bfloat16),
            jax.ShapeDtypeStruct((halves, seq_len, PAIR), bfloat16),
            jax.ShapeDtypeStruct((halves, 2, seq_len), float32),
        ]
        + outs,
        scratch_shapes=[
            pltpu.VMEM((halves, seq_len, 3 * PAIR), bfloat16),
            pltpu.VMEM((halves, seq_len, PAIR), bfloat16),
            pltpu.VMEM((PAIR, seq_len), bfloat16),
            pltpu.VMEM((2, seq_len, tok_rows), float32),
        ]
        + [pltpu.SemaphoreType.DMA((halves, devices))] * 4
        + scratch,
        compiler_params=pltpu.CompilerParams(
            collective_id=collective_id, has_side_effects=True, vmem_limit_bytes=VMEM_LIMIT
        ),
        cost_estimate=pl.CostEstimate(
            flops=4 * halves * 2 * 4 * seq_len * seq_len * HEAD,
            bytes_accessed=16 * seq_len * PAIR * halves,
            transcendentals=0,
        ),
    )(lengths, *packed, *parts)
    gathered = [
        result.reshape(part.shape[0], 1 << bits, *part.shape[1:])
        for result, part in zip(results[4:], parts)
    ]
    return list(results[:4]) + gathered


def attend_backward_kernel(
    safe, chunk, halves, plan, slots, length_ref, scene_ref, o_ref, log_ref, d_merged, *refs
):
    count = plan[4]
    sources, packed_out, outs = refs[:count], refs[count], refs[count + 1 : 2 * count + 1]
    do_ref, stage_ref, kt_ref, dk_sum, dv_sum = refs[2 * count + 1 : 2 * count + 6]
    near_sem, in_sem, q_send, q_recv, kv_send, kv_recv = refs[2 * count + 6 : 2 * count + 12]
    others, begin, finish, drain = reduce_steps(*plan[:4], sources, outs, refs[2 * count + 12 :])
    total = len(plan[3])
    me, peers = group_peers()
    devices = len(peers)
    seq_len = scene_ref.shape[1]
    tok_rows = seq_len // devices
    length = length_ref[0]
    half, step = pl.program_id(0), pl.program_id(1)
    own = rows_at(me, tok_rows)
    chunks = seq_len // chunk

    def move(which, stage):
        finish(which, stage)
        if stage == 0 and which + AHEAD < total:
            begin(which + AHEAD)

    def move_at(head, part):
        for h in range(halves):
            for s in range(devices):
                todo = slots[((h * devices + s) * 2 + head) * chunks + part]
                if todo:

                    @pl.when((half == h) & (step == s))
                    def _(todo=todo):
                        for which, stage in todo:
                            move(which, stage)

    def bring(h, d):
        device, place = peers[d]
        column = pl.ds(pl.multiple_of((place * halves + h) * PAIR, PAIR), PAIR)
        source, target = d_merged.at[:, column], do_ref.at[h, own]
        if d == 0:
            return pltpu.make_async_copy(source, target, in_sem.at[h, 0])
        return pltpu.make_async_remote_copy(
            src_ref=source,
            dst_ref=target,
            send_sem=near_sem.at[h, d],
            recv_sem=in_sem.at[h, d],
            device_id=device,
            device_id_type=MESH,
        )

    def give(h, d, columns, send_sem, recv_sem, sender):
        device, place = peers[d]
        source = stage_ref.at[h, rows_at(place, tok_rows), columns]
        target = packed_out.at[h, sender, :, columns]
        if d == 0:
            return pltpu.make_async_copy(source, target, recv_sem.at[h, 0])
        return pltpu.make_async_remote_copy(
            src_ref=source,
            dst_ref=target,
            send_sem=send_sem.at[h, d],
            recv_sem=recv_sem.at[h, d],
            device_id=device,
            device_id_type=MESH,
        )

    q_columns, kv_columns = pl.ds(0, PAIR), pl.ds(PAIR, 2 * PAIR)

    @pl.when((half == 0) & (step == 0))
    def _():
        narrow_bits = plan[1]
        greet(peers[1:] + others[narrow_bits:])
        for h in range(halves):
            for d in range(devices):
                bring(h, d).start()
        for which in range(min(AHEAD, total)):
            begin(which)

    for h in range(halves):

        @pl.when((half == h) & (step == 0))
        def _(h=h):
            kt_ref[...] = scene_ref[0, :, PAIR : 2 * PAIR].T
            dk_sum[...] = jnp.zeros_like(dk_sum)
            dv_sum[...] = jnp.zeros_like(dv_sum)
            for d in range(devices):
                if d:
                    bring(h, d).wait_recv()
                else:
                    bring(h, d).wait()

    here = rows_at(lax.rem(me + 1 + step, devices), tok_rows)
    products = (o_ref[0, here, :].astype(float32) * do_ref[half, here, :].astype(float32)).T
    turned = []
    for head in range(2):
        lanes = slice(head * HEAD, (head + 1) * HEAD)
        queries = one_head(scene_ref[0, here, :PAIR], head) * bfloat16(HEAD**-0.5)
        d_mixed = one_head(do_ref[half, here, :], head)
        inner = jnp.sum(products[lanes, :], 0, keepdims=True)
        log_total = log_ref[0, head : head + 1, here]
        d_queries = jnp.zeros((HEAD, tok_rows), float32)
        for index in range(chunks):
            move_at(head, index)
            at = index * chunk
            part = slice(at, at + chunk)
            scores = lax.dot_general(
                scene_ref[0, part, PAIR : 2 * PAIR], queries, NT, preferred_element_type=float32
            )
            probs = jnp.exp(hide(scores, at, safe, length) - log_total)
            d_probs = lax.dot_general(
                scene_ref[0, part, 2 * PAIR :], d_mixed, NT, preferred_element_type=float32
            )
            dv_sum[part, :] += jnp.dot(
                probs.astype(bfloat16), d_mixed, preferred_element_type=float32
            )
            d_scores = (probs * (d_probs - inner)).astype(bfloat16)
            dk_sum[part, :] += jnp.dot(d_scores, queries, preferred_element_type=float32)
            d_queries += jnp.dot(kt_ref[lanes, part], d_scores, preferred_element_type=float32)
        turned.append(d_queries * HEAD**-0.5)
    stage_ref[half, here, :PAIR] = jnp.concatenate(turned, 0).T.astype(bfloat16)

    for h in range(halves):
        for s in range(devices):

            @pl.when((half == h) & (step == s))
            def _(h=h, s=s):
                give(h, (s + 1) % devices, q_columns, q_send, q_recv, me).start()
                if s == devices - 1:
                    stage_ref[h, :, PAIR : 2 * PAIR] = dk_sum[...].astype(bfloat16)
                    stage_ref[h, :, 2 * PAIR :] = dv_sum[...].astype(bfloat16)
                    for d in range(devices):
                        give(h, d, kv_columns, kv_send, kv_recv, me).start()

    @pl.when((half == halves - 1) & (step == devices - 1))
    def _():
        for which, stage in slots[-1]:
            move(which, stage)
        drain()
        for h in range(halves):
            for d in range(devices):
                for columns, send_sem, recv_sem in (
                    (q_columns, q_send, q_recv),
                    (kv_columns, kv_send, kv_recv),
                ):
                    sender = lax.rem(me + devices - d, devices)
                    copy = give(h, d, columns, send_sem, recv_sem, sender)
                    if d:
                        copy.wait_recv()
                        copy.wait_send()
                    else:
                        copy.wait()
                if d:
                    bring(h, d).wait_send()


def attend_backward(
    lengths, scenes, mixed, d_merged, log_totals, safe, parts, pieces, collective_id, chunk=512
):
    halves, seq_len, _ = scenes.shape
    devices = lax.axis_size("narrow")
    tok_rows = seq_len // devices
    bits, narrow_bits, plans, chunks, halved, outs, scratch = reduce_plan(parts, pieces)
    slots = slot_table(
        len(chunks), bits, halves * devices * 2 * (seq_len // chunk), PACE, DELAY
    )
    anywhere = pl.BlockSpec(memory_space=pl.ANY)

    def of_half(array):
        return pl.BlockSpec((1,) + array.shape[1:], lambda p, i: (p, 0, 0))

    return pl.pallas_call(
        partial(
            attend_backward_kernel,
            safe,
            chunk,
            halves,
            (bits, narrow_bits, plans, chunks, len(parts)),
            slots,
        ),
        grid=(halves, devices),
        in_specs=[
            pl.BlockSpec(memory_space=pltpu.SMEM),
            of_half(scenes),
            of_half(mixed),
            of_half(log_totals),
            anywhere,
        ]
        + [anywhere] * len(parts),
        out_specs=[anywhere] + [pl.BlockSpec(out.shape, lambda p, i: (0, 0)) for out in outs],
        out_shape=[jax.ShapeDtypeStruct((halves, devices, tok_rows, 3 * PAIR), bfloat16)] + outs,
        scratch_shapes=[
            pltpu.VMEM((halves, seq_len, PAIR), bfloat16),
            pltpu.VMEM((halves, seq_len, 3 * PAIR), bfloat16),
            pltpu.VMEM((PAIR, seq_len), bfloat16),
            pltpu.VMEM((seq_len, PAIR), float32),
            pltpu.VMEM((seq_len, PAIR), float32),
        ]
        + [pltpu.SemaphoreType.DMA((halves, devices))] * 6
        + scratch,
        compiler_params=pltpu.CompilerParams(
            collective_id=collective_id, has_side_effects=True, vmem_limit_bytes=60 * 2**20
        ),
        cost_estimate=pl.CostEstimate(
            flops=4 * halves * 2 * 10 * seq_len * seq_len * HEAD,
            bytes_accessed=32 * seq_len * PAIR,
            transcendentals=0,
        ),
    )(lengths, scenes, mixed, log_totals, d_merged, *halved)


def settle_kernel(plan, acts_ref, grads_ref, weights_ref, sum_ref, back_ref, right_ref, left_ref, dealt, *scratch):
    bits = plan[0]
    halves, groups, tok_rows, _ = grads_ref.shape
    width = acts_ref.shape[1]
    bands = width // BLOCK
    chunks = plan[3]
    peers, begin, finish, drain = reduce_steps(*plan[:4], [dealt], [sum_ref], scratch)
    left_ref[...] = acts_ref[...].T
    blocks = 3 * width // BLOCK
    for half in range(halves):
        for group in range(groups):
            for third in range(3):
                start = third * width + (group * halves + half) * PAIR
                right_ref[:, start : start + PAIR] = grads_ref[
                    half, group, :, third * PAIR : (third + 1) * PAIR
                ]
    rows = BLOCK >> bits

    def band_product(band):
        left = left_ref[band * BLOCK : (band + 1) * BLOCK, :]
        for at in range(0, blocks, 2):
            pair = jnp.dot(
                left, right_ref[:, at * BLOCK : (at + 2) * BLOCK], preferred_element_type=float32
            ).astype(bfloat16)
            pair = [pair[:, h * BLOCK : (h + 1) * BLOCK].reshape(-1, rows, BLOCK) for h in range(2)]
            low = (band * blocks + at) * rows
            both = jnp.concatenate(pair, 1)
            dealt[(slice(None),) * bits + (slice(low, low + 2 * rows),)] = both.reshape(
                (2,) * bits + both.shape[1:]
            )

    def back_product(band):
        here = slice(band * BLOCK, (band + 1) * BLOCK)
        back_ref[:, here] = lax.dot_general(
            right_ref[...], weights_ref[here, :], NT, preferred_element_type=float32
        )

    each = len(chunks) // bands
    work = [(2.5 * band, -1, band, -1) for band in range(2 * bands)]
    for chunk in range(len(chunks)):
        for stage in range(bits):
            ready = max(2.5 * (chunk // each + 1), 3.5 * chunk)
            work.append((ready + SETTLE_DELAY * (stage + 1), -stage, chunk, stage))
    for _, _, which, stage in sorted(work):
        if stage >= 0:
            finish(which, stage)
        elif which < bands:
            band_product(which)
            if which == 0:
                greet(peers)
            for chunk in range(which * each, (which + 1) * each):
                begin(chunk)
        else:
            back_product(which - bands)
    drain()


def settle(acts, grads, weights, device_count, collective_id):
    tok_rows, width = acts.shape
    rows = 3 * width * width // BLOCK // device_count
    dealt = jax.ShapeDtypeStruct((device_count, rows, BLOCK), bfloat16)
    bits, narrow_bits, plans, chunks, _, outs, scratch = reduce_plan(
        [dealt], (2 * width // BLOCK,), ORDERS[:2]
    )
    vmem = pl.BlockSpec(memory_space=pltpu.VMEM)
    return pl.pallas_call(
        partial(settle_kernel, (bits, narrow_bits, plans, chunks)),
        in_specs=[vmem] * 3,
        out_specs=[vmem] * 2,
        out_shape=outs + [jax.ShapeDtypeStruct((tok_rows, width), float32)],
        scratch_shapes=[
            pltpu.VMEM((tok_rows, 3 * width), bfloat16),
            pltpu.VMEM((width, tok_rows), bfloat16),
            pltpu.VMEM((2,) * bits + (rows, BLOCK), bfloat16),
        ]
        + scratch,
        compiler_params=pltpu.CompilerParams(
            collective_id=collective_id, has_side_effects=True, vmem_limit_bytes=60 * 2**20
        ),
        cost_estimate=pl.CostEstimate(
            flops=12 * tok_rows * width**2, bytes_accessed=10**8, transcendentals=0
        ),
    )(acts, grads, weights)


def feed_kernel(deal, acts_ref, grad_ref, middle_ref, up_ref, down_ref, out_ref, back_ref, one_ref, two_ref, turned_ref, sum_ref):
    at, last = pl.program_id(0), pl.num_programs(0) - 1

    @pl.when(at == 0)
    def _():
        sum_ref[...] = middle_ref[...]
        back_ref[...] = jnp.zeros_like(back_ref)
        turned_ref[...] = acts_ref[...].T

    acts, grad = acts_ref[...], grad_ref[...]
    hidden = jnp.dot(acts, up_ref[...], preferred_element_type=float32)
    square = hidden * hidden
    bend = jnp.tanh(GELU * hidden * (1.0 + CUBIC * square))
    share = 0.5 + 0.5 * bend
    active = (hidden * share).astype(bfloat16)
    slope = share + hidden * (0.5 - 0.5 * bend * bend) * (GELU + 3.0 * GELU * CUBIC * square)
    d_active = lax.dot_general(grad, down_ref[...], NT, preferred_element_type=float32)
    d_hidden = (d_active * slope).astype(bfloat16)
    sum_ref[...] += jnp.dot(active, down_ref[...], preferred_element_type=float32)
    back_ref[...] += lax.dot_general(d_hidden, up_ref[...], NT, preferred_element_type=float32)
    if deal:
        rows = BLOCK // one_ref.shape[0]
        d_up = jnp.dot(turned_ref[...], d_hidden, preferred_element_type=float32)
        d_up = d_up.astype(bfloat16)
        d_down = jnp.dot(active.T, grad, preferred_element_type=float32).astype(bfloat16)
        for band in range(d_up.shape[0] // BLOCK):
            blocks = [
                d_up[band * BLOCK : (band + 1) * BLOCK, start : start + BLOCK].reshape(-1, rows, BLOCK)
                for start in range(0, d_up.shape[1], BLOCK)
            ]
            one_ref[:, band] = jnp.concatenate(blocks, 1)
        blocks = [
            d_down[low : low + BLOCK, start : start + BLOCK].reshape(-1, rows, BLOCK)
            for low in range(0, d_down.shape[0], BLOCK)
            for start in range(0, d_down.shape[1], BLOCK)
        ]
        two_ref[...] = jnp.concatenate(blocks, 1)
    else:
        one_ref[...] = active
        two_ref[...] = d_hidden

    @pl.when(at == last)
    def _():
        out_ref[...] = sum_ref[...].astype(bfloat16)


def feed_forward(acts, grad, middle, w_up, w_down, device_count, tile=2 * BLOCK):
    tok_rows, width = acts.shape
    hidden = w_up.shape[1]
    rows = BLOCK // device_count
    deal = rows % 8 == 0
    full = pl.BlockSpec((tok_rows, width), lambda j: (0, 0))
    if deal:
        bands, blocks = width // BLOCK, hidden // BLOCK
        kinds = [(device_count, bands, blocks * rows, BLOCK), (device_count, blocks * bands * rows, BLOCK)]
        part = tile // BLOCK * rows
        specs = [
            pl.BlockSpec((device_count, bands, part, BLOCK), lambda j: (0, 0, j, 0)),
            pl.BlockSpec((device_count, bands * part, BLOCK), lambda j: (0, j, 0)),
        ]
    else:
        kinds = [(tok_rows, hidden)] * 2
        specs = [pl.BlockSpec((tok_rows, tile), lambda j: (0, j))] * 2
    out, back, one, two = pl.pallas_call(
        partial(feed_kernel, deal),
        grid=(hidden // tile,),
        in_specs=[full, full, full]
        + [
            pl.BlockSpec((width, tile), lambda j: (0, j)),
            pl.BlockSpec((tile, width), lambda j: (j, 0)),
        ],
        out_specs=[full, full] + specs,
        out_shape=[
            jax.ShapeDtypeStruct((tok_rows, width), bfloat16),
            jax.ShapeDtypeStruct((tok_rows, width), float32),
        ]
        + [jax.ShapeDtypeStruct(kind, bfloat16) for kind in kinds],
        scratch_shapes=[pltpu.VMEM((width, tok_rows), bfloat16), pltpu.VMEM((tok_rows, width), float32)],
        compiler_params=pltpu.CompilerParams(vmem_limit_bytes=58 * 2**20),
        cost_estimate=pl.CostEstimate(
            flops=12 * tok_rows * width * hidden, bytes_accessed=8 * width * hidden, transcendentals=0
        ),
    )(acts, grad, middle, w_up, w_down)
    if deal:
        return out, back, one.reshape(device_count, -1, BLOCK), two
    columns = lambda size: tuple(((0, 0, start, BLOCK),) for start in range(0, size, BLOCK))
    return (
        out,
        back,
        weight_grad(acts, [two[None]], columns(hidden), device_count),
        weight_grad(one, [grad[None]], columns(width), device_count),
    )


def ship_kernel(narrow_count, held_ref, *refs):
    shards, gain_ref = refs[:4], refs[4]
    arrived, total_ref = refs[5:7]
    pieces, outgoing, squares, send_sem, recv_sem, tile_send, tile_recv = refs[7:]
    devices, slots = outgoing.shape[:2]
    me = lax.axis_index("wide") * narrow_count + lax.axis_index("narrow")

    def device(d):
        place = lax.rem(me + d, devices)
        return place, {"wide": place // narrow_count, "narrow": lax.rem(place, narrow_count)}

    barrier = pltpu.get_barrier_semaphore()

    def announce(d, carry):
        pl.semaphore_signal(barrier, inc=1, device_id=device(d)[1], device_id_type=MESH)
        return carry

    lax.fori_loop(1, devices, announce, 0)
    at, own = 0, jnp.zeros((), float32)
    for shard in shards:
        values = shard[...]
        own += jnp.sum(values * values)
        pieces[at : at + values.shape[0]] = values
        at += values.shape[0]
    squares[me, : gain_ref.shape[0]] = gain_ref[...]
    squares[me, gain_ref.shape[0] :] = jnp.full((8, 128), own, float32)

    def pack(place, carry):
        for slot in range(slots):
            block = held_ref[place * slots + slot]
            piece = pieces[jnp.maximum(block, 0)]
            outgoing[place, slot] = jnp.where(block >= 0, piece, 0.0).astype(bfloat16)
        return carry

    lax.fori_loop(0, devices, pack, 0)
    pl.semaphore_wait(barrier, devices - 1)

    def copies(d):
        place, target = device(d)
        return (
            pltpu.make_async_remote_copy(
                src_ref=outgoing.at[place],
                dst_ref=arrived.at[:, me],
                send_sem=send_sem.at[d],
                recv_sem=recv_sem.at[d],
                device_id=target,
                device_id_type=MESH,
            ),
            pltpu.make_async_remote_copy(
                src_ref=squares.at[me],
                dst_ref=squares.at[me],
                send_sem=tile_send.at[d],
                recv_sem=tile_recv.at[d],
                device_id=target,
                device_id_type=MESH,
            ),
        )

    def start(d, carry):
        for copy in copies(d):
            copy.start()
        return carry

    lax.fori_loop(1, devices, start, 0)
    arrived[:, me] = outgoing[me]

    def arrive(d, carry):
        sender = lax.rem(me + devices - d, devices)
        pltpu.make_async_remote_copy(
            src_ref=outgoing.at[sender],
            dst_ref=arrived.at[:, sender],
            send_sem=send_sem.at[d],
            recv_sem=recv_sem.at[d],
            device_id=device(d)[1],
            device_id_type=MESH,
        ).wait_recv()
        pltpu.make_async_remote_copy(
            src_ref=squares.at[sender],
            dst_ref=squares.at[sender],
            send_sem=tile_send.at[d],
            recv_sem=tile_recv.at[d],
            device_id=device(d)[1],
            device_id_type=MESH,
        ).wait_recv()
        for copy in copies(d):
            copy.wait_send()
        return carry

    lax.fori_loop(1, devices, arrive, 0)
    total_ref[...] = jnp.sum(squares[...], 0)


def ship(shards, gain_grad, held, cap_slots, collective_id):
    devices = held.shape[0] // cap_slots
    rows = shards[0].shape[1]
    blocks = sum(shard.shape[0] for shard in shards)
    tile = (gain_grad.shape[0] + 8, 128)
    vmem = pl.BlockSpec(memory_space=pltpu.VMEM)
    return pl.pallas_call(
        partial(ship_kernel, lax.axis_size("narrow")),
        in_specs=[pl.BlockSpec(memory_space=pltpu.SMEM)] + [vmem] * (len(shards) + 1),
        out_specs=[vmem, vmem],
        out_shape=[
            jax.ShapeDtypeStruct((cap_slots, devices, rows, BLOCK), bfloat16),
            jax.ShapeDtypeStruct(tile, float32),
        ],
        scratch_shapes=[
            pltpu.VMEM((blocks, rows, BLOCK), float32),
            pltpu.VMEM((devices, cap_slots, rows, BLOCK), bfloat16),
            pltpu.VMEM((devices,) + tile, float32),
        ]
        + [pltpu.SemaphoreType.DMA((devices,))] * 4,
        compiler_params=pltpu.CompilerParams(
            collective_id=collective_id, has_side_effects=True, vmem_limit_bytes=VMEM_LIMIT
        ),
    )(held, *shards, gain_grad)


def update_kernel(rates, slot_ref, back_ref, *refs):
    masters, outs = refs[: len(rates)], refs[len(rates) :]
    block = 0
    for rate, master, out in zip(rates, masters, outs):
        bands, _, columns = master.shape
        for band in range(bands):
            for start in range(0, columns, BLOCK):
                here = slice(start, start + BLOCK)
                old = master[band, :, here]
                step = back_ref[slot_ref[block]].astype(float32)
                out[band, :, here] = old - rate * (step + weight_decay * old)
                block += 1


def update(masters, rates, places, back):
    vmem = pl.BlockSpec(memory_space=pltpu.VMEM)
    return pl.pallas_call(
        partial(update_kernel, rates),
        in_specs=[pl.BlockSpec(memory_space=pltpu.SMEM)] + [vmem] * (len(masters) + 1),
        out_specs=[vmem] * len(masters),
        out_shape=[jax.ShapeDtypeStruct(master.shape, float32) for master in masters],
        compiler_params=pltpu.CompilerParams(vmem_limit_bytes=VMEM_LIMIT),
    )(places, back, *masters)


def weight_grad_kernel(columns, band_rows, left_ref, *refs):
    right_refs, out_ref = refs[:-1], refs[-1]
    left = left_ref[...].T
    for at in range(0, len(columns), 2):
        blocks = []
        for spots in columns[at : at + 2]:
            right = [right_refs[i][g, :, start : start + size] for i, g, start, size in spots]
            right = right[0] if len(right) == 1 else jnp.concatenate(right, 1)
            block = jnp.dot(left, right, preferred_element_type=float32)
            blocks.append(block.astype(bfloat16).reshape(-1, band_rows, BLOCK))
        out_ref[:, at * band_rows : (at + 2) * band_rows, :] = jnp.concatenate(blocks, 1)


def weight_grad(left, rights, columns, device_count):
    tok_rows, height = left.shape
    band_rows = BLOCK // device_count
    bands, wide = height // BLOCK, len(columns)
    if band_rows % 8:
        right = [rights[i][g, :, start : start + n] for spots in columns for i, g, start, n in spots]
        right = jnp.concatenate(right, 1)
        product = jnp.einsum("td,te->de", left, right, preferred_element_type=float32)
        product = product.astype(bfloat16).reshape(bands, device_count, band_rows, wide, BLOCK)
        return product.transpose(1, 0, 3, 2, 4).reshape(device_count, -1, BLOCK)
    return pl.pallas_call(
        partial(weight_grad_kernel, columns, band_rows),
        grid=(bands,),
        in_specs=[
            pl.BlockSpec((tok_rows, BLOCK), lambda i: (0, i)),
        ]
        + [pl.BlockSpec(right.shape, lambda i: (0, 0, 0)) for right in rights],
        out_specs=pl.BlockSpec((device_count, wide * band_rows, BLOCK), lambda i: (0, i, 0)),
        out_shape=jax.ShapeDtypeStruct((device_count, bands * wide * band_rows, BLOCK), bfloat16),
        compiler_params=pltpu.CompilerParams(vmem_limit_bytes=VMEM_LIMIT),
        cost_estimate=pl.CostEstimate(
            flops=2 * tok_rows * bands * wide * BLOCK**2,
            bytes_accessed=2 * (tok_rows * (height + wide * BLOCK) + bands * wide * BLOCK**2),
            transcendentals=0,
        ),
    )(left, *rights)


def body(
    tokens,
    cotangent,
    lengths,
    owners,
    w_qkv,
    w_out,
    w_up,
    w_down,
    norm_gains,
    gain_first,
    gain_second,
    moment_first,
    moment_second,
    left_stat,
    right_stat,
    left_basis,
    right_basis,
):
    tok_rows, width = tokens.shape
    narrow_count = lax.axis_size("narrow")
    device_count = lax.axis_size("wide") * narrow_count
    seq_len = tok_rows * narrow_count
    cap_slots = moment_first.shape[0]
    masters = (w_qkv, w_out, w_up, w_down)
    lowered = tuple((layout.astype(jnp.bfloat16) for layout in masters)) + (
        norm_gains.astype(jnp.bfloat16),
    )
    share = norm_gains.shape[1]
    gains_low = jnp.pad(lowered[4], ((0, 6), (0, 128 - share)))[None]
    w_attn, gain_pair = gather_bands((lowered[0], gains_low), ((4, 2), (1, 1)), 3)
    w_attn = w_attn.reshape(width, 3 * width)
    gain_pair = gain_pair[0, :, :2, :share].transpose(1, 0, 2).reshape(2, width)
    gain_pair = gain_pair.astype(jnp.float32)
    w_proj, w_back = (
        gathered.reshape(-1, width)
        for gathered in lax.all_gather(lowered[1:4:2], ("wide", "narrow"), axis=1, tiled=True)
    )
    inputs = tokens.astype(jnp.float32)
    normed_one, inverse_one = normalize(inputs)
    act_one = (normed_one * gain_pair[0]).astype(jnp.bfloat16)
    head_width = width // narrow_count
    safe = seq_len - tok_rows
    packed = project(act_one, w_attn, narrow_count)
    halves = len(packed)
    scenes, merged, mixed, log_totals, w_hidden = attend(
        lengths, packed, safe, (lowered[2],), ((4, 2),), 4
    )
    w_hidden = w_hidden.reshape(width, FF)
    middle = inputs + jnp.dot(merged, w_proj, preferred_element_type=jnp.float32)
    normed_two, inverse_two = normalize(middle)
    act_two = (normed_two * gain_pair[1]).astype(jnp.bfloat16)
    block_out, d_act_two, d_w_hidden, d_back = feed_forward(
        act_two, cotangent, middle, w_hidden, w_back, device_count
    )
    d_norm_two, d_gain_two = norm_backward(d_act_two, normed_two, inverse_two, gain_pair[1])
    d_middle = cotangent.astype(jnp.float32) + d_norm_two
    d_branch = d_middle.astype(jnp.bfloat16)
    plain = lambda size: tuple(((0, 0, start, BLOCK),) for start in range(0, size, BLOCK))
    d_proj = weight_grad(merged, [d_branch[None]], plain(width), device_count)
    d_merged = jnp.einsum("te,de->td", d_branch, w_proj, preferred_element_type=jnp.float32).astype(
        jnp.bfloat16
    )
    ready = (d_w_hidden, d_back, d_proj)
    d_packed, hidden_sum, back_sum, proj_sum = attend_backward(
        lengths, scenes, mixed, d_merged, log_totals, safe, ready, (8, 8, 2), 5
    )
    if BLOCK // device_count % 8:
        d_packed = [d_packed[half] for half in range(halves)]
        grouped = tuple(
            tuple((half, group, third * PAIR, PAIR) for half in range(halves))
            for third in range(3)
            for group in range(narrow_count)
        )
        d_attn = weight_grad(act_one, d_packed, grouped, device_count)
        (attn_sum,) = reduce_to_shards((d_attn,), (6,), 1)
        d_act_one = project_back(d_packed, w_attn)
    else:
        attn_sum, d_act_one = settle(act_one, d_packed, w_attn, device_count, 1)
    d_norm_one, d_gain_one = norm_backward(d_act_one, normed_one, inverse_one, gain_pair[0])
    grad_tokens = (d_middle + d_norm_one).astype(jnp.bfloat16)
    gain_parts = jnp.stack([d_gain_one, d_gain_two]).reshape(-1, 128)
    band_rows = BLOCK // device_count
    block_count = owners.shape[0]
    order = lax.iota(jnp.int32, block_count)
    earlier = (owners[None, :] == owners[:, None]) & (order[None, :] < order[:, None])
    rank = jnp.sum(earlier.astype(jnp.int32), 1)
    slots = owners * cap_slots + rank
    every = lax.iota(jnp.int32, device_count * cap_slots)
    held = jnp.max(jnp.where(slots[None, :] == every[:, None], order[None, :], -1), 1)
    shards = [
        shard.reshape(-1, band_rows, BLOCK)
        for shard in (attn_sum, proj_sum, hidden_sum, back_sum)
    ]
    slot_grads, totals = ship(shards, gain_parts, held, cap_slots, 2)
    place = lax.axis_index(("wide", "narrow"))
    gain_grad = totals[:-8].reshape(2, width)
    grad_norm = jnp.sqrt(totals[-1, 0] + jnp.sum(gain_grad * gain_grad))
    gain_grad = lax.dynamic_slice_in_dim(gain_grad, place * share, share, 1)
    factor = jnp.minimum(1.0, clip_bound / grad_norm)
    slot_grads = slot_grads.reshape(cap_slots, BLOCK, BLOCK)
    restored, first_new, second_new, left_new, right_new, gram, turn = soap_update(
        factor, slot_grads, moment_first, moment_second, left_stat, right_stat, left_basis, right_basis
    )
    square = (-1, BLOCK, BLOCK)
    left_turn, right_turn = renew_bases(gram.reshape(square), turn.reshape(square))
    returned = lax.all_to_all(
        shortened(restored.reshape(cap_slots, device_count, -1, BLOCK)),
        ("wide", "narrow"),
        split_axis=1,
        concat_axis=1,
        tiled=True,
    )
    fan_list = (2 * width, max(1, width * 16 // seq_len), width, FF)
    rates = tuple(fan_in ** (-0.5) for fan_in in fan_list)
    places = rank * device_count + owners
    updated = update(masters, rates, places, returned.reshape(-1, band_rows, BLOCK))
    clipped = gain_grad * factor
    gain_one_new = decay_rate * gain_first + (1.0 - decay_rate) * clipped
    gain_two_new = decay_rate * gain_second + (1.0 - decay_rate) * clipped * clipped
    correct = 1.0 - decay_rate**STEP
    gain_values = norm_gains - gain_rate * (gain_one_new / correct) / (
        jnp.sqrt(gain_two_new / correct) + eps_adam
    )
    return (
        block_out,
        grad_tokens,
        grad_norm,
        updated[0],
        updated[1],
        updated[2],
        updated[3],
        gain_values,
        gain_one_new,
        gain_two_new,
        first_new,
        second_new,
        left_new,
        right_new,
        left_turn,
        right_turn,
    )


def solution(mesh):
    in_specs = (
        P(("wide", "narrow"), None),
        P(("wide", "narrow"), None),
        P("wide"),
        P(),
        P(None, ("wide", "narrow"), None),
        P(None, ("wide", "narrow"), None),
        P(None, ("wide", "narrow"), None),
        P(None, ("wide", "narrow"), None),
        P(None, ("wide", "narrow")),
        P(None, ("wide", "narrow")),
        P(None, ("wide", "narrow")),
        P(("wide", "narrow"), None, None),
        P(("wide", "narrow"), None, None),
        P(("wide", "narrow"), None, None),
        P(("wide", "narrow"), None, None),
        P(("wide", "narrow"), None, None),
        P(("wide", "narrow"), None, None),
    )
    out_specs = (
        P(("wide", "narrow"), None),
        P(("wide", "narrow"), None),
        P(),
        P(None, ("wide", "narrow"), None),
        P(None, ("wide", "narrow"), None),
        P(None, ("wide", "narrow"), None),
        P(None, ("wide", "narrow"), None),
        P(None, ("wide", "narrow")),
        P(None, ("wide", "narrow")),
        P(None, ("wide", "narrow")),
        P(("wide", "narrow"), None, None),
        P(("wide", "narrow"), None, None),
        P(("wide", "narrow"), None, None),
        P(("wide", "narrow"), None, None),
        P(("wide", "narrow"), None, None),
        P(("wide", "narrow"), None, None),
    )
    return jax.shard_map(body, mesh=mesh, in_specs=in_specs, out_specs=out_specs, check_vma=False)
```
